32 devices in a mesh: dp: 8 (over z, x), head: 4 (over y, core).
Axes of the slice: x: 2, y: 2, z: 4, core: 2. Of those that a mesh axis runs over, the one named last changes fastest.
Arguments:
- hidden_in: bfloat16 [8, 2048, 1024], P('dp', 'head'), may hold values from -6 to 6
- first_values: bfloat16 [8, 2048, 1024], P('dp', 'head'), may hold values from -6 to 6
- doc_lengths: int32 [8, 16], P('dp'), may hold values from 1 to 1537, as said below
- out_grad: bfloat16 [8, 2048, 1024], P('dp', 'head'), may hold values from -6 to 6
- qkv_weight: bfloat16 [1024, 3, 1024], P('dp', None, 'head'), may hold values from -0.1875 to 0.1875
- out_weight: bfloat16 [1024, 1024], P('head', 'dp'), may hold values from -6 to 6
- gate_up_weight: bfloat16 [1024, 2, 2816], P('dp', None, 'head'), may hold values from -0.1875 to 0.1875
- down_weight: bfloat16 [2816, 1024], P('head', 'dp'), may hold values from -0.109375 to 0.109375
- attn_gain: float32 [1024], replicated, may hold values from 0.1 to 1.9
- mlp_gain: float32 [1024], replicated, may hold values from 0.1 to 1.9
Outputs:
- layer_out: bfloat16 [8, 2048, 1024], P('dp', 'head')
- input_grad: float32 [8, 2048, 1024], P('dp', 'head')
- first_values_grad: float32 [8, 2048, 1024], P('dp', 'head')
- qkv_weight_grad: float32 [1024, 3, 1024], P('dp', None, 'head')
- out_weight_grad: float32 [1024, 1024], P('head', 'dp')
- gate_up_weight_grad: float32 [1024, 2, 2816], P('dp', None, 'head')
- down_weight_grad: float32 [2816, 1024], P('head', 'dp')
- attn_gain_grad: float32 [1024], replicated
- mlp_gain_grad: float32 [1024], replicated
The draws below stay inside these ranges and needn't reach their ends.
Inputs may be any that keep to these rules, and one draw needn't show every extreme that they name: `doc_lengths`: each row's lengths sum to 2048.
All inputs are finite; a program needn't handle non-finite values.
Results may differ from the reference program's by a relative error of at most 0.023.
Values may be sent and summed in bfloat16 or wider, within the bound.
No kernel may reach another device: no remote copies, remote signals or barrier semaphores. Data moves between devices by JAX's collectives and lax.ppermute only.
A program may use at most 256 MiB of HBM per device.

```python
import math
import jax
import jax.numpy as jnp
from jax import lax

D = 1024
HEADS = 16
HEAD_DIM = 64
FF = 2816
SEQ = 2048
NDOC = 16
QBLOCK = 512
ROWS = 8
SHARD = 512


def draw_doc_lengths(key, part):
    key = jax.random.fold_in(key, 11)

    def one_row(row_key):
        key_one, key_two, key_three = jax.random.split(row_key, 3)
        spare = SHARD - NDOC
        shares = jax.random.randint(key_one, (NDOC - 2,), 1, 1000)
        extra = shares * spare // jnp.sum(shares)
        extra = extra.at[0].add(spare - jnp.sum(extra))
        shorts = jnp.concatenate([jnp.ones((1,), jnp.int32), 1 + extra.astype(jnp.int32)])
        shorts = shorts[jax.random.permutation(key_two, NDOC - 1)]
        place = jax.random.randint(key_three, (), 0, NDOC)
        doc_index = jnp.arange(NDOC)
        picked = jnp.clip(jnp.where(doc_index < place, doc_index, doc_index - 1), 0, NDOC - 2)
        return jnp.where(doc_index == place, SEQ - SHARD + 1, shorts[picked]).astype(jnp.int32)
    return jax.vmap(one_row)(jax.random.split(key, ROWS))


def level_of(stream_key, extent, shards, least, largest):
    def one(position, blocks):
        steps = jax.random.uniform(jax.random.fold_in(jax.random.fold_in(stream_key, 6), position), (blocks,), jnp.float32, least / len(shards), largest / len(shards))
        return jnp.repeat(jnp.exp(steps), extent[position] // blocks).reshape((-1,) + (1,) * (len(extent) - position - 1))

    level = one(*shards[0])
    for cut in shards[1:]:
        level = level * one(*cut)
    return level


def centred(stream_key, shape, width, limit, cuts=(), held_as=jnp.bfloat16):
    entries = width * jax.random.normal(stream_key, shape, jnp.float32)
    if cuts:
        entries = entries * level_of(stream_key, shape, cuts, -0.22, 0.18)
    return jnp.clip(entries, -limit, limit).astype(held_as)


def setup_inputs(seed: int = 0) -> dict:
    streams_of = jax.random.split(jax.random.key(seed), 11)
    return {
        "hidden_in": centred(streams_of[0], (ROWS, SEQ, D), 1.0, 6.0, ((0, 8), (1, 4))),
        "first_values": centred(streams_of[1], (ROWS, SEQ, D), 1.0, 6.0, ((0, 8), (1, 4))),
        "doc_lengths": draw_doc_lengths(jax.random.fold_in(streams_of[10], 71), 0),
        "out_grad": centred(streams_of[3], (ROWS, SEQ, D), 1.0, 6.0, ((0, 8), (1, 4))),
        "qkv_weight": centred(streams_of[4], (D, 3, D), D ** -0.5, 0.1875, ((0, 8), (2, 4))),
        "out_weight": centred(streams_of[5], (D, D), (max(1, 2 * D // SEQ)) ** -0.5, 6.0, ((0, 4), (1, 8))),
        "gate_up_weight": centred(streams_of[6], (D, 2, FF), D ** -0.5, 0.1875, ((0, 8), (2, 4))),
        "down_weight": centred(streams_of[7], (FF, D), FF ** -0.5, 0.109375, ((0, 4), (1, 8))),
        "attn_gain": jnp.clip(1.0 + 0.18 * jax.random.normal(streams_of[8], (D,), jnp.float32), 0.1, 1.9),
        "mlp_gain": jnp.clip(1.0 + 0.18 * jax.random.normal(streams_of[9], (D,), jnp.float32), 0.1, 1.9),
    }


norm_eps = 1e-06
highest = lax.Precision.HIGHEST

@jax.custom_vjp
def low(v):
    return lax.optimization_barrier(v.astype(jnp.bfloat16)).astype(jnp.float32)

@jax.custom_vjp
def low_back(v):
    return v

def low_keep(v):
    return (low(v), None)

def low_pass(kept, grad):
    return (grad,)

def back_keep(v):
    return (v, None)

def back_low(kept, grad):
    return (low(grad),)
low.defvjp(low_keep, low_pass)
low_back.defvjp(back_keep, back_low)

def doc_layout(lengths):
    tok_index = jnp.arange(SEQ, dtype=jnp.int32)
    doc_ends = jnp.cumsum(lengths).astype(jnp.int32)
    starts = doc_ends - lengths
    segment = lax.optimization_barrier(jnp.sum((tok_index[:, None] >= doc_ends[None, :]).astype(jnp.int32), axis=1))
    owners = segment[:, None] == jnp.arange(NDOC, dtype=jnp.int32)[None, :]
    positions = tok_index - lax.optimization_barrier(jnp.sum(jnp.where(owners, starts[None, :], 0), axis=1))
    return (segment, positions.astype(jnp.int32))

def rope_tables(positions):
    freq_index = jnp.arange(HEAD_DIM // 2, dtype=jnp.float32)
    inverse = jnp.exp(freq_index * (-2.0 * math.log(10000.0) / HEAD_DIM))
    angles = positions.astype(jnp.float32)[..., None] * inverse
    angles = jnp.concatenate([angles, angles], axis=-1)
    return (jnp.cos(angles), jnp.sin(angles))

def rotate(tensor, cos_table, sin_table):
    half_dim = tensor.shape[-1] // 2
    turned = jnp.concatenate([-tensor[..., half_dim:], tensor[..., :half_dim]], axis=-1)
    return tensor * cos_table + turned * sin_table

def rms_scale(stream):
    return lax.rsqrt(lax.optimization_barrier(jnp.mean(stream * stream, axis=-1, keepdims=True)) + norm_eps)

def layer_row(stream, first_row, lengths, w_qkv, w_out, w_gate_up, w_down, gain_attn, gain_mlp):
    segment, positions = doc_layout(lengths)
    cos_table, sin_table = rope_tables(positions)
    cos_table = cos_table[:, None, :]
    sin_table = sin_table[:, None, :]
    normed = low(stream * rms_scale(stream) * gain_attn)
    project = low_back(jnp.einsum('sd,dcf->scf', normed, w_qkv, precision=highest))
    head_shape = (SEQ, HEADS, HEAD_DIM)
    queries = low(rotate(project[:, 0].reshape(head_shape), cos_table, sin_table)).transpose(1, 0, 2)
    key_rows = low(rotate(project[:, 1].reshape(head_shape), cos_table, sin_table)).transpose(1, 0, 2)
    value_rows = low(0.5 * project[:, 2] + 0.5 * first_row).reshape(head_shape).transpose(1, 0, 2)
    scaling = HEAD_DIM ** (-0.5)
    key_index = jnp.arange(SEQ, dtype=jnp.int32)

    def block_fn(block_item):
        q_block, q_start = block_item
        q_index = q_start + jnp.arange(QBLOCK, dtype=jnp.int32)
        q_segment = lax.dynamic_slice_in_dim(segment, q_start, QBLOCK)
        allowed = (q_segment[:, None] == segment[None, :]) & (key_index[None, :] <= q_index[:, None])
        scores = low_back(jnp.einsum('hqd,hkd->hqk', q_block, key_rows, precision=highest)) * scaling
        scores = jnp.where(allowed[None], scores, -1e+30)
        row_max = lax.optimization_barrier(jnp.max(scores, axis=-1, keepdims=True))
        exp_terms = jnp.exp(scores - row_max)
        weights_p = exp_terms / lax.optimization_barrier(jnp.sum(exp_terms, axis=-1, keepdims=True))
        return jnp.einsum('hqk,hkd->hqd', low(weights_p), value_rows, precision=highest)
    blocks = queries.reshape(HEADS, SEQ // QBLOCK, QBLOCK, HEAD_DIM).transpose(1, 0, 2, 3)
    starts = jnp.arange(SEQ // QBLOCK, dtype=jnp.int32) * QBLOCK
    context = lax.map(jax.checkpoint(block_fn), (blocks, starts))
    context = context.transpose(0, 2, 1, 3).reshape(SEQ, D)
    context = low(low_back(context))
    middle = stream + low_back(jnp.dot(context, w_out, precision=highest))
    normed_mid = low(middle * rms_scale(middle) * gain_mlp)
    gate_up = low_back(jnp.einsum('sd,dcf->scf', normed_mid, w_gate_up, precision=highest))
    mixed_act = low(jax.nn.silu(gate_up[:, 0]) * gate_up[:, 1])
    return middle + low_back(jnp.dot(mixed_act, w_down, precision=highest))

def reference(hidden_in, first_values, doc_lengths, out_grad, qkv_weight, out_weight, gate_up_weight, down_weight, attn_gain, mlp_gain):

    def forward(stream, firsts, w_qkv, w_out, w_gate_up, w_down, gain_attn, gain_mlp):

        def row_step(carry, row_item):
            return (carry, layer_row(row_item[0], row_item[1], row_item[2], w_qkv, w_out, w_gate_up, w_down, gain_attn, gain_mlp))
        unused, result = lax.scan(jax.checkpoint(row_step), jnp.zeros((), jnp.float32), (stream, firsts, doc_lengths))
        return result
    inputs = tuple((tensor.astype(jnp.float32) for tensor in (hidden_in, first_values, qkv_weight, out_weight, gate_up_weight, down_weight, attn_gain, mlp_gain)))
    result, pullback = jax.vjp(forward, *inputs)
    gradients = pullback(out_grad.astype(jnp.float32))
    return (result.astype(jnp.bfloat16), gradients[0], gradients[1], gradients[2], gradients[3], gradients[4], gradients[5], gradients[6], gradients[7])
```

```python
import functools
import math

import jax
import jax.numpy as jnp
from jax import lax
from jax.experimental import pallas as pl
from jax.experimental.pallas import tpu as pltpu
from jax.sharding import PartitionSpec as P

HEAD_DIM = 64
HALF = HEAD_DIM // 2
SEQ = 2048
NDOC = 16
NORM_EPS = 1e-06
NEG = -1e30
F32 = jnp.float32
BF16 = jnp.bfloat16
VMEM_LIMIT = 56 << 20

VMEM = pl.BlockSpec(memory_space=pltpu.VMEM)
SMEM = pl.BlockSpec(memory_space=pltpu.SMEM)


def shape(dims, dtype):
    return jax.ShapeDtypeStruct(dims, dtype)


def dot(a, b):
    return jnp.dot(a, b, preferred_element_type=F32)


def dot_nt(a, b):
    return lax.dot_general(a, b, (((1,), (1,)), ((), ())), preferred_element_type=F32)


def dot_tn(a, b):
    return lax.dot_general(a, b, (((0,), (0,)), ((), ())), preferred_element_type=F32)


def call(body, name, ins, outs, scratch=(), flops=0):
    moved = sum(a.size * a.dtype.itemsize for a, _ in ins)
    moved += sum(math.prod(o.shape) * o.dtype.itemsize for o in outs)
    return pl.pallas_call(
        body,
        name=name,
        out_shape=outs,
        in_specs=[s for _, s in ins],
        out_specs=[VMEM] * len(outs),
        scratch_shapes=list(scratch),
        compiler_params=pltpu.CompilerParams(vmem_limit_bytes=VMEM_LIMIT),
        cost_estimate=pl.CostEstimate(flops=flops, bytes_accessed=moved, transcendentals=0),
    )(*[a for a, _ in ins])


def in_vmem(*arrays):
    return [(a, VMEM) for a in arrays]


def row_scale(stream):
    return lax.rsqrt(jnp.mean(stream * stream, axis=-1, keepdims=True) + NORM_EPS)


def swap(value, axis, size, bit):
    return lax.ppermute(value, axis, [(i, i ^ bit) for i in range(size)])


def bits_down(size):
    return [1 << b for b in reversed(range(size.bit_length() - 1))]


def gather_relative(value, axis, size):
    parts = {0: value}
    for bit in bits_down(size):
        parts.update({j | bit: swap(v, axis, size, bit) for j, v in list(parts.items())})
    return [parts[j] for j in range(size)]


def sum_relative(parts, axis, size):
    parts = dict(enumerate(parts))
    bit = 1
    while bit < size:
        kept = {}
        for j in sorted((j for j in parts if not j & bit), reverse=True):
            got = swap(parts[j | bit], axis, size, bit)
            total = parts[j].astype(F32) + got.astype(F32)
            kept[j] = total if bit * 2 == size else total.astype(BF16)
        parts = kept
        bit *= 2
    return parts[0]


def exchange_relative(parts, axis, size):
    return [p if j == 0 else swap(p, axis, size, j) for j, p in enumerate(parts)]


def assemble_kernel(dp_ref, *refs):
    *parts, out = refs
    lanes = parts[0].shape[1]
    for j, part in enumerate(parts):
        out[:, pl.ds(pl.multiple_of((dp_ref[0] ^ j) * lanes, 128), lanes)] = part[...]


def gather_columns(value, dp, size):
    if value.shape[1] % 128:
        return lax.all_gather(value, "dp", axis=1, tiled=True)
    half = value.shape[0] // 2
    parts = [value[:half], value[half:]]
    for bit in bits_down(size):
        parts = [jnp.concatenate([p, swap(p, "dp", size, bit)], axis=0) for p in parts]
    order = [0]
    for bit in bits_down(size):
        order = order + [j | bit for j in order]
    place = [order.index(j) for j in range(size)]
    pieces = []
    for p in parts:
        p = p.reshape(size, half, value.shape[1])
        ins = [(dp, SMEM)] + in_vmem(*[p[i] for i in place])
        pieces += call(
            assemble_kernel, "assemble", ins, [shape((half, size * value.shape[1]), BF16)]
        )
    return pieces


def project_kernel(n, tile, me_ref, *refs):
    xs, fvs = refs[:n], refs[n : 2 * n]
    w_ref, gain_ref, cos_ref, sin_ref, q_out, k_out, kt_out, v_out, vt_out = refs[2 * n :]
    width = q_out.shape[0]
    shard = xs[0].shape[0]
    for j in range(n):

        def step(t, carry, j=j):
            rows = pl.ds(pl.multiple_of(t * tile, tile), tile)
            at = pl.ds(pl.multiple_of((me_ref[0] ^ j) * shard + t * tile, tile), tile)
            stream = xs[j][rows, :].astype(F32)
            normed = (stream * row_scale(stream) * gain_ref[...]).astype(BF16)
            qk = dot_nt(w_ref[: 2 * width, :], normed)
            cos, sin = cos_ref[:, at], sin_ref[:, at]
            turned = []
            for row in range(0, 2 * width, HEAD_DIM):
                first, second = qk[row : row + HALF], qk[row + HALF : row + HEAD_DIM]
                turned += [first * cos - second * sin, second * cos + first * sin]
            turned = jnp.concatenate(turned, axis=0)
            q_out[:, at] = (turned[:width] * HEAD_DIM ** (-0.5)).astype(BF16)
            keys = turned[width:]
            kt_out[:, at] = keys.astype(BF16)
            k_out[at, :] = keys.T.astype(BF16)
            values = 0.5 * dot_nt(normed, w_ref[2 * width :, :]) + 0.5 * fvs[j][rows, :].astype(F32)
            v_out[at, :] = values.astype(BF16)
            vt_out[:, at] = values.T.astype(BF16)
            return carry

        lax.fori_loop(0, shard // tile, step, 0)


def doc_of(len_ref, token):
    run, first, last = jnp.int32(0), jnp.int32(0), jnp.int32(SEQ)
    for doc in range(NDOC):
        end = run + len_ref[0, doc]
        inside = (token >= run) & (token < end)
        first, last = jnp.where(inside, run, first), jnp.where(inside, end, last)
        run = end
    return first, last


def attend_kernel(bq, heads, len_ref, me_ref, q_ref, k_ref, vt_ref, start_ref, ctx_ref, ot_ref, lse_ref, s_ref):
    bk = bq
    block = pl.program_id(0)
    first, _ = doc_of(len_ref, block * bq)
    starts = start_ref[...]

    def score(kb, tops, diagonal):
        at = pl.ds(pl.multiple_of(kb * bk, bk), bk)
        key_index = lax.broadcasted_iota(jnp.int32, (bk, bq), 0) + kb * bk
        allowed = key_index >= starts
        if diagonal:
            allowed &= key_index <= lax.broadcasted_iota(jnp.int32, (bk, bq), 1) + block * bq
        out = []
        for h in range(heads):
            rows = slice(h * HEAD_DIM, (h + 1) * HEAD_DIM)
            scores = jnp.where(allowed, dot(k_ref[at, rows], q_ref[rows, :]), NEG)
            s_ref[h, at, :] = scores
            out.append(jnp.maximum(tops[h], jnp.max(scores.reshape(bk // 8, 8, bq), axis=0)))
        return tuple(out)

    tops = score(block, tuple(jnp.full((8, bq), NEG, F32) for _ in range(heads)), True)
    tops = lax.fori_loop(first // bk, block, lambda kb, c: score(kb, c, False), tops)
    tops = [jnp.max(t, axis=0, keepdims=True) for t in tops]

    def gather(kb, carry):
        at = pl.ds(pl.multiple_of(kb * bk, bk), bk)
        out = []
        for h in range(heads):
            rows = slice(h * HEAD_DIM, (h + 1) * HEAD_DIM)
            total, acc = carry[h]
            probs = jnp.exp(s_ref[h, at, :] - tops[h])
            total = total + jnp.sum(probs.reshape(bk // 8, 8, bq), axis=0)
            out.append((total, acc + dot(vt_ref[rows, at], probs.astype(BF16))))
        return tuple(out)

    zero = tuple((jnp.zeros((8, bq), F32), jnp.zeros((HEAD_DIM, bq), F32)) for _ in range(heads))
    sums = lax.fori_loop(first // bk, block + 1, gather, zero)
    outs = []
    for h in range(heads):
        total = jnp.sum(sums[h][0], axis=0, keepdims=True)
        outs.append(sums[h][1] * (1.0 / total))
        lse_ref[h : h + 1, :] = tops[h] + jnp.log(total)
    out = jnp.concatenate(outs, axis=0)
    ot_ref[...] = out.astype(BF16)
    ctx_ref[...] = out.T.astype(BF16).reshape(ctx_ref.shape)


def attend(lengths, me, q_t, keys, v_t, starts, shard):
    width = q_t.shape[0]
    heads = width // HEAD_DIM
    bq = min(512, shard)
    per = shard // bq
    spec = pltpu.PrefetchScalarGridSpec(
        num_scalar_prefetch=2,
        grid=(SEQ // bq,),
        in_specs=[
            pl.BlockSpec((width, bq), lambda i, l, h: (0, i)),
            pl.BlockSpec((SEQ, width), lambda i, l, h: (0, 0)),
            pl.BlockSpec((width, SEQ), lambda i, l, h: (0, 0)),
            pl.BlockSpec((1, bq), lambda i, l, h: (0, i)),
        ],
        out_specs=[
            pl.BlockSpec((1, bq, width), lambda i, l, h: ((i // per) ^ h[0], i % per, 0)),
            pl.BlockSpec((width, bq), lambda i, l, h: (0, i)),
            pl.BlockSpec((heads, bq), lambda i, l, h: (0, i)),
        ],
        scratch_shapes=[pltpu.VMEM((heads, SEQ, bq), F32)],
    )
    return pl.pallas_call(
        functools.partial(attend_kernel, bq, heads),
        name="attend",
        grid_spec=spec,
        out_shape=[
            shape((SEQ // shard, shard, width), BF16),
            shape((width, SEQ), BF16),
            shape((heads, SEQ), F32),
        ],
        compiler_params=pltpu.CompilerParams(vmem_limit_bytes=VMEM_LIMIT),
        cost_estimate=pl.CostEstimate(
            flops=16 * SEQ * SEQ * width, bytes_accessed=8 * SEQ * width, transcendentals=0
        ),
    )(lengths, me, q_t, keys, v_t, starts)


def attend_back_kernel(n, block, len_ref, me_ref, *refs):
    q_ref, k_ref, kt_ref, v_ref, ot_ref, lse_ref, start_ref, cos_ref, sin_ref = refs[:9]
    dos = refs[9 : 9 + n]
    out_ref, dq_ref, dk_ref, dv_ref, do_ref, delta_ref = refs[9 + n :]
    width = q_ref.shape[0]
    heads = width // HEAD_DIM
    shard = SEQ // n
    for j in range(n):
        at = pl.ds(pl.multiple_of((me_ref[0] ^ j) * shard, shard), shard)
        do_ref[:, at] = dos[j][...]
        product = dos[j][...].astype(F32) * ot_ref[:, at].astype(F32)
        for h in range(heads):
            delta_ref[h : h + 1, at] = jnp.sum(
                product[h * HEAD_DIM : (h + 1) * HEAD_DIM], axis=0, keepdims=True
            )
    dq_ref[...] = jnp.zeros_like(dq_ref)
    dk_ref[...] = jnp.zeros_like(dk_ref)
    dv_ref[...] = jnp.zeros_like(dv_ref)

    def pair(kb, qb, diagonal):
        k_at = pl.ds(pl.multiple_of(kb * block, block), block)
        q_at = pl.ds(pl.multiple_of(qb * block, block), block)
        key_index = lax.broadcasted_iota(jnp.int32, (block, block), 0) + kb * block
        allowed = key_index >= start_ref[:, q_at]
        if diagonal:
            allowed &= key_index <= lax.broadcasted_iota(jnp.int32, (block, block), 1) + qb * block
        every = range(heads)
        rows = [slice(h * HEAD_DIM, (h + 1) * HEAD_DIM) for h in every]
        q_t = [q_ref[r, q_at] for r in rows]
        do_t = [do_ref[r, q_at] for r in rows]
        scores = [dot(k_ref[k_at, r], q_t[h]) for h, r in enumerate(rows)]
        dprobs = [dot(v_ref[k_at, r], do_t[h]) for h, r in enumerate(rows)]
        probs = [
            jnp.exp(jnp.where(allowed, scores[h], NEG) - lse_ref[h : h + 1, q_at]) for h in every
        ]
        dscores = [
            (probs[h] * (dprobs[h] - delta_ref[h : h + 1, q_at])).astype(BF16) for h in every
        ]
        probs = [p.astype(BF16) for p in probs]
        dv = [dot_nt(do_t[h], probs[h]) for h in every]
        dk = [dot_nt(q_t[h], dscores[h]) for h in every]
        dq = [dot(kt_ref[rows[h], k_at], dscores[h]) for h in every]
        for h in every:
            dv_ref[rows[h], k_at] += dv[h]
            dk_ref[rows[h], k_at] += dk[h]
            dq_ref[rows[h], q_at] += dq[h]

    def outer(kb, carry):
        _, end = doc_of(len_ref, kb * block + block - 1)
        pair(kb, kb, True)

        def inner(qb, c):
            pair(kb, qb, False)
            return c

        lax.fori_loop(kb + 1, (end - 1) // block + 1, inner, 0)
        return carry

    lax.fori_loop(0, SEQ // block, outer, 0)
    cos, sin = cos_ref[...], sin_ref[...]
    for base, ref, scale in ((0, dq_ref, HEAD_DIM ** (-0.5)), (width, dk_ref, 1.0)):
        for row in range(0, width, HEAD_DIM):
            first = ref[row : row + HALF, :] * scale
            second = ref[row + HALF : row + HEAD_DIM, :] * scale
            out_ref[base + row : base + row + HALF, :] = (first * cos + second * sin).astype(BF16)
            out_ref[base + row + HALF : base + row + HEAD_DIM, :] = (
                second * cos - first * sin
            ).astype(BF16)
    out_ref[2 * width :, :] = (0.5 * dv_ref[...]).astype(BF16)


def join_kernel(n, *refs):
    ctx, w_out = refs[:n], refs[n : 2 * n]
    x_ref, gain_ref, mid_ref, normed_ref = refs[2 * n :]
    total = x_ref[...].astype(F32)
    for c, w in zip(ctx, w_out):
        total = total + dot(c[...], w[...])
    mid_ref[...] = total
    normed_ref[...] = (total * row_scale(total) * gain_ref[...]).astype(BF16)


def mlp_kernel(n, tile, *refs):
    normed, grads = refs[:n], refs[n : 2 * n]
    gu_ref, down_ref, mixed_ref, dgate_ref, dup_ref, gn_ref = refs[2 * n :]
    for j in range(n):

        def step(t, carry, j=j):
            rows = pl.ds(pl.multiple_of(t * tile, tile), tile)
            tokens = normed[j][rows, :]
            gate = dot_nt(tokens, gu_ref[0])
            up = dot_nt(tokens, gu_ref[1])
            gm = dot_nt(grads[j][rows, :], down_ref[...])
            sig = 1.0 / (1.0 + jnp.exp(-gate))
            act = gate * sig
            mixed_ref[j, rows, :] = (act * up).astype(BF16)
            dup = (gm * act).astype(BF16)
            dgate = (gm * up * sig * (1.0 + gate * (1.0 - sig))).astype(BF16)
            dup_ref[j, rows, :] = dup
            dgate_ref[j, rows, :] = dgate
            gn_ref[j, rows, :] = (dot(dgate, gu_ref[0]) + dot(dup, gu_ref[1])).astype(BF16)
            return carry

        lax.fori_loop(0, normed[j].shape[0] // tile, step, 0)


def mlp_out_kernel(tile, mixed_ref, down_ref, out_ref):
    for j in range(mixed_ref.shape[0]):

        def step(t, carry, j=j):
            rows = pl.ds(pl.multiple_of(t * tile, tile), tile)
            out_ref[j, rows, :] = dot(mixed_ref[j, rows, :], down_ref[...]).astype(BF16)
            return carry

        lax.fori_loop(0, mixed_ref.shape[1] // tile, step, 0)


def mlp_weights_kernel(n, out_ref_count, *refs):
    normed, grads = refs[:n], refs[n : 2 * n]
    groups = refs[2 * n : -2]
    out_ref, acc_ref = refs[-2], refs[-1]
    hidden = acc_ref.shape[0]
    lanes = out_ref.shape[2]
    per = len(groups) // 3
    for which in range(3):
        for j in range(n):
            ref = groups[which * per + j // (n // per)]
            left = ref[j % (n // per)]
            right = (grads if which == 2 else normed)[j][...]
            part = dot_tn(left, right)
            if j == 0:
                acc_ref[...] = part
            else:
                acc_ref[...] += part
        for i in range(out_ref.shape[0]):
            out_ref[i, which * hidden : (which + 1) * hidden, :] = acc_ref[
                :, i * lanes : (i + 1) * lanes
            ].astype(BF16)


def middle_back_kernel(n, *refs):
    gn_ref, mid_ref, og_ref, gain_ref = refs[:4]
    w_out = refs[4 : 4 + n]
    gmid_ref, ga_ref, gain_out, *gctx = refs[4 + n :]
    mid = mid_ref[...]
    grad = gn_ref[...]
    scale = row_scale(mid)
    normed = mid * scale
    scaled = grad * gain_ref[...]
    back = scale * (scaled - normed * jnp.mean(scaled * normed, axis=-1, keepdims=True))
    gain_out[...] = jnp.sum(grad * normed, axis=0, keepdims=True)
    gmid = og_ref[...].astype(F32) + back
    gmid_ref[...] = gmid
    ga = gmid.astype(BF16)
    ga_ref[...] = ga
    for w, out in zip(w_out, gctx):
        out[...] = dot_nt(w[...], ga).astype(BF16)


def out_weight_kernel(n, *refs):
    ctx, ga_ref, outs = refs[:n], refs[n], refs[n + 1 :]
    for c, out in zip(ctx, outs):
        out[...] = dot_tn(c[...], ga_ref[...]).astype(BF16)


def unproject_kernel(n, tile, me_ref, *refs):
    xs = refs[:n]
    gp_ref, w_ref, gain_ref, gn_ref, dv_ref, gain_out = refs[n:]
    shard = xs[0].shape[0]
    width = w_ref.shape[0] // 3
    gain_out[...] = jnp.zeros_like(gain_out)
    for j in range(n):

        def step(t, carry, j=j):
            rows = pl.ds(pl.multiple_of(t * tile, tile), tile)
            at = pl.ds(pl.multiple_of((me_ref[0] ^ j) * shard + t * tile, tile), tile)
            gp = gp_ref[:, at].T
            dv_ref[j, rows, :] = gp[:, 2 * width :]
            grad = dot(gp, w_ref[...])
            gn_ref[j, rows, :] = grad.astype(BF16)
            stream = xs[j][rows, :].astype(F32)
            gain_out[...] += jnp.sum(grad * (stream * row_scale(stream)), axis=0, keepdims=True)
            return carry

        lax.fori_loop(0, shard // tile, step, 0)


def qkv_weight_kernel(n, me_ref, *refs):
    xs = refs[:n]
    gp_ref, gain_ref, out_ref, acc_ref = refs[n:]
    shard = xs[0].shape[0]
    lanes = out_ref.shape[2]
    for j in range(n):
        at = pl.ds(pl.multiple_of((me_ref[0] ^ j) * shard, shard), shard)
        stream = xs[j][...].astype(F32)
        normed = (stream * row_scale(stream) * gain_ref[...]).astype(BF16)
        part = dot(gp_ref[:, at], normed)
        if j == 0:
            acc_ref[...] = part
        else:
            acc_ref[...] += part
    for i in range(out_ref.shape[0]):
        out_ref[i] = acc_ref[:, i * lanes : (i + 1) * lanes].astype(BF16)


def input_back_kernel(gn_ref, x_ref, gain_ref, gmid_ref, out_ref):
    stream = x_ref[...].astype(F32)
    scale = row_scale(stream)
    normed = stream * scale
    scaled = gn_ref[...] * gain_ref[...]
    back = scale * (scaled - normed * jnp.mean(scaled * normed, axis=-1, keepdims=True))
    out_ref[...] = gmid_ref[...] + back


def doc_tables(lengths):
    index = jnp.arange(SEQ, dtype=jnp.int32)
    ends = jnp.cumsum(lengths)
    begins = ends - lengths
    starts = jnp.max(jnp.where(begins[:, None] <= index[None, :], begins[:, None], 0), axis=0)
    inverse = jnp.exp(jnp.arange(HALF, dtype=F32) * (-2.0 * math.log(10000.0) / HEAD_DIM))
    angles = (index - starts).astype(F32)[None, :] * inverse[:, None]
    return starts[None, :], jnp.cos(angles), jnp.sin(angles)


def local(
    n,
    n_dp,
    hidden_in,
    first_values,
    doc_lengths,
    out_grad,
    qkv_weight,
    out_weight,
    gate_up_weight,
    down_weight,
    attn_gain,
    mlp_gain,
):
    shard, width = hidden_in.shape[1], qkv_weight.shape[2]
    hidden = down_weight.shape[0]
    lanes = qkv_weight.shape[0]
    dim = hidden_in.shape[2]
    tile = min(256, shard)
    me = lax.axis_index("head").reshape(1).astype(jnp.int32)
    dp = lax.axis_index("dp").reshape(1).astype(jnp.int32)
    x_own, og_own = hidden_in[0], out_grad[0]
    gain_one, gain_two = attn_gain[None, :], mlp_gain[None, :]

    xs = gather_relative(x_own, "head", n)
    qkv_out = jnp.concatenate(
        [qkv_weight.transpose(1, 2, 0).reshape(3 * width, lanes), out_weight], axis=0
    )
    gathered = gather_columns(qkv_out, dp, n_dp)
    if isinstance(gathered, list):
        gathered = jnp.concatenate(gathered, axis=0)
    w_qkv, w_out = gathered[: 3 * width], gathered[3 * width :]
    mlp_rows = jnp.concatenate(
        [gate_up_weight.transpose(1, 2, 0).reshape(2 * hidden, lanes), down_weight], axis=0
    )
    mlp_all = lax.all_gather(mlp_rows, "dp", axis=1, tiled=True)
    w_gu = mlp_all[: 2 * hidden].reshape(2, hidden, dim)
    w_down = mlp_all[2 * hidden :]

    fv_parts = [
        lax.dynamic_slice(first_values[0], (0, (me[0] ^ j) * width), (shard, width))
        for j in range(n)
    ]
    fvs = exchange_relative(fv_parts, "head", n)
    starts, cos, sin = doc_tables(doc_lengths[0])

    q_t, keys, k_t, values, v_t = call(
        functools.partial(project_kernel, n, tile),
        "project",
        [(me, SMEM)] + in_vmem(*xs, *fvs, w_qkv, gain_one, cos, sin),
        [
            shape((width, SEQ), BF16),
            shape((SEQ, width), BF16),
            shape((width, SEQ), BF16),
            shape((SEQ, width), BF16),
            shape((width, SEQ), BF16),
        ],
        flops=6 * SEQ * dim * width,
    )
    ctx, o_t, lse = attend(doc_lengths, me, q_t, keys, v_t, starts, shard)

    ctxs = exchange_relative([ctx[j] for j in range(n)], "head", n)
    w_outs = gather_relative(w_out, "head", n)
    middle, normed_two = call(
        functools.partial(join_kernel, n),
        "join",
        in_vmem(*ctxs, *w_outs, x_own, gain_two),
        [shape((shard, dim), F32), shape((shard, dim), BF16)],
        flops=2 * shard * dim * dim,
    )

    ogs = gather_relative(og_own, "head", n)
    normed = gather_relative(normed_two, "head", n)
    half = n // 2
    mlp_flops = 10 * half * shard * dim * hidden
    groups = []
    for lo in (0, half):
        groups.append(
            call(
                functools.partial(mlp_kernel, half, tile),
                "mlp",
                in_vmem(*normed[lo : lo + half], *ogs[lo : lo + half], w_gu, w_down),
                [shape((half, shard, hidden), BF16)] * 3 + [shape((half, shard, dim), BF16)],
                flops=mlp_flops,
            )
        )
    gn_parts = [g[3][j] for g in groups for j in range(half)]
    gn_two = sum_relative(gn_parts, "head", n)

    mlp_parts = []
    for g in groups:
        (out,) = call(
            functools.partial(mlp_out_kernel, tile),
            "mlp_out",
            in_vmem(g[0], w_down),
            [shape((half, shard, dim), BF16)],
            flops=2 * half * shard * dim * hidden,
        )
        mlp_parts += [out[j] for j in range(half)]
    (mlp_grads,) = call(
        functools.partial(mlp_weights_kernel, n, 1),
        "mlp_weights",
        in_vmem(*normed, *ogs, *[groups[i][k] for k in (1, 2, 0) for i in range(2)]),
        [shape((n_dp, 3 * hidden, lanes), BF16)],
        [pltpu.VMEM((hidden, dim), F32)],
        flops=6 * SEQ * dim * hidden,
    )
    mlp_grads = lax.psum_scatter(mlp_grads, "dp", scatter_dimension=0, tiled=False).astype(F32)

    layer_out = (middle + sum_relative(mlp_parts, "head", n)).astype(BF16)

    grad_middle, ga, gain_two_part, *gctx = call(
        functools.partial(middle_back_kernel, n),
        "middle_back",
        in_vmem(gn_two, middle, og_own, gain_two, *w_outs),
        [shape((shard, dim), F32), shape((shard, dim), BF16), shape((1, dim), F32)]
        + [shape((width, shard), BF16)] * n,
        flops=2 * shard * dim * dim,
    )
    dos = exchange_relative(gctx, "head", n)
    out_parts = call(
        functools.partial(out_weight_kernel, n),
        "out_weight",
        in_vmem(*ctxs, ga),
        [shape((width, dim), BF16)] * n,
        flops=2 * shard * dim * dim,
    )
    out_sum = sum_relative(out_parts, "head", n).astype(BF16)

    (gp_t,) = call(
        functools.partial(attend_back_kernel, n, min(256, shard)),
        "attend_back",
        [(doc_lengths, SMEM), (me, SMEM)]
        + in_vmem(q_t, keys, k_t, values, o_t, lse, starts, cos, sin, *dos),
        [shape((3 * width, SEQ), BF16)],
        [pltpu.VMEM((width, SEQ), F32)] * 3
        + [pltpu.VMEM((width, SEQ), BF16), pltpu.VMEM((width // HEAD_DIM, SEQ), F32)],
        flops=20 * SEQ * SEQ * width,
    )
    gn_one_parts, dv, gain_one_part = call(
        functools.partial(unproject_kernel, n, tile),
        "unproject",
        [(me, SMEM)] + in_vmem(*xs, gp_t, w_qkv, gain_one),
        [shape((n, shard, dim), BF16), shape((n, shard, width), BF16), shape((1, dim), F32)],
        flops=6 * SEQ * dim * width,
    )
    gn_one = sum_relative([gn_one_parts[j] for j in range(n)], "head", n)
    (qkv_grads,) = call(
        functools.partial(qkv_weight_kernel, n),
        "qkv_weight",
        [(me, SMEM)] + in_vmem(*xs, gp_t, gain_one),
        [shape((n_dp, 3 * width, lanes), BF16)],
        [pltpu.VMEM((3 * width, dim), F32)],
        flops=6 * SEQ * dim * width,
    )
    attn_grads = jnp.concatenate(
        [qkv_grads, out_sum.reshape(width, n_dp, lanes).transpose(1, 0, 2)], axis=1
    )
    attn_grads = lax.psum_scatter(attn_grads, "dp", scatter_dimension=0, tiled=False).astype(F32)
    gains = lax.psum(jnp.concatenate([gain_one_part, gain_two_part], axis=0), ("dp", "head"))

    dvs = jnp.stack(exchange_relative([dv[j] for j in range(n)], "head", n))
    first_grad = jnp.concatenate(
        [lax.dynamic_index_in_dim(dvs, me[0] ^ i, keepdims=False) for i in range(n)], axis=1
    ).astype(F32)
    (input_grad,) = call(
        input_back_kernel,
        "input_back",
        in_vmem(gn_one, x_own, gain_one, grad_middle),
        [shape((shard, dim), F32)],
    )
    return (
        layer_out[None],
        input_grad[None],
        first_grad[None],
        attn_grads[: 3 * width].reshape(3, width, lanes).transpose(2, 0, 1),
        attn_grads[3 * width :],
        mlp_grads[: 2 * hidden].reshape(2, hidden, lanes).transpose(2, 0, 1),
        mlp_grads[2 * hidden :],
        gains[0],
        gains[1],
    )


def solution(mesh):
    tokens = P("dp", "head", None)
    columns = P("dp", None, "head")
    rows = P("head", "dp")
    return jax.shard_map(
        functools.partial(local, mesh.shape["head"], mesh.shape["dp"]),
        mesh=mesh,
        in_specs=(tokens, tokens, P("dp", None), tokens, columns, rows, columns, rows, P(), P()),
        out_specs=(tokens, tokens, tokens, columns, rows, columns, rows, P(), P()),
        check_vma=False,
    )
```

```python
import functools
import math

import jax
import jax.numpy as jnp
from jax import lax
from jax.experimental import pallas as pl
from jax.experimental.pallas import tpu as pltpu
from jax.sharding import PartitionSpec as P

HEAD_DIM = 64
HALF = HEAD_DIM // 2
SEQ = 2048
NDOC = 16
NORM_EPS = 1e-06
NEG = -1e30
F32 = jnp.float32
BF16 = jnp.bfloat16
VMEM_LIMIT = 58 << 20

VMEM = pl.BlockSpec(memory_space=pltpu.VMEM)
SMEM = pl.BlockSpec(memory_space=pltpu.SMEM)


def shape(dims, dtype):
    return jax.ShapeDtypeStruct(dims, dtype)


def dot(a, b):
    return jnp.dot(a, b, preferred_element_type=F32)


def dot_nt(a, b):
    return lax.dot_general(a, b, (((1,), (1,)), ((), ())), preferred_element_type=F32)


def dot_tn(a, b):
    return lax.dot_general(a, b, (((0,), (0,)), ((), ())), preferred_element_type=F32)


def padded(dims, dtype):
    size = jnp.dtype(dtype).itemsize
    *lead, rows, lanes = (1, 1, *dims)
    return math.prod(lead) * (-(-rows // 8) * 8) * (-(-lanes // 128) * 128) * size


def call(body, name, ins, outs, scratch=(), flops=0, after=()):
    held = [(a.shape, a.dtype) for a, s in ins if s is VMEM] + [(o.shape, o.dtype) for o in outs]
    held += [(v.shape, v.dtype) for v in scratch]
    need = sum(padded(*h) for h in held)
    skip = len(ins)

    def kernel(*refs):
        body(*refs[:skip], *refs[skip + len(after) :])

    return pl.pallas_call(
        kernel,
        name=name,
        out_shape=outs,
        in_specs=[s for _, s in ins] + [pl.BlockSpec(memory_space=pl.ANY)] * len(after),
        out_specs=[VMEM] * len(outs),
        scratch_shapes=list(scratch),
        compiler_params=pltpu.CompilerParams(vmem_limit_bytes=VMEM_LIMIT),
        cost_estimate=pl.CostEstimate(flops=flops, bytes_accessed=need, transcendentals=0),
    )(*[a for a, _ in ins], *after)


def grid_call(body, name, steps, scalars, ins, outs, scratch=(), flops=0, after=()):
    moved = sum(padded(a.shape, a.dtype) for a, _, _ in ins)
    moved += sum(padded(o.shape, o.dtype) for o, _, _ in outs)
    skip = len(scalars) + len(ins)

    def kernel(*refs):
        body(*refs[:skip], *refs[skip + len(after) :])

    return pl.pallas_call(
        kernel,
        name=name,
        grid_spec=pltpu.PrefetchScalarGridSpec(
            num_scalar_prefetch=len(scalars),
            grid=(steps,),
            in_specs=[pl.BlockSpec(b, f) for _, b, f in ins]
            + [pl.BlockSpec(memory_space=pl.ANY)] * len(after),
            out_specs=[pl.BlockSpec(b, f) for _, b, f in outs],
            scratch_shapes=list(scratch),
        ),
        out_shape=[o for o, _, _ in outs],
        compiler_params=pltpu.CompilerParams(vmem_limit_bytes=VMEM_LIMIT),
        cost_estimate=pl.CostEstimate(flops=flops, bytes_accessed=moved, transcendentals=0),
    )(*scalars, *[a for a, _, _ in ins], *after)


def whole(*arrays):
    return [(a, a.shape, lambda i, *s, d=len(a.shape): (0,) * d) for a in arrays]


def by_rows(tile, *arrays):
    return [(a, (tile, a.shape[1]), lambda i, *s: (i, 0)) for a in arrays]


def by_chunk(tile, *arrays):
    per = arrays[0].shape[0] // tile
    return [
        (a, (tile, a.shape[1]), lambda i, *s, j=j: (jnp.clip(i - j * per, 0, per - 1), 0))
        for j, a in enumerate(arrays)
    ]


def token_tile(per):
    return lambda i, me: (i // per ^ me[0]) * per + i % per


def gate(value, after):
    if not after:
        return value
    return pl.pallas_call(
        lambda *refs: None,
        name="gate",
        out_shape=shape(value.shape, value.dtype),
        in_specs=[pl.BlockSpec(memory_space=pl.ANY)] * (1 + len(after)),
        out_specs=pl.BlockSpec(memory_space=pl.ANY),
        input_output_aliases={0: 0},
    )(value, *after)


def in_vmem(*arrays):
    return [(a, VMEM) for a in arrays]


def row_scale(stream):
    return lax.rsqrt(jnp.mean(stream * stream, axis=-1, keepdims=True) + NORM_EPS)


def swap(value, axis, size, bit):
    return lax.ppermute(value, axis, [(i, i ^ bit) for i in range(size)])


def bits_down(size):
    return [1 << b for b in reversed(range(size.bit_length() - 1))]


def gather_relative(value, axis, size, hold=None):
    parts = {0: value}
    for bit in bits_down(size):
        moved = {0: swap(value, axis, size, bit)}
        if bit == 1 and hold:
            after = hold(parts[0], moved[0])
            parts.update({j: gate(v, after) for j, v in parts.items() if j})
        moved.update({j: swap(v, axis, size, bit) for j, v in parts.items() if j})
        parts.update({j | bit: v for j, v in moved.items()})
    return [parts[j] for j in range(size)]


def fold_kernel(*refs):
    *terms, out = refs
    out[...] = sum(t[...].astype(F32) for t in terms).astype(BF16)


def sum_relative(parts, axis, size, after=()):
    parts = dict(enumerate([[p] for p in parts]))
    bit, sent = 1, []
    while bit < size:
        kept = {}
        for j in sorted((j for j in parts if not j & bit), reverse=True):
            away = parts[j | bit]
            if len(away) > 1:
                out = [shape(away[0].shape, BF16)]
                away = call(fold_kernel, "fold", in_vmem(*away), out, after=after)
                sent += away
            kept[j] = parts[j] + [swap(away[0], axis, size, bit)]
        parts = kept
        bit *= 2
    return parts[0], sent


def exchange_relative(parts, axis, size):
    return [p if j == 0 else swap(p, axis, size, j) for j, p in enumerate(parts)]


def sum_everywhere(value, sizes):
    for axis, size in sizes:
        for bit in reversed(bits_down(size)):
            value = value + swap(value, axis, size, bit)
    return value


def column_orders(size):
    bits = bits_down(size)
    return [bits, bits[-1:] + bits[:-1]]


def ring_sources(dp, size):
    line = size // 2
    place = dp // 2 ^ dp // 4
    held = [jnp.remainder(place - k, line) for k in range(line)]
    held = [2 * (p ^ p // 2) for p in held]
    return jnp.stack([h + (dp & 1) for h in held] + [h + 1 - (dp & 1) for h in held])


def gather_columns(rows, size):
    line = size // 2
    ring = [p ^ p // 2 for p in range(line)]
    pairs = [(2 * ring[p] + i, 2 * ring[(p + 1) % line] + i) for p in range(line) for i in range(2)]
    held = [rows]
    for _ in range(line - 1):
        held.append(lax.ppermute(held[-1], "dp", pairs))
    return held + [swap(h, "dp", size, 1) for h in held]


def column_places(size, bits):
    places = [0]
    for bit in reversed(bits):
        places = places + [j | bit for j in places]
    return places


def scatter_columns(kept, sent, size, bits, after):
    for bit in bits:
        total = kept.astype(F32) + swap(sent, "dp", size, bit).astype(F32)
        if bit == bits[-1]:
            return total[0]
        half = total.shape[0] // 2
        kept, sent = total[:half], total[half:].astype(BF16)
        if bit == bits[0]:
            sent = gate(sent, after)


def pick(step, per, refs, out_ref):
    for j, ref in enumerate(refs):

        @pl.when(step // per == j)
        def _(ref=ref):
            out_ref[...] = ref[...]


def join_columns(from_ref, parts, outs):
    for i, part in enumerate(parts):
        lanes = part.shape[1]
        at = slice(None)
        if len(parts) > 1:
            at = pl.ds(pl.multiple_of(from_ref[i] * lanes, 128), lanes)
        for row, rows, out in outs:
            out[:, at] = part[row : row + rows, :]


def project_kernel(n, per, count, me_ref, from_ref, *refs):
    xs, fvs = refs[:n], refs[n : 2 * n]
    parts = refs[2 * n : 2 * n + count]
    gain_ref, cos_ref, sin_ref, q_out, k_out, kt_out, v_out, vt_out, w_ref, wo_ref, x_ref, fv_ref = (
        refs[2 * n + count :]
    )
    width = q_out.shape[0]
    step = pl.program_id(0)

    @pl.when(step == 0)
    def _():
        join_columns(from_ref, parts, [(0, 3 * width, w_ref), (3 * width, width, wo_ref)])

    pick(step, per, xs, x_ref)
    pick(step, per, fvs, fv_ref)
    stream = x_ref[...].astype(F32)
    normed = (stream * row_scale(stream) * gain_ref[...]).astype(BF16)
    qk = dot_nt(w_ref[: 2 * width, :], normed)
    cos, sin = cos_ref[...], sin_ref[...]
    turned = []
    for row in range(0, 2 * width, HEAD_DIM):
        first, second = qk[row : row + HALF], qk[row + HALF : row + HEAD_DIM]
        turned += [first * cos - second * sin, second * cos + first * sin]
    turned = jnp.concatenate(turned, axis=0)
    q_out[...] = (turned[:width] * HEAD_DIM ** (-0.5)).astype(BF16)
    keys = turned[width:]
    kt_out[...] = keys.astype(BF16)
    k_out[...] = keys.T.astype(BF16)
    values = 0.5 * dot_nt(normed, w_ref[2 * width :, :]) + 0.5 * fv_ref[...].astype(F32)
    v_out[...] = values.astype(BF16)
    vt_out[...] = values.T.astype(BF16)


def doc_of(len_ref, token):
    run, first, last = jnp.int32(0), jnp.int32(0), jnp.int32(SEQ)
    for doc in range(NDOC):
        end = run + len_ref[0, doc]
        inside = (token >= run) & (token < end)
        first, last = jnp.where(inside, run, first), jnp.where(inside, end, last)
        run = end
    return first, last


def attend_kernel(bq, per, heads, skip, len_ref, me_ref, q_ref, k_ref, vt_ref, start_ref, *refs):
    *ctx_refs, ot_ref, lse_ref, s_ref = refs[skip:]
    bk = bq
    block = pl.program_id(0)
    first, _ = doc_of(len_ref, block * bq)
    starts = start_ref[...]

    def score(kb, tops, diagonal):
        at = pl.ds(pl.multiple_of(kb * bk, bk), bk)
        key_index = lax.broadcasted_iota(jnp.int32, (bk, bq), 0) + kb * bk
        allowed = key_index >= starts
        if diagonal:
            allowed &= key_index <= lax.broadcasted_iota(jnp.int32, (bk, bq), 1) + block * bq
        out = []
        for h in range(heads):
            rows = slice(h * HEAD_DIM, (h + 1) * HEAD_DIM)
            scores = jnp.where(allowed, dot(k_ref[at, rows], q_ref[rows, :]), NEG)
            s_ref[h, at, :] = scores
            out.append(jnp.maximum(tops[h], jnp.max(scores.reshape(bk // 8, 8, bq), axis=0)))
        return tuple(out)

    tops = score(block, tuple(jnp.full((8, bq), NEG, F32) for _ in range(heads)), True)
    tops = lax.fori_loop(first // bk, block, lambda kb, c: score(kb, c, False), tops)
    tops = [jnp.max(t, axis=0, keepdims=True) for t in tops]

    def gather(kb, carry):
        at = pl.ds(pl.multiple_of(kb * bk, bk), bk)
        out = []
        for h in range(heads):
            rows = slice(h * HEAD_DIM, (h + 1) * HEAD_DIM)
            total, acc = carry[h]
            probs = jnp.exp(s_ref[h, at, :] - tops[h])
            total = total + jnp.sum(probs.reshape(bk // 8, 8, bq), axis=0)
            out.append((total, acc + dot(vt_ref[rows, at], probs.astype(BF16))))
        return tuple(out)

    zero = tuple((jnp.zeros((8, bq), F32), jnp.zeros((HEAD_DIM, bq), F32)) for _ in range(heads))
    sums = lax.fori_loop(first // bk, block + 1, gather, zero)
    outs = []
    for h in range(heads):
        total = jnp.sum(sums[h][0], axis=0, keepdims=True)
        outs.append(sums[h][1] * (1.0 / total))
        lse_ref[h : h + 1, :] = tops[h] + jnp.log(total)
    out = jnp.concatenate(outs, axis=0)
    ot_ref[...] = out.astype(BF16)
    out = out.T.astype(BF16)
    for j, ref in enumerate(ctx_refs):

        @pl.when((block // per) ^ me_ref[0] == j)
        def _(ref=ref):
            ref[pl.ds(pl.multiple_of((block % per) * bq, bq), bq), :] = out


def attend(lengths, me, q_t, keys, v_t, starts, shard, after):
    width = q_t.shape[0]
    heads = width // HEAD_DIM
    bq = min(512, shard)
    per = shard // bq
    n = SEQ // shard
    spec = pltpu.PrefetchScalarGridSpec(
        num_scalar_prefetch=2,
        grid=(SEQ // bq,),
        in_specs=[
            pl.BlockSpec((width, bq), lambda i, l, h: (0, i)),
            pl.BlockSpec((SEQ, width), lambda i, l, h: (0, 0)),
            pl.BlockSpec((width, SEQ), lambda i, l, h: (0, 0)),
            pl.BlockSpec((1, bq), lambda i, l, h: (0, i)),
        ]
        + [pl.BlockSpec(memory_space=pl.ANY)] * len(after),
        out_specs=[
            *[pl.BlockSpec((shard, width), lambda i, l, h: (0, 0))] * n,
            pl.BlockSpec((width, bq), lambda i, l, h: (0, i)),
            pl.BlockSpec((heads, bq), lambda i, l, h: (0, i)),
        ],
        scratch_shapes=[pltpu.VMEM((heads, SEQ, bq), F32)],
    )
    return pl.pallas_call(
        functools.partial(attend_kernel, bq, per, heads, len(after)),
        name="attend",
        grid_spec=spec,
        out_shape=[
            *[shape((shard, width), BF16)] * n,
            shape((width, SEQ), BF16),
            shape((heads, SEQ), F32),
        ],
        compiler_params=pltpu.CompilerParams(vmem_limit_bytes=VMEM_LIMIT),
        cost_estimate=pl.CostEstimate(
            flops=16 * SEQ * SEQ * width, bytes_accessed=8 * SEQ * width, transcendentals=0
        ),
    )(lengths, me, q_t, keys, v_t, starts, *after)


def attend_back_kernel(n, block, len_ref, me_ref, *refs):
    q_ref, k_ref, kt_ref, v_ref, ot_ref, lse_ref, start_ref, cos_ref, sin_ref = refs[:9]
    dos = refs[9 : 9 + n]
    out_ref, *first_refs = refs[9 + n : 10 + 2 * n]
    dq_ref, dk_ref, dv_ref, do_ref, delta_ref = refs[10 + 2 * n :]
    width = q_ref.shape[0]
    heads = width // HEAD_DIM
    shard = SEQ // n
    for j in range(n):
        at = pl.ds(pl.multiple_of((me_ref[0] ^ j) * shard, shard), shard)
        do_ref[:, at] = dos[j][...]
        product = dos[j][...].astype(F32) * ot_ref[:, at].astype(F32)
        for h in range(heads):
            delta_ref[h : h + 1, at] = jnp.sum(
                product[h * HEAD_DIM : (h + 1) * HEAD_DIM], axis=0, keepdims=True
            )
    dq_ref[...] = jnp.zeros_like(dq_ref)
    dk_ref[...] = jnp.zeros_like(dk_ref)
    dv_ref[...] = jnp.zeros_like(dv_ref)

    def pair(kb, qb, diagonal):
        k_at = pl.ds(pl.multiple_of(kb * block, block), block)
        q_at = pl.ds(pl.multiple_of(qb * block, block), block)
        key_index = lax.broadcasted_iota(jnp.int32, (block, block), 0) + kb * block
        allowed = key_index >= start_ref[:, q_at]
        if diagonal:
            allowed &= key_index <= lax.broadcasted_iota(jnp.int32, (block, block), 1) + qb * block
        every = range(heads)
        rows = [slice(h * HEAD_DIM, (h + 1) * HEAD_DIM) for h in every]
        q_t = [q_ref[r, q_at] for r in rows]
        do_t = [do_ref[r, q_at] for r in rows]
        scores = [dot(k_ref[k_at, r], q_t[h]) for h, r in enumerate(rows)]
        dprobs = [dot(v_ref[k_at, r], do_t[h]) for h, r in enumerate(rows)]
        probs = [
            jnp.exp(jnp.where(allowed, scores[h], NEG) - lse_ref[h : h + 1, q_at]) for h in every
        ]
        dscores = [
            (probs[h] * (dprobs[h] - delta_ref[h : h + 1, q_at])).astype(BF16) for h in every
        ]
        probs = [p.astype(BF16) for p in probs]
        dv = [dot_nt(do_t[h], probs[h]) for h in every]
        dk = [dot_nt(q_t[h], dscores[h]) for h in every]
        dq = [dot(kt_ref[rows[h], k_at], dscores[h]) for h in every]
        for h in every:
            dv_ref[rows[h], k_at] += dv[h]
            dk_ref[rows[h], k_at] += dk[h]
            dq_ref[rows[h], q_at] += dq[h]

    def outer(kb, carry):
        _, end = doc_of(len_ref, kb * block + block - 1)
        pair(kb, kb, True)

        def inner(qb, c):
            pair(kb, qb, False)
            return c

        lax.fori_loop(kb + 1, (end - 1) // block + 1, inner, 0)
        return carry

    lax.fori_loop(0, SEQ // block, outer, 0)
    cos, sin = cos_ref[...], sin_ref[...]
    for base, ref, scale in ((0, dq_ref, HEAD_DIM ** (-0.5)), (width, dk_ref, 1.0)):
        for row in range(0, width, HEAD_DIM):
            first = ref[row : row + HALF, :] * scale
            second = ref[row + HALF : row + HEAD_DIM, :] * scale
            out_ref[base + row : base + row + HALF, :] = (first * cos + second * sin).astype(BF16)
            out_ref[base + row + HALF : base + row + HEAD_DIM, :] = (
                second * cos - first * sin
            ).astype(BF16)
    for j in range(n):
        at = pl.ds(pl.multiple_of((me_ref[0] ^ j) * shard, shard), shard)
        grad = 0.5 * dv_ref[:, at]
        out_ref[2 * width :, at] = grad.astype(BF16)
        first_refs[j][...] = grad.T.astype(BF16)


def add_rows(out_ref, rows):
    total = jnp.sum(rows, axis=0, keepdims=True)

    @pl.when(pl.program_id(0) == 0)
    def _():
        out_ref[...] = total

    @pl.when(pl.program_id(0) > 0)
    def _():
        out_ref[...] += total


def join_kernel(n, *refs):
    ctx, w_out = refs[:n], refs[n : 2 * n]
    x_ref, gain_ref, mid_ref, normed_ref = refs[2 * n :]
    total = x_ref[...].astype(F32)
    for c, w in zip(ctx, w_out):
        total = total + dot(c[...], w[...])
    mid_ref[...] = total
    normed_ref[...] = (total * row_scale(total) * gain_ref[...]).astype(BF16)


def mlp_kernel(n, per, count, from_ref, *refs):
    normed, grads = refs[:n], refs[n : 2 * n]
    parts = refs[2 * n : 2 * n + count]
    outs, (tokens_ref, og_ref) = refs[2 * n + count : -2], refs[-2:]
    mixed_ref, dgate_ref, dup_ref, *gn_refs = outs
    w_ref = parts[0]
    step = pl.program_id(0)
    if count > 1:
        *gn_refs, w_ref = gn_refs

        @pl.when(step == 0)
        def _():
            join_columns(from_ref, parts, [(0, w_ref.shape[0], w_ref)])

    pick(step, per, normed, tokens_ref)
    pick(step, per, grads, og_ref)
    hidden = mixed_ref.shape[1]
    w_gate, w_up, w_down = (w_ref.at[i * hidden : (i + 1) * hidden, :] for i in range(3))
    gate = dot_nt(tokens_ref[...], w_gate[...])
    up = dot_nt(tokens_ref[...], w_up[...])
    gm = dot_nt(og_ref[...], w_down[...])
    sig = 1.0 / (1.0 + jnp.exp(-gate))
    act = gate * sig
    mixed_ref[...] = (act * up).astype(BF16)
    dup = (gm * act).astype(BF16)
    dgate = (gm * up * sig * (1.0 + gate * (1.0 - sig))).astype(BF16)
    dup_ref[...] = dup
    dgate_ref[...] = dgate
    back = (dot(dgate, w_gate[...]) + dot(dup, w_up[...])).astype(BF16)
    for j, ref in enumerate(gn_refs):

        @pl.when(step // per == j)
        def _(ref=ref):
            ref[...] = back


def mlp_rest_kernel(n, tile, *refs):
    normed, grads = refs[:n], refs[n : 2 * n]
    dgates, dups, mixeds = refs[2 * n : 2 * n + 2], refs[2 * n + 2 : 2 * n + 4], refs[2 * n + 4 : 2 * n + 6]
    w_ref, *outs, grad_ref, acc_ref = refs[2 * n + 6 :]
    half = n // 2
    shard = normed[0].shape[0]
    hidden = acc_ref.shape[0]
    lanes = grad_ref.shape[2]
    w_down = w_ref.at[2 * hidden :, :]
    for j in range(n):

        def step(t, carry, j=j):
            rows = pl.ds(pl.multiple_of(t * tile, tile), tile)
            part = mixeds[j // half][pl.ds(j % half * shard + t * tile, tile), :]
            outs[j][rows, :] = dot(part, w_down[...]).astype(BF16)
            return carry

        lax.fori_loop(0, outs[j].shape[0] // tile, step, 0)
    for which, (lefts, rights) in enumerate(((dgates, normed), (dups, normed), (mixeds, grads))):
        for j in range(n):
            left = lefts[j // half][j % half * shard : (j % half + 1) * shard, :]
            part = dot_tn(left, rights[j][...])
            if j == 0:
                acc_ref[...] = part
            else:
                acc_ref[...] += part
        for i in range(grad_ref.shape[0]):
            grad_ref[i, which * hidden : (which + 1) * hidden, :] = acc_ref[
                :, i * lanes : (i + 1) * lanes
            ].astype(BF16)


def middle_back_kernel(n, count, *refs):
    mid_ref, og_ref, gain_ref = refs[:3]
    w_out = refs[3 : 3 + n]
    terms = refs[3 + n : 3 + n + count]
    gmid_ref, ga_ref, gain_out, *gctx = refs[3 + n + count :]
    mid = mid_ref[...]
    grad = sum(t[...].astype(F32) for t in terms)
    scale = row_scale(mid)
    normed = mid * scale
    scaled = grad * gain_ref[...]
    back = scale * (scaled - normed * jnp.mean(scaled * normed, axis=-1, keepdims=True))
    add_rows(gain_out, grad * normed)
    gmid = og_ref[...].astype(F32) + back
    gmid_ref[...] = gmid
    ga = gmid.astype(BF16)
    ga_ref[...] = ga
    for w, out in zip(w_out, gctx):
        out[...] = dot_nt(w[...], ga).astype(BF16)


def out_weight_kernel(n, *refs):
    ctx, ga_ref, outs = refs[:n], refs[n], refs[n + 1 :]
    for c, out in zip(ctx, outs):
        out[...] = dot_tn(c[...], ga_ref[...]).astype(BF16)


def unproject_kernel(n, per, me_ref, *refs):
    xs = refs[:n]
    gp_ref, w_ref = refs[n : n + 2]
    *gns, gain_out, x_ref = refs[n + 2 :]
    step = pl.program_id(0)
    pick(step, per, xs, x_ref)
    grad = dot_tn(gp_ref[...], w_ref[...])
    for j, ref in enumerate(gns):

        @pl.when(step // per == j)
        def _(ref=ref):
            ref[...] = grad.astype(BF16)

    stream = x_ref[...].astype(F32)
    add_rows(gain_out, grad * (stream * row_scale(stream)))


def qkv_weight_kernel(n, count, orders, me_ref, dp_ref, *refs):
    xs = refs[:n]
    gp_ref, gain_ref = refs[n : n + 2]
    terms = refs[n + 2 : n + 2 + count]
    *outs, acc_ref = refs[n + 2 + count :]
    shard = xs[0].shape[0]
    lanes = outs[0].shape[2]
    wide = gp_ref.shape[0]
    for j in range(n):
        at = pl.ds(pl.multiple_of((me_ref[0] ^ j) * shard, shard), shard)
        stream = xs[j][...].astype(F32)
        normed = (stream * row_scale(stream) * gain_ref[...]).astype(BF16)
        part = dot(gp_ref[:, at], normed)
        if j == 0:
            acc_ref[:wide, :] = part
        else:
            acc_ref[:wide, :] += part
    acc_ref[wide:, :] = sum(t[...].astype(F32) for t in terms)
    if orders is None:
        for i in range(outs[0].shape[0]):
            outs[0][i] = acc_ref[:, i * lanes : (i + 1) * lanes].astype(BF16)
        return
    rows = acc_ref.shape[0] // 2
    for half, places in enumerate(orders):
        for i, j in enumerate(places):
            at = pl.ds(pl.multiple_of((dp_ref[0] ^ j) * lanes, 128), lanes)
            out = outs[2 * half + i // (len(places) // 2)]
            out[i % (len(places) // 2)] = acc_ref[half * rows : (half + 1) * rows, at].astype(BF16)


def input_back_kernel(n, count, me_ref, x_ref, gain_ref, gmid_ref, *refs):
    terms, dvs = refs[:count], refs[count : count + (n if len(refs) > count + 1 else 0)]
    out_ref, *first_ref = refs[count + len(dvs) :]
    stream = x_ref[...].astype(F32)
    scale = row_scale(stream)
    normed = stream * scale
    scaled = sum(t[...].astype(F32) for t in terms) * gain_ref[...]
    back = scale * (scaled - normed * jnp.mean(scaled * normed, axis=-1, keepdims=True))
    out_ref[...] = gmid_ref[...] + back
    for j, dv in enumerate(dvs):
        width = dv.shape[1]
        at = pl.ds(pl.multiple_of((me_ref[0] ^ j) * width, 128), width)
        first_ref[0][:, at] = dv[...].astype(F32)


def doc_tables(lengths):
    index = jnp.arange(SEQ, dtype=jnp.int32)
    ends = jnp.cumsum(lengths)
    begins = ends - lengths
    starts = jnp.max(jnp.where(begins[:, None] <= index[None, :], begins[:, None], 0), axis=0)
    inverse = jnp.exp(jnp.arange(HALF, dtype=F32) * (-2.0 * math.log(10000.0) / HEAD_DIM))
    angles = (index - starts).astype(F32)[None, :] * inverse[:, None]
    return starts[None, :], jnp.cos(angles), jnp.sin(angles)


def local(
    n,
    n_dp,
    hidden_in,
    first_values,
    doc_lengths,
    out_grad,
    qkv_weight,
    out_weight,
    gate_up_weight,
    down_weight,
    attn_gain,
    mlp_gain,
):
    shard, width = hidden_in.shape[1], qkv_weight.shape[2]
    hidden = down_weight.shape[0]
    lanes = qkv_weight.shape[0]
    dim = hidden_in.shape[2]
    tile = min(256, shard)
    me = lax.axis_index("head").reshape(1).astype(jnp.int32)
    dp = lax.axis_index("dp").reshape(1).astype(jnp.int32)
    x_own, og_own = hidden_in[0], out_grad[0]
    gain_one, gain_two = attn_gain[None, :], mlp_gain[None, :]

    rows = jnp.concatenate(
        [qkv_weight.transpose(1, 2, 0).reshape(3 * width, lanes), out_weight], axis=0
    )
    mlp_rows = jnp.concatenate(
        [gate_up_weight.transpose(1, 2, 0).reshape(2 * hidden, lanes), down_weight], axis=0
    )
    sources = ring_sources(dp[0], n_dp)
    ringed = lanes % 128 == 0
    if ringed:
        parts = gather_columns(rows, n_dp)
        xs = gather_relative(x_own, "head", n, lambda *x: [parts[n_dp // 2 - 1]])
        mlp_columns = gather_columns(gate(mlp_rows, [xs[n // 2], parts[n_dp // 2 - 1]]), n_dp)
        line = n_dp // 2
        early, middle_ones, late = mlp_columns[1:2], mlp_columns[2:3] + mlp_columns[line:line + 1], mlp_columns[3:]
    else:
        xs = gather_relative(x_own, "head", n)
        parts = [lax.all_gather(rows, "dp", axis=1, tiled=True)]
        mlp_columns = [lax.all_gather(mlp_rows, "dp", axis=1, tiled=True)]
        early, middle_ones, late = [], [], []

    fv_parts = [
        lax.dynamic_slice(first_values[0], (0, (me[0] ^ j) * width), (shard, width))
        for j in range(n)
    ]
    fvs = exchange_relative(fv_parts, "head", n)
    starts, cos, sin = doc_tables(doc_lengths[0])

    per = shard // tile
    at = token_tile(per)
    columns = lambda i, me, *_: (0, at(i, me))
    rows_at = lambda i, me, *_: (at(i, me), 0)
    q_t, keys, k_t, values, v_t, w_qkv, w_out = grid_call(
        functools.partial(project_kernel, n, per, len(parts)),
        "project",
        n * per,
        [me, sources],
        by_chunk(tile, *xs)
        + by_chunk(tile, *fvs)
        + whole(*parts, gain_one)
        + [(t, (HALF, tile), columns) for t in (cos, sin)],
        [
            (shape((width, SEQ), BF16), (width, tile), columns),
            (shape((SEQ, width), BF16), (tile, width), rows_at),
            (shape((width, SEQ), BF16), (width, tile), columns),
            (shape((SEQ, width), BF16), (tile, width), rows_at),
            (shape((width, SEQ), BF16), (width, tile), columns),
        ]
        + whole(shape((3 * width, dim), BF16), shape((width, dim), BF16)),
        [pltpu.VMEM((tile, dim), BF16), pltpu.VMEM((tile, width), BF16)],
        flops=6 * SEQ * dim * width,
        after=early,
    )
    *ctx, o_t, lse = attend(doc_lengths, me, q_t, keys, v_t, starts, shard, middle_ones)

    ctxs = exchange_relative(ctx, "head", n)
    w_outs = gather_relative(w_out, "head", n, lambda *w: [o_t])
    ogs = gather_relative(og_own, "head", n, lambda *g: [o_t])
    middle, normed_two = grid_call(
        functools.partial(join_kernel, n),
        "join",
        per,
        [],
        by_rows(tile, *ctxs) + whole(*w_outs) + by_rows(tile, x_own) + whole(gain_two),
        by_rows(tile, shape((shard, dim), F32), shape((shard, dim), BF16)),
        flops=2 * shard * dim * dim,
        after=ogs[1:] + late,
    )

    half = n // 2
    groups = []

    def mlp(tokens, lo, weights, after=()):
        hiddens = [shape((half * shard, hidden), BF16)] * 3
        made = [shape((3 * hidden, dim), BF16)] if len(weights) > 1 else []
        out = grid_call(
            functools.partial(mlp_kernel, half, per, len(weights)),
            "mlp",
            half * per,
            [sources],
            by_chunk(tile, *tokens) + by_chunk(tile, *ogs[lo : lo + half]) + whole(*weights),
            by_rows(tile, *hiddens)
            + by_chunk(tile, *[shape((shard, dim), BF16)] * half)
            + whole(*made),
            [pltpu.VMEM((tile, dim), BF16)] * 2,
            flops=10 * half * shard * dim * hidden,
            after=after,
        )
        groups.append(out)
        return [out[3]]

    if n == 4:
        normed = gather_relative(
            normed_two, "head", n, lambda *tokens: mlp(tokens, 0, mlp_columns)
        )
    else:
        normed = gather_relative(normed_two, "head", n)
        mlp(normed[:half], 0, mlp_columns)
    w_mlp = groups[0][-1] if len(mlp_columns) > 1 else mlp_columns[0]
    mlp(normed[half:], half, [w_mlp])
    gn_two, gn_sent = sum_relative([p for g in groups for p in g[3 : 3 + half]], "head", n)

    *mlp_parts, mlp_grads = call(
        functools.partial(mlp_rest_kernel, n, tile),
        "mlp_rest",
        in_vmem(*normed, *ogs, *[g[k] for k in (1, 2, 0) for g in groups], w_mlp),
        [shape((shard, dim), BF16)] * n + [shape((n_dp, 3 * hidden, lanes), BF16)],
        [pltpu.VMEM((hidden, dim), F32)],
        flops=8 * SEQ * dim * hidden,
        after=gn_sent,
    )
    mlp_grads = gate(mlp_grads, gn_two[-1:])
    mlp_grads = lax.psum_scatter(mlp_grads, "dp", scatter_dimension=0, tiled=False).astype(F32)

    grad_middle, ga, gain_two_part, *gctx = grid_call(
        functools.partial(middle_back_kernel, n, len(gn_two)),
        "middle_back",
        per,
        [],
        by_rows(tile, middle, og_own)
        + whole(gain_two, *w_outs)
        + by_rows(tile, *gn_two),
        by_rows(tile, shape((shard, dim), F32), shape((shard, dim), BF16))
        + whole(shape((1, dim), F32))
        + [(shape((width, shard), BF16), (width, tile), lambda i: (0, i))] * n,
        flops=2 * shard * dim * dim,
        after=mlp_parts[:1],
    )
    dos = exchange_relative(gctx, "head", n)

    layer_terms, layer_sent = sum_relative(mlp_parts, "head", n, after=dos[2:])
    out_parts = call(
        functools.partial(out_weight_kernel, n),
        "out_weight",
        in_vmem(*ctxs, ga),
        [shape((width, dim), BF16)] * n,
        flops=2 * shard * dim * dim,
    )
    out_terms, out_sent = sum_relative(out_parts, "head", n)

    gp_t, *dv = call(
        functools.partial(attend_back_kernel, n, min(256, shard)),
        "attend_back",
        [(doc_lengths, SMEM), (me, SMEM)]
        + in_vmem(q_t, keys, k_t, values, o_t, lse, starts, cos, sin, *dos),
        [shape((3 * width, SEQ), BF16)] + [shape((shard, width), BF16)] * n,
        [pltpu.VMEM((width, SEQ), F32)] * 3
        + [pltpu.VMEM((width, SEQ), BF16), pltpu.VMEM((width // HEAD_DIM, SEQ), F32)],
        flops=20 * SEQ * SEQ * width,
        after=[*out_sent, *layer_sent],
    )
    dvs = exchange_relative(dv, "head", n)
    unprojected = grid_call(
        functools.partial(unproject_kernel, n, per),
        "unproject",
        n * per,
        [me],
        by_chunk(tile, *xs) + [(gp_t, (3 * width, tile), columns)] + whole(w_qkv),
        by_chunk(tile, *[shape((shard, dim), BF16)] * n) + whole(shape((1, dim), F32)),
        [pltpu.VMEM((tile, dim), BF16)],
        flops=6 * SEQ * dim * width,
        after=[layer_terms[-1], out_terms[-1]],
    )
    *gn_parts, gain_one_part = unprojected
    gn_one, gn_sent = sum_relative(gn_parts, "head", n, after=dvs[1:])
    layer_out = (middle + sum(t.astype(F32) for t in layer_terms)).astype(BF16)

    orders = None
    outs = [shape((n_dp, 4 * width, lanes), BF16)]
    if lanes % 128 == 0:
        bit_orders = [bits[::-1] for bits in column_orders(n_dp)]
        orders = [column_places(n_dp, bits) for bits in bit_orders]
        outs = [shape((n_dp // 2, 2 * width, lanes), BF16)] * 4
    grads = call(
        functools.partial(qkv_weight_kernel, n, len(out_terms), orders),
        "qkv_weight",
        [(me, SMEM), (dp, SMEM)] + in_vmem(*xs, gp_t, gain_one, *out_terms),
        outs,
        [pltpu.VMEM((4 * width, dim), F32)],
        flops=6 * SEQ * dim * width,
        after=gn_sent,
    )
    gains = jnp.concatenate([gain_one_part, gain_two_part], axis=0)
    gains = sum_everywhere(gate(gains, grads[:1]), [("head", n), ("dp", n_dp)])
    if orders is None:
        grads = lax.psum_scatter(grads[0], "dp", scatter_dimension=0, tiled=False).astype(F32)
    else:
        grads = jnp.concatenate(
            [
                scatter_columns(grads[2 * i], grads[2 * i + 1], n_dp, bits, gn_one[-1:])
                for i, bits in enumerate(bit_orders)
            ],
            axis=0,
        )
    small = min(128, shard)
    back_outs = by_rows(small, shape((shard, dim), F32))
    if width % 128 == 0:
        back_outs = back_outs * 2
    input_grad, *first_grad = grid_call(
        functools.partial(input_back_kernel, n, len(gn_one)),
        "input_back",
        shard // small,
        [me],
        by_rows(small, x_own)
        + whole(gain_one)
        + by_rows(small, grad_middle, *gn_one, *(dvs if width % 128 == 0 else [])),
        back_outs,
    )
    if not first_grad:
        stacked = jnp.stack(dvs)
        placed = [
            lax.dynamic_index_in_dim(stacked, me[0] ^ i, keepdims=False) for i in range(n)
        ]
        first_grad = [jnp.concatenate(placed, axis=1).astype(F32)]
    return (
        layer_out[None],
        input_grad[None],
        first_grad[0][None],
        grads[: 3 * width].reshape(3, width, lanes).transpose(2, 0, 1),
        grads[3 * width :],
        mlp_grads[: 2 * hidden].reshape(2, hidden, lanes).transpose(2, 0, 1),
        mlp_grads[2 * hidden :],
        gains[0],
        gains[1],
    )


def solution(mesh):
    tokens = P("dp", "head", None)
    columns = P("dp", None, "head")
    rows = P("head", "dp")
    return jax.shard_map(
        functools.partial(local, mesh.shape["head"], mesh.shape["dp"]),
        mesh=mesh,
        in_specs=(tokens, tokens, P("dp", None), tokens, columns, rows, columns, rows, P(), P()),
        out_specs=(tokens, tokens, tokens, columns, rows, columns, rows, P(), P()),
        check_vma=False,
    )
```

```python
import functools
import math

import jax
import jax.numpy as jnp
from jax import lax
from jax.experimental import pallas as pl
from jax.experimental.pallas import tpu as pltpu
from jax.sharding import PartitionSpec as P

HEAD_DIM = 64
HALF = HEAD_DIM // 2
SEQ = 2048
NDOC = 16
NORM_EPS = 1e-06
NEG = -1e30
F32 = jnp.float32
BF16 = jnp.bfloat16
VMEM_LIMIT = 65280 << 10
COST = pl.CostEstimate(flops=3 << 30, bytes_accessed=1, transcendentals=0)

VMEM = pl.BlockSpec(memory_space=pltpu.VMEM)
SMEM = pl.BlockSpec(memory_space=pltpu.SMEM)


def shape(dims, dtype):
    return jax.ShapeDtypeStruct(dims, dtype)


def dot(a, b):
    return jnp.dot(a, b, preferred_element_type=F32)


def dot_nt(a, b):
    return lax.dot_general(a, b, (((1,), (1,)), ((), ())), preferred_element_type=F32)


def dot_tn(a, b):
    return lax.dot_general(a, b, (((0,), (0,)), ((), ())), preferred_element_type=F32)


class Fetched:
    def __init__(self, source, buffer, sems, pieces):
        self.buffer, self.waiting = buffer, {}
        self.rows = buffer.shape[0] // pieces
        for i in range(pieces):
            at = (pl.ds(i * self.rows, self.rows),) if pieces > 1 else ()
            src, dst = (source.at[at], buffer.at[at]) if at else (source, buffer)
            self.waiting[i] = pltpu.make_async_copy(src, dst, sems.at[i])

    def start(self, i):
        if i in self.waiting:
            self.waiting[i].start()

    def tile(self, first, rows):
        for i in list(self.waiting):
            if first < (i + 1) * self.rows and first + rows > i * self.rows:
                self.waiting.pop(i).wait()
        return self.buffer[first : first + rows, :]

    @property
    def ref(self):
        for i in list(self.waiting):
            self.waiting.pop(i).wait()
        return self.buffer


class Stored:
    def __init__(self, target, buffer, sems):
        self.target, self.ref, self.sems, self.copies = target, buffer, sems, []

    def send(self, *at):
        copy = pltpu.make_async_copy(
            self.ref.at[at], self.target.at[at], self.sems.at[len(self.copies)]
        )
        copy.start()
        self.copies.append(copy)


def far_call(body, name, scalars, near, ins, outs, scratch=(), flops=0, after=()):
    pieces = [i[1] if isinstance(i, tuple) else 1 for i in ins]
    ins = [i[0] if isinstance(i, tuple) else i for i in ins]
    counts = [len(scalars), len(near), len(ins), len(after), len(outs)]
    held = [*ins, *[o for o, _ in outs]]

    def kernel(*refs):
        groups = []
        for count in (*counts, len(ins), len(outs), len(outs), len(ins)):
            groups.append(refs[:count])
            refs = refs[count:]
        scalar_refs, near_refs, sources, _, targets, buffers, out_buffers, out_sems, sems = groups
        fetched = [Fetched(*f) for f in zip(sources, buffers, sems, pieces)]
        for i in range(max(pieces)):
            for f in fetched:
                f.start(i)
        stored = [Stored(*t) for t in zip(targets, out_buffers, out_sems)]
        body(scalar_refs, near_refs, fetched, stored, *refs)
        for out in stored:
            if not out.copies:
                out.send()
        for out in stored:
            for copy in out.copies:
                copy.wait()

    far = pl.BlockSpec(memory_space=pl.ANY)
    moved = sum(math.prod(a.shape) * jnp.dtype(a.dtype).itemsize for a in held)
    return pl.pallas_call(
        kernel,
        name=name,
        out_shape=[o for o, _ in outs],
        in_specs=[SMEM] * len(scalars) + [VMEM] * len(near) + [far] * (len(ins) + len(after)),
        out_specs=[far] * len(outs),
        scratch_shapes=[pltpu.VMEM(a.shape, a.dtype) for a in held]
        + [pltpu.SemaphoreType.DMA((pieces,)) for _, pieces in outs]
        + [pltpu.SemaphoreType.DMA((count,)) for count in pieces]
        + list(scratch),
        compiler_params=pltpu.CompilerParams(vmem_limit_bytes=VMEM_LIMIT),
        cost_estimate=COST,
    )(*scalars, *near, *ins, *after)


def gate(value, after):
    if not after:
        return value
    return pl.pallas_call(
        lambda *refs: None,
        name="gate",
        out_shape=shape(value.shape, value.dtype),
        in_specs=[pl.BlockSpec(memory_space=pl.ANY)] * (1 + len(after)),
        out_specs=pl.BlockSpec(memory_space=pl.ANY),
        input_output_aliases={0: 0},
    )(value, *after)


def row_scale(stream):
    return lax.rsqrt(jnp.mean(stream * stream, axis=-1, keepdims=True) + NORM_EPS)


def swap(value, axis, size, bit):
    return lax.ppermute(value, axis, [(i, i ^ bit) for i in range(size)])


def bits_down(size):
    return [1 << b for b in reversed(range(size.bit_length() - 1))]


def gather_relative(value, axis, size, hold=None):
    parts = {0: value}
    for bit in bits_down(size):
        moved = {0: swap(value, axis, size, bit)}
        if bit == 1 and hold:
            after = hold(parts[0], moved[0])
            parts.update({j: gate(v, after) for j, v in parts.items() if j})
        moved.update({j: swap(v, axis, size, bit) for j, v in parts.items() if j})
        parts.update({j | bit: v for j, v in moved.items()})
    return [parts[j] for j in range(size)]


def fold_body(scalars, near, ins, outs):
    rows = outs[0].ref.shape[0]
    step = min(rows, 128)
    for row in range(0, rows, step):
        at = slice(row, row + step)
        outs[0].ref[at, :] = sum(t.tile(row, step).astype(F32) for t in ins).astype(BF16)
        outs[0].send(at)


def fold(terms):
    pieces = max(1, terms[0].shape[0] // 128)
    outs = [(shape(terms[0].shape, BF16), pieces)]
    return far_call(fold_body, "fold", [], [], [(t, pieces) for t in terms], outs)[0]


def sum_relative(parts, axis, size, after=(), first_after=()):
    parts = dict(enumerate([[p] for p in parts]))
    bit, sent = 1, []
    while bit < size:
        kept = {}
        for j in sorted((j for j in parts if not j & bit), reverse=True):
            away = parts[j | bit]
            if len(away) > 1:
                away = gate(fold(away), after)
                sent.append(away)
            else:
                away = gate(away[0], first_after)
            kept[j] = parts[j] + [swap(away, axis, size, bit)]
        parts = kept
        bit *= 2
    return parts[0], sent


def exchange_relative(parts, axis, size):
    return [p if j == 0 else swap(p, axis, size, j) for j, p in enumerate(parts)]


def exchange_two(parts, size, after):
    width = parts[0].shape[1]
    far = gate(swap(jnp.concatenate(parts[2:], axis=1), "head", size, 2), after)
    near = swap(parts[1], "head", size, 1)
    return [parts[0], near, far[:, :width], swap(far[:, width:], "head", size, 1)]


def sum_everywhere(value, sizes):
    for axis, size in sizes:
        for bit in reversed(bits_down(size)):
            value = value + swap(value, axis, size, bit)
    return value


def column_orders(size):
    bits = bits_down(size)
    return [bits, bits[-1:] + bits[:-1]]


def ring_sources(dp, size):
    line = size // 2
    place = dp // 2 ^ dp // 4
    held = [jnp.remainder(place - k, line) for k in range(line)]
    held = [2 * (p ^ p // 2) for p in held]
    return jnp.stack([h + (dp & 1) for h in held] + [h + 1 - (dp & 1) for h in held])


def ring_step(value, size):
    line = size // 2
    ring = [p ^ p // 2 for p in range(line)]
    pairs = [(2 * ring[p] + i, 2 * ring[(p + 1) % line] + i) for p in range(line) for i in range(2)]
    return lax.ppermute(value, "dp", pairs)


def gather_columns(rows, size, holds=()):
    held, other = [rows], []
    for step in range(size // 2):
        after = holds[step](held, other) if step < len(holds) else other[-1:]
        held[step] = gate(held[step], after)
        other.append(swap(held[step], "dp", size, 1))
        if step + 1 < size // 2:
            held.append(ring_step(held[step], size))
    return held + other


def column_places(size, bits):
    places = [0]
    for bit in reversed(bits):
        places = places + [j | bit for j in places]
    return places


def scatter_step(kept, received, size, bit, hold):
    total = kept.astype(F32) + received.astype(F32)
    half = total.shape[0] // 2
    return total[:half], swap(gate(total[half:].astype(BF16), hold), "dp", size, bit)


def join_columns(from_ref, parts, outs):
    for i, part in enumerate(parts):
        part = part.ref
        lanes = part.shape[1]
        at = slice(None)
        if len(parts) > 1:
            at = pl.ds(pl.multiple_of(from_ref[i] * lanes, 128), lanes)
        for row, rows, out in outs:
            out[:, at] = part[row : row + rows, :]


def project_body(n, tile, scalars, near, ins, outs):
    me_ref, from_ref = scalars
    gain_ref, cos_ref, sin_ref = near
    count = len(ins) - 2 * n
    parts, xs, fvs = ins[:count], ins[count : count + n], ins[count + n :]
    q_out, k_out, kt_out, v_out, vt_out, w_out, wo_out = outs
    width = q_out.ref.shape[0]
    shard = xs[0].buffer.shape[0]
    w_ref = w_out.ref
    join_columns(from_ref, parts, [(0, 3 * width, w_ref), (3 * width, width, wo_out.ref)])
    w_out.send()
    wo_out.send()
    for j in range(n):
        x_ref, fv_ref = xs[j].ref, fvs[j].ref
        base = pl.multiple_of((me_ref[0] ^ j) * shard, shard)
        for t in range(0, shard, tile):
            at = pl.ds(pl.multiple_of(base + t, tile), tile)
            stream = x_ref[t : t + tile, :].astype(F32)
            normed = (stream * row_scale(stream) * gain_ref[...]).astype(BF16)
            qk = dot_nt(w_ref[: 2 * width, :], normed)
            cos, sin = cos_ref[:, at], sin_ref[:, at]
            turned = []
            for row in range(0, 2 * width, HEAD_DIM):
                first, second = qk[row : row + HALF], qk[row + HALF : row + HEAD_DIM]
                turned += [first * cos - second * sin, second * cos + first * sin]
            turned = jnp.concatenate(turned, axis=0)
            q_out.ref[:, at] = (turned[:width] * HEAD_DIM ** (-0.5)).astype(BF16)
            keys = turned[width:]
            kt_out.ref[:, at] = keys.astype(BF16)
            k_out.ref[at, :] = keys.T.astype(BF16)
            first_values = fv_ref[t : t + tile, :].astype(F32)
            values = 0.5 * dot_nt(normed, w_ref[2 * width :, :]) + 0.5 * first_values
            v_out.ref[at, :] = values.astype(BF16)
            vt_out.ref[:, at] = values.T.astype(BF16)
        at = pl.ds(base, shard)
        for out in (q_out, kt_out, vt_out):
            out.send(slice(None), at)
        for out in (k_out, v_out):
            out.send(at, slice(None))


def doc_of(len_ref, token):
    run, first, last = jnp.int32(0), jnp.int32(0), jnp.int32(SEQ)
    for doc in range(NDOC):
        end = run + len_ref[0, doc]
        inside = (token >= run) & (token < end)
        first, last = jnp.where(inside, run, first), jnp.where(inside, end, last)
        run = end
    return first, last


def attend_kernel(bq, per, heads, skip, len_ref, me_ref, q_ref, k_ref, vt_ref, start_ref, *refs):
    *ctx_refs, ot_ref, lse_ref, s_ref = refs[skip:]
    bk = bq
    block = pl.program_id(0)
    first, _ = doc_of(len_ref, block * bq)
    starts = start_ref[...]

    def score(kb, tops, diagonal):
        at = pl.ds(pl.multiple_of(kb * bk, bk), bk)
        key_index = lax.broadcasted_iota(jnp.int32, (bk, bq), 0) + kb * bk
        allowed = key_index >= starts
        if diagonal:
            allowed &= key_index <= lax.broadcasted_iota(jnp.int32, (bk, bq), 1) + block * bq
        out = []
        for h in range(heads):
            rows = slice(h * HEAD_DIM, (h + 1) * HEAD_DIM)
            scores = jnp.where(allowed, dot(k_ref[at, rows], q_ref[rows, :]), NEG)
            s_ref[h, at, :] = scores
            out.append(jnp.maximum(tops[h], jnp.max(scores.reshape(bk // 8, 8, bq), axis=0)))
        return tuple(out)

    tops = score(block, tuple(jnp.full((8, bq), NEG, F32) for _ in range(heads)), True)
    tops = lax.fori_loop(first // bk, block, lambda kb, c: score(kb, c, False), tops)
    tops = [jnp.max(t, axis=0, keepdims=True) for t in tops]

    def gather(kb, carry):
        at = pl.ds(pl.multiple_of(kb * bk, bk), bk)
        out = []
        for h in range(heads):
            rows = slice(h * HEAD_DIM, (h + 1) * HEAD_DIM)
            total, acc = carry[h]
            probs = jnp.exp(s_ref[h, at, :] - tops[h])
            total = total + jnp.sum(probs.reshape(bk // 8, 8, bq), axis=0)
            out.append((total, acc + dot(vt_ref[rows, at], probs.astype(BF16))))
        return tuple(out)

    zero = tuple((jnp.zeros((8, bq), F32), jnp.zeros((HEAD_DIM, bq), F32)) for _ in range(heads))
    sums = lax.fori_loop(first // bk, block + 1, gather, zero)
    outs = []
    for h in range(heads):
        total = jnp.sum(sums[h][0], axis=0, keepdims=True)
        outs.append(sums[h][1] * (1.0 / total))
        lse_ref[h : h + 1, :] = tops[h] + jnp.log(total)
    out = jnp.concatenate(outs, axis=0)
    ot_ref[...] = out.astype(BF16)
    out = out.T.astype(BF16)
    for j, ref in enumerate(ctx_refs):

        @pl.when((block // per) ^ me_ref[0] == j)
        def _(ref=ref):
            ref[pl.ds(pl.multiple_of((block % per) * bq, bq), bq), :] = out


def attend(lengths, me, q_t, keys, v_t, starts, shard, after):
    width = q_t.shape[0]
    heads = width // HEAD_DIM
    bq = min(512, shard)
    per = shard // bq
    n = SEQ // shard
    spec = pltpu.PrefetchScalarGridSpec(
        num_scalar_prefetch=2,
        grid=(SEQ // bq,),
        in_specs=[
            pl.BlockSpec((width, bq), lambda i, l, h: (0, i)),
            pl.BlockSpec((SEQ, width), lambda i, l, h: (0, 0)),
            pl.BlockSpec((width, SEQ), lambda i, l, h: (0, 0)),
            pl.BlockSpec((1, bq), lambda i, l, h: (0, i)),
        ]
        + [pl.BlockSpec(memory_space=pl.ANY)] * len(after),
        out_specs=[
            *[pl.BlockSpec((shard, width), lambda i, l, h: (0, 0))] * n,
            pl.BlockSpec((width, bq), lambda i, l, h: (0, i)),
            pl.BlockSpec((heads, bq), lambda i, l, h: (0, i)),
        ],
        scratch_shapes=[pltpu.VMEM((heads, SEQ, bq), F32)],
    )
    return pl.pallas_call(
        functools.partial(attend_kernel, bq, per, heads, len(after)),
        name="attend",
        grid_spec=spec,
        out_shape=[
            *[shape((shard, width), BF16)] * n,
            shape((width, SEQ), BF16),
            shape((heads, SEQ), F32),
        ],
        compiler_params=pltpu.CompilerParams(vmem_limit_bytes=VMEM_LIMIT),
        cost_estimate=COST,
    )(lengths, me, q_t, keys, v_t, starts, *after)


def attend_back_body(n, block, scalars, near, ins, outs, *scratch):
    len_ref, me_ref = scalars
    lse_ref, start_ref, cos_ref, sin_ref = near
    dos, (ot_in, *rest) = ins[:n], ins[n:]
    gp_out, *firsts = outs
    out_ref = gp_out.ref
    dq_ref, dk_ref, dv_ref, do_ref, delta_ref = scratch
    width = dq_ref.shape[0]
    heads = width // HEAD_DIM
    shard = SEQ // n
    ot_ref = ot_in.ref
    for j in range(n):
        at = pl.ds(pl.multiple_of((me_ref[0] ^ j) * shard, shard), shard)
        grad = dos[j].ref[...]
        do_ref[:, at] = grad
        product = grad.astype(F32) * ot_ref[:, at].astype(F32)
        for h in range(heads):
            delta_ref[h : h + 1, at] = jnp.sum(
                product[h * HEAD_DIM : (h + 1) * HEAD_DIM], axis=0, keepdims=True
            )
    dq_ref[...] = jnp.zeros_like(dq_ref)
    dk_ref[...] = jnp.zeros_like(dk_ref)
    dv_ref[...] = jnp.zeros_like(dv_ref)
    q_ref, k_ref, kt_ref, v_ref = (r.ref for r in rest)

    def pair(kb, qb, diagonal):
        k_at = pl.ds(pl.multiple_of(kb * block, block), block)
        q_at = pl.ds(pl.multiple_of(qb * block, block), block)
        key_index = lax.broadcasted_iota(jnp.int32, (block, block), 0) + kb * block
        allowed = key_index >= start_ref[:, q_at]
        if diagonal:
            allowed &= key_index <= lax.broadcasted_iota(jnp.int32, (block, block), 1) + qb * block
        every = range(heads)
        rows = [slice(h * HEAD_DIM, (h + 1) * HEAD_DIM) for h in every]
        q_t = [q_ref[r, q_at] for r in rows]
        do_t = [do_ref[r, q_at] for r in rows]
        scores = [dot(k_ref[k_at, r], q_t[h]) for h, r in enumerate(rows)]
        dprobs = [dot(v_ref[k_at, r], do_t[h]) for h, r in enumerate(rows)]
        probs = [
            jnp.exp(jnp.where(allowed, scores[h], NEG) - lse_ref[h : h + 1, q_at]) for h in every
        ]
        dscores = [
            (probs[h] * (dprobs[h] - delta_ref[h : h + 1, q_at])).astype(BF16) for h in every
        ]
        probs = [p.astype(BF16) for p in probs]
        dv = [dot_nt(do_t[h], probs[h]) for h in every]
        dk = [dot_nt(q_t[h], dscores[h]) for h in every]
        dq = [dot(kt_ref[rows[h], k_at], dscores[h]) for h in every]
        for h in every:
            dv_ref[rows[h], k_at] += dv[h]
            dk_ref[rows[h], k_at] += dk[h]
            dq_ref[rows[h], q_at] += dq[h]

    def outer(kb, carry):
        _, end = doc_of(len_ref, kb * block + block - 1)
        pair(kb, kb, True)

        def inner(qb, c):
            pair(kb, qb, False)
            return c

        lax.fori_loop(kb + 1, (end - 1) // block + 1, inner, 0)
        return carry

    lax.fori_loop(0, SEQ // block, outer, 0)
    for j in range(n):
        at = pl.ds(pl.multiple_of((me_ref[0] ^ j) * shard, shard), shard)
        grad = 0.5 * dv_ref[:, at]
        out_ref[2 * width :, at] = grad.astype(BF16)
        firsts[j].ref[...] = grad.T.astype(BF16)
        firsts[j].send()
    gp_out.send(slice(2 * width, 3 * width))
    cos, sin = cos_ref[...], sin_ref[...]
    for base, ref, scale in ((0, dq_ref, HEAD_DIM ** (-0.5)), (width, dk_ref, 1.0)):
        for row in range(0, width, HEAD_DIM):
            first = ref[row : row + HALF, :] * scale
            second = ref[row + HALF : row + HEAD_DIM, :] * scale
            out_ref[base + row : base + row + HALF, :] = (first * cos + second * sin).astype(BF16)
            out_ref[base + row + HALF : base + row + HEAD_DIM, :] = (
                second * cos - first * sin
            ).astype(BF16)
        gp_out.send(slice(base, base + width))


def join_body(n, tile, scalars, near, ins, outs):
    (gain_ref,) = near
    ctx, x_in, w_out = ins[:n], ins[n], ins[n + 1 :]
    mid, normed = outs
    for row in range(0, x_in.buffer.shape[0], tile):
        at = slice(row, row + tile)
        total = x_in.tile(row, tile).astype(F32)
        for c, w in zip(ctx, w_out):
            total = total + dot(c.tile(row, tile), w.ref[...])
        normed.ref[at, :] = (total * row_scale(total) * gain_ref[...]).astype(BF16)
        normed.send(at)
        mid.ref[at, :] = total
        mid.send(at)


def mlp_body(n, tile, scalars, near, ins, outs):
    (from_ref,) = scalars
    count = len(ins) - 2 * n
    parts, normed, grads = ins[:count], ins[count : count + n], ins[count + n :]
    mixed, dgate_out, dup_out, *gns = outs
    hidden = mixed.ref.shape[1]
    shard = normed[0].buffer.shape[0]
    if count > 1:
        *gns, made = gns
        w_ref = made.ref
        join_columns(from_ref, parts, [(0, 3 * hidden, w_ref)])
        made.send()
    else:
        w_ref = parts[0].ref
    w_gate, w_up, w_down = (w_ref.at[i * hidden : (i + 1) * hidden, :] for i in range(3))
    for j in reversed(range(n)):
        tokens_ref, og_ref = normed[j].ref, grads[j].ref

        def step(t, carry, tokens_ref=tokens_ref, og_ref=og_ref, j=j):
            rows = pl.ds(pl.multiple_of(t * tile, tile), tile)
            at = pl.ds(pl.multiple_of(j * shard + t * tile, tile), tile)
            tokens = tokens_ref[rows, :]
            gate = dot_nt(tokens, w_gate[...])
            up = dot_nt(tokens, w_up[...])
            gm = dot_nt(og_ref[rows, :], w_down[...])
            sig = 1.0 / (1.0 + jnp.exp(-gate))
            act = gate * sig
            mixed.ref[at, :] = (act * up).astype(BF16)
            dup = (gm * act).astype(BF16)
            dgate = (gm * up * sig * (1.0 + gate * (1.0 - sig))).astype(BF16)
            dup_out.ref[at, :] = dup
            dgate_out.ref[at, :] = dgate
            gns[j].ref[rows, :] = (dot(dgate, w_gate[...]) + dot(dup, w_up[...])).astype(BF16)
            return carry

        lax.fori_loop(0, shard // tile, step, 0)
        gns[j].send()
        for out in (mixed, dgate_out, dup_out):
            out.send(slice(j * shard, (j + 1) * shard))


def mlp_rest_body(n, tile, scalars, near, ins, outs, acc_ref):
    w_in, mixeds, ogs = ins[0], ins[1:3], ins[3 : 3 + n]
    dgates, normed, dups = ins[3 + n : 5 + n], ins[5 + n : 5 + 2 * n], ins[5 + 2 * n :]
    *parts, grads = outs
    half = n // 2
    hidden = acc_ref.shape[0]
    lanes = grads.ref.shape[2]
    shard = normed[0].buffer.shape[0]
    w_down = w_in.ref.at[2 * hidden :, :]
    for j in reversed(range(n)):
        mixed_ref = mixeds[j // half].ref
        for t in range(0, shard, tile):
            rows = mixed_ref[j % half * shard + t : j % half * shard + t + tile, :]
            parts[j].ref[t : t + tile, :] = dot(rows, w_down[...]).astype(BF16)
        parts[j].send()
    for which, (lefts, rights) in ((2, (mixeds, ogs)), (0, (dgates, normed)), (1, (dups, normed))):
        for j in range(n):
            left = lefts[j // half].ref[j % half * shard : (j % half + 1) * shard, :]
            part = dot_tn(left, rights[j].ref[...])
            if j == 0:
                acc_ref[...] = part
            else:
                acc_ref[...] += part
        at = slice(which * hidden, (which + 1) * hidden)
        for i in range(grads.ref.shape[0]):
            grads.ref[i, at, :] = acc_ref[:, i * lanes : (i + 1) * lanes].astype(BF16)
        grads.send(slice(None), at)


def middle_back_body(n, tile, scalars, near, ins, outs):
    (gain_ref,) = near
    mid_in, og_in, *terms = ins[:-n]
    w_out = ins[-n:]
    gmid_out, ga_out, gain_out, *gctx = outs
    for row in range(0, mid_in.buffer.shape[0], tile):
        at = slice(row, row + tile)
        mid = mid_in.tile(row, tile)
        grad = sum(t.tile(row, tile).astype(F32) for t in terms)
        scale = row_scale(mid)
        normed = mid * scale
        scaled = grad * gain_ref[...]
        back = scale * (scaled - normed * jnp.mean(scaled * normed, axis=-1, keepdims=True))
        total = jnp.sum(grad * normed, axis=0, keepdims=True)
        gain_out.ref[...] = total if row == 0 else gain_out.ref[...] + total
        gmid = og_in.tile(row, tile).astype(F32) + back
        ga = gmid.astype(BF16)
        for w, out in reversed(list(zip(w_out, gctx))):
            out.ref[:, at] = dot_nt(w.ref[...], ga).astype(BF16)
            out.send(slice(None), at)
        ga_out.ref[at, :] = ga
        ga_out.send(at)
        gmid_out.ref[at, :] = gmid
        gmid_out.send(at)


def out_weight_body(n, scalars, near, ins, outs):
    *ctx, ga = ins
    for c, out in reversed(list(zip(ctx, outs))):
        out.ref[...] = dot_tn(c.ref[...], ga.ref[...]).astype(BF16)
        out.send()


def unproject_body(n, tile, scalars, near, ins, outs):
    (me_ref,) = scalars
    w_in, gp_in, *xs = ins
    *gns, gain_out = outs
    shard = xs[0].buffer.shape[0]
    gp_ref, w_ref = gp_in.ref, w_in.ref
    total = 0.0
    for j in reversed(range(n)):
        base = (me_ref[0] ^ j) * shard
        for t in range(0, shard, tile):
            at = pl.ds(pl.multiple_of(base + t, tile), tile)
            grad = dot_tn(gp_ref[:, at], w_ref[...])
            gns[j].ref[t : t + tile, :] = grad.astype(BF16)
            stream = xs[j].ref[t : t + tile, :].astype(F32)
            total = total + jnp.sum(grad * (stream * row_scale(stream)), axis=0, keepdims=True)
        gns[j].send()
    gain_out.ref[...] = total


def qkv_weight_body(n, orders, scalars, near, ins, outs, acc_ref):
    me_ref, dp_ref = scalars
    (gain_ref,) = near
    gp_in, xs, terms = ins[0], ins[1 : 1 + n], ins[1 + n :]
    shard = xs[0].buffer.shape[0]
    lanes = outs[0].ref.shape[2]
    gp_ref = gp_in.ref
    wide = gp_ref.shape[0]
    for j in range(n):
        at = pl.ds(pl.multiple_of((me_ref[0] ^ j) * shard, shard), shard)
        stream = xs[j].ref[...].astype(F32)
        normed = (stream * row_scale(stream) * gain_ref[...]).astype(BF16)
        part = dot(gp_ref[:, at], normed)
        if j == 0:
            acc_ref[:wide, :] = part
        else:
            acc_ref[:wide, :] += part
    acc_ref[wide:, :] = sum(t.ref[...].astype(F32) for t in terms)
    if orders is None:
        for i in range(outs[0].ref.shape[0]):
            outs[0].ref[i] = acc_ref[:, i * lanes : (i + 1) * lanes].astype(BF16)
        return
    rows = acc_ref.shape[0] // 2
    for half, places in enumerate(orders):
        for i, j in reversed(list(enumerate(places))):
            at = pl.ds(pl.multiple_of((dp_ref[0] ^ j) * lanes, 128), lanes)
            out = outs[2 * half + i // (len(places) // 2)]
            out.ref[i % (len(places) // 2)] = acc_ref[half * rows : (half + 1) * rows, at].astype(BF16)
            if i % (len(places) // 2) == 0:
                out.send()


def layer_out_body(tile, scalars, near, ins, outs):
    for row in range(0, ins[0].buffer.shape[0], tile):
        at = slice(row, row + tile)
        outs[0].ref[at, :] = sum(t.tile(row, tile).astype(F32) for t in ins).astype(BF16)
        outs[0].send(at)


def input_back_body(n, tile, scalars, near, ins, outs):
    (me_ref,) = scalars
    (gain_ref,) = near
    x_in, gmid_in, *rest = ins
    terms, dvs = rest[:3], rest[3:]
    if n != 4:
        terms, dvs = rest, []
    for row in range(0, x_in.buffer.shape[0], tile):
        at = slice(row, row + tile)
        stream = x_in.tile(row, tile).astype(F32)
        scale = row_scale(stream)
        normed = stream * scale
        scaled = sum(t.tile(row, tile).astype(F32) for t in terms) * gain_ref[...]
        back = scale * (scaled - normed * jnp.mean(scaled * normed, axis=-1, keepdims=True))
        outs[0].ref[at, :] = gmid_in.tile(row, tile) + back
        outs[0].send(at)
    for j, dv in enumerate(dvs):
        width = dv.buffer.shape[1]
        at = pl.ds(pl.multiple_of((me_ref[0] ^ j) * width, 128), width)
        outs[1].ref[:, at] = dv.ref[...].astype(F32)


def doc_tables(lengths):
    index = jnp.arange(SEQ, dtype=jnp.int32)
    ends = jnp.cumsum(lengths)
    begins = ends - lengths
    starts = jnp.max(jnp.where(begins[:, None] <= index[None, :], begins[:, None], 0), axis=0)
    inverse = jnp.exp(jnp.arange(HALF, dtype=F32) * (-2.0 * math.log(10000.0) / HEAD_DIM))
    angles = (index - starts).astype(F32)[None, :] * inverse[:, None]
    return starts[None, :], jnp.cos(angles), jnp.sin(angles)


def local(
    n,
    n_dp,
    hidden_in,
    first_values,
    doc_lengths,
    out_grad,
    qkv_weight,
    out_weight,
    gate_up_weight,
    down_weight,
    attn_gain,
    mlp_gain,
):
    shard, width = hidden_in.shape[1], qkv_weight.shape[2]
    hidden = down_weight.shape[0]
    lanes = qkv_weight.shape[0]
    dim = hidden_in.shape[2]
    tile = min(256, shard)
    me = lax.axis_index("head").reshape(1).astype(jnp.int32)
    dp = lax.axis_index("dp").reshape(1).astype(jnp.int32)
    x_own, og_own = hidden_in[0], out_grad[0]
    gain_one, gain_two = attn_gain[None, :], mlp_gain[None, :]

    per = shard // tile
    rows = jnp.concatenate(
        [qkv_weight.transpose(1, 2, 0).reshape(3 * width, lanes), out_weight], axis=0
    )
    mlp_rows = jnp.concatenate(
        [gate_up_weight.transpose(1, 2, 0).reshape(2 * hidden, lanes), down_weight], axis=0
    )
    fv_parts = [
        lax.dynamic_slice(first_values[0], (0, (me[0] ^ j) * width), (shard, width))
        for j in range(n)
    ]
    sources = ring_sources(dp[0], n_dp)
    line = n_dp // 2
    ringed = lanes % 128 == 0
    if ringed:
        parts = gather_columns(rows, n_dp)
        xs = gather_relative(x_own, "head", n, lambda *x: [parts[line - 1]])
        fvs = exchange_two(fv_parts, n, [parts[line - 1]])
    else:
        xs = gather_relative(x_own, "head", n)
        fvs = exchange_relative(fv_parts, "head", n)
        parts = [lax.all_gather(rows, "dp", axis=1, tiled=True)]

    starts, cos, sin = doc_tables(doc_lengths[0])

    done = {}

    def project(after=()):
        return far_call(
            functools.partial(project_body, n, tile),
            "project",
            [me, sources],
            [gain_one, cos, sin],
            [*parts, *xs, *fvs],
            [
                (shape((width, SEQ), BF16), n),
                (shape((SEQ, width), BF16), n),
                (shape((width, SEQ), BF16), n),
                (shape((SEQ, width), BF16), n),
                (shape((width, SEQ), BF16), n),
                (shape((3 * width, dim), BF16), 1),
                (shape((width, dim), BF16), 1),
            ],
            flops=6 * SEQ * dim * width,
            after=after,
        )

    def first_stage(held, other):
        done["project"] = project(held[1:2])
        return done["project"][:1]

    def second_stage(held, other):
        q_t, keys, _, _, v_t, *_ = done["project"]
        done["attend"] = attend(
            doc_lengths, me, q_t, keys, v_t, starts, shard, held[2:3] + other[:2]
        )
        return done["attend"][-1:]

    if ringed:
        begin = lambda held, other: [parts[line - 1]]
        stages = [begin] + [lambda held, other: []] * (line - 3) + [first_stage, second_stage]
        mlp_columns = gather_columns(mlp_rows, n_dp, stages)
    else:
        mlp_columns = [lax.all_gather(mlp_rows, "dp", axis=1, tiled=True)]
        done["project"] = project()
        second_stage([], [])
    q_t, keys, k_t, values, v_t, w_qkv, w_out = done["project"]
    *ctx, o_t, lse = done["attend"]

    ctxs = exchange_relative(ctx, "head", n)
    w_outs = gather_relative(w_out, "head", n, lambda *w: [o_t, *mlp_columns[-2:-1]])
    ogs = gather_relative(og_own, "head", n, lambda *g: [o_t])
    middle, normed_two = far_call(
        functools.partial(join_body, n, tile),
        "join",
        [],
        [gain_two],
        [*[(a, per) for a in (*ctxs, x_own)], *w_outs],
        [(shape((shard, dim), F32), per), (shape((shard, dim), BF16), per)],
        flops=2 * shard * dim * dim,
        after=ogs[1:] + (mlp_columns[-1:] if ringed else []),
    )

    half = n // 2
    groups = []

    def mlp(tokens, lo, weights):
        hiddens = [(shape((half * shard, hidden), BF16), half)] * 3
        made = [(shape((3 * hidden, dim), BF16), 1)] if len(weights) > 1 else []
        out = far_call(
            functools.partial(mlp_body, half, tile),
            "mlp",
            [sources],
            [],
            [*weights, *tokens, *ogs[lo : lo + half]],
            hiddens + [(shape((shard, dim), BF16), 1)] * half + made,
            flops=10 * half * shard * dim * hidden,
        )
        groups.append(out)
        return [out[3]]

    if n == 4:
        normed = gather_relative(normed_two, "head", n, lambda *tokens: mlp(tokens, 0, mlp_columns))
    else:
        normed = gather_relative(normed_two, "head", n)
        mlp(normed[:half], 0, mlp_columns)
    w_mlp = groups[0][-1] if ringed else mlp_columns[0]
    mlp(normed[half:], half, [w_mlp])
    gn_two, gn_sent = sum_relative([p for g in groups for p in g[3 : 3 + half]], "head", n)

    *mlp_parts, mlp_grads = far_call(
        functools.partial(mlp_rest_body, n, tile),
        "mlp_rest",
        [],
        [],
        [w_mlp, groups[0][0], groups[1][0], *ogs]
        + [groups[0][1], groups[1][1], *normed, groups[0][2], groups[1][2]],
        [(shape((shard, dim), BF16), 1)] * n + [(shape((n_dp, 3 * hidden, lanes), BF16), 3)],
        [pltpu.VMEM((hidden, dim), F32)],
        flops=8 * SEQ * dim * hidden,
        after=[*gn_sent, gn_two[1]],
    )
    mlp_grads = gate(mlp_grads, gn_two[-1:])
    mlp_grads = lax.psum_scatter(mlp_grads, "dp", scatter_dimension=0, tiled=False).astype(F32)

    grad_middle, ga, gain_two_part, *gctx = far_call(
        functools.partial(middle_back_body, n, tile),
        "middle_back",
        [],
        [gain_two],
        [*[(a, per) for a in (middle, og_own, *gn_two)], *w_outs],
        [
            (shape((shard, dim), F32), per),
            (shape((shard, dim), BF16), per),
            (shape((1, dim), F32), 1),
        ]
        + [(shape((width, shard), BF16), per)] * n,
        flops=2 * shard * dim * dim,
        after=mlp_parts[:1],
    )
    dos = exchange_relative(gctx, "head", n)
    layer_terms, _ = sum_relative(mlp_parts, "head", n, after=dos[2:])
    out_parts = far_call(
        functools.partial(out_weight_body, n),
        "out_weight",
        [],
        [],
        [*ctxs, ga],
        [(shape((width, dim), BF16), 1)] * n,
        flops=2 * shard * dim * dim,
        after=dos[1:2],
    )
    out_terms, out_sent = sum_relative(out_parts, "head", n, after=dos[2:])

    gp_t, *dv = far_call(
        functools.partial(attend_back_body, n, min(256, shard)),
        "attend_back",
        [doc_lengths, me],
        [lse, starts, cos, sin],
        [*dos, o_t, q_t, keys, k_t, values],
        [(shape((3 * width, SEQ), BF16), 3)] + [(shape((shard, width), BF16), 1)] * n,
        [pltpu.VMEM((width, SEQ), F32)] * 3
        + [pltpu.VMEM((width, SEQ), BF16), pltpu.VMEM((width // HEAD_DIM, SEQ), F32)],
        flops=20 * SEQ * SEQ * width,
        after=out_sent,
    )
    dvs = exchange_relative(dv, "head", n)

    *gn_parts, gain_one_part = far_call(
        functools.partial(unproject_body, n, tile),
        "unproject",
        [me],
        [],
        [w_qkv, gp_t, *xs],
        [(shape((shard, dim), BF16), 1)] * n + [(shape((1, dim), F32), 1)],
        flops=6 * SEQ * dim * width,
        after=[layer_terms[-1], out_terms[-1]],
    )
    gn_one, gn_sent = sum_relative(gn_parts, "head", n, first_after=dvs[1:])
    orders = None
    outs = [(shape((n_dp, 4 * width, lanes), BF16), 1)]
    if ringed:
        bit_orders = [bits[::-1] for bits in column_orders(n_dp)]
        orders = [column_places(n_dp, bits) for bits in bit_orders]
        outs = [(shape((n_dp // 2, 2 * width, lanes), BF16), 1)] * 4
    grads = far_call(
        functools.partial(qkv_weight_body, n, orders),
        "qkv_weight",
        [me, dp],
        [gain_one],
        [gp_t, *xs, *out_terms],
        outs,
        [pltpu.VMEM((4 * width, dim), F32)],
        flops=6 * SEQ * dim * width,
        after=gn_sent,
    )
    (layer_out,) = far_call(
        functools.partial(layer_out_body, tile),
        "layer_out",
        [],
        [],
        [(a, per) for a in (middle, *layer_terms)],
        [(shape((shard, dim), BF16), per)],
        after=grads[:1],
    )
    gains = gate(jnp.concatenate([gain_one_part, gain_two_part], axis=0), gn_one[-1:])
    gains = sum_everywhere(gains, [("dp", n_dp), ("head", n)])
    if ringed:
        held = [
            (grads[2 * i], swap(grads[2 * i + 1], "dp", n_dp, bits[0]))
            for i, bits in enumerate(bit_orders)
        ]
        for step in range(1, len(bit_orders[0])):
            hold = gn_one[-1:] if step == 1 else []
            held = [
                scatter_step(*h, n_dp, bits[step], hold) for h, bits in zip(held, bit_orders)
            ]
        grads = jnp.concatenate([(k + r.astype(F32))[0] for k, r in held], axis=0)
    else:
        grads = lax.psum_scatter(grads[0], "dp", scatter_dimension=0, tiled=False).astype(F32)

    back_outs = [(shape((shard, dim), F32), per)]
    if n == 4:
        back_outs.append((shape((shard, dim), F32), 1))
    input_grad, *first_grad = far_call(
        functools.partial(input_back_body, n, tile),
        "input_back",
        [me],
        [gain_one],
        [*[(a, per) for a in (x_own, grad_middle, *gn_one)], *(dvs if n == 4 else [])],
        back_outs,
        after=[layer_out],
    )
    if not first_grad:
        stacked = jnp.stack(dvs)
        placed = [
            lax.dynamic_index_in_dim(stacked, me[0] ^ i, keepdims=False) for i in range(n)
        ]
        first_grad = [jnp.concatenate(placed, axis=1).astype(F32)]
    return (
        layer_out[None],
        input_grad[None],
        first_grad[0][None],
        grads[: 3 * width].reshape(3, width, lanes).transpose(2, 0, 1),
        grads[3 * width :],
        mlp_grads[: 2 * hidden].reshape(2, hidden, lanes).transpose(2, 0, 1),
        mlp_grads[2 * hidden :],
        gains[0],
        gains[1],
    )


def solution(mesh):
    tokens = P("dp", "head", None)
    columns = P("dp", None, "head")
    rows = P("head", "dp")
    return jax.shard_map(
        functools.partial(local, mesh.shape["head"], mesh.shape["dp"]),
        mesh=mesh,
        in_specs=(tokens, tokens, P("dp", None), tokens, columns, rows, columns, rows, P(), P()),
        out_specs=(tokens, tokens, tokens, columns, rows, columns, rows, P(), P()),
        check_vma=False,
    )
```

```python
import functools
import math

import jax
import jax.numpy as jnp
from jax import lax
from jax.experimental import pallas as pl
from jax.experimental.pallas import tpu as pltpu
from jax.sharding import PartitionSpec as P

HEAD_DIM = 64
HALF = HEAD_DIM // 2
SEQ = 2048
NDOC = 16
NORM_EPS = 1e-06
NEG = -1e30
F32 = jnp.float32
BF16 = jnp.bfloat16
VMEM_LIMIT = 65280 << 10
SHORT, MIDDLE, MOST, LONG = (
    pl.CostEstimate(flops=f << 30, bytes_accessed=1, transcendentals=0) for f in (0, 3, 6, 12)
)
COSTS = {
    "project": MOST,
    **dict.fromkeys(("mlp", "mlp_rest", "middle_back"), LONG),
    **dict.fromkeys(("attend_back", "unproject", "qkv_weight"), LONG),
    **dict.fromkeys(("fold", "out_weight"), MIDDLE),
}

VMEM = pl.BlockSpec(memory_space=pltpu.VMEM)
SMEM = pl.BlockSpec(memory_space=pltpu.SMEM)


def shape(dims, dtype):
    return jax.ShapeDtypeStruct(dims, dtype)


def dot(a, b):
    return jnp.dot(a, b, preferred_element_type=F32)


def dot_nt(a, b):
    return lax.dot_general(a, b, (((1,), (1,)), ((), ())), preferred_element_type=F32)


def dot_tn(a, b):
    return lax.dot_general(a, b, (((0,), (0,)), ((), ())), preferred_element_type=F32)


class Fetched:
    def __init__(self, source, buffer, sems, pieces):
        self.buffer, self.waiting = buffer, {}
        self.rows = buffer.shape[0] // pieces
        for i in range(pieces):
            at = (pl.ds(i * self.rows, self.rows),) if pieces > 1 else ()
            src, dst = (source.at[at], buffer.at[at]) if at else (source, buffer)
            self.waiting[i] = pltpu.make_async_copy(src, dst, sems.at[i])

    def start(self, i):
        if i in self.waiting:
            self.waiting[i].start()

    def tile(self, first, rows):
        for i in list(self.waiting):
            if first < (i + 1) * self.rows and first + rows > i * self.rows:
                self.waiting.pop(i).wait()
        return self.buffer[first : first + rows, :]

    @property
    def ref(self):
        for i in list(self.waiting):
            self.waiting.pop(i).wait()
        return self.buffer


class Stored:
    def __init__(self, target, buffer, sems):
        self.target, self.ref, self.sems, self.copies = target, buffer, sems, []

    def send(self, *at):
        copy = pltpu.make_async_copy(
            self.ref.at[at], self.target.at[at], self.sems.at[len(self.copies)]
        )
        copy.start()
        self.copies.append(copy)


def far_call(body, name, scalars, near, ins, outs, scratch=(), flops=0, after=()):
    pieces = [i[1] if isinstance(i, tuple) else 1 for i in ins]
    spans = [i[2:] if isinstance(i, tuple) and len(i) > 2 else None for i in ins]
    ins = [i[0] if isinstance(i, tuple) else i for i in ins]
    held_in = [
        a if s is None else shape((s[1] - s[0], *a.shape[1:]), a.dtype) for a, s in zip(ins, spans)
    ]
    counts = [len(scalars), len(near), len(ins), len(after), len(outs)]
    held = [*held_in, *[o for o, _ in outs]]

    def kernel(*refs):
        groups = []
        for count in (*counts, len(ins), len(outs), len(outs), len(ins)):
            groups.append(refs[:count])
            refs = refs[count:]
        scalar_refs, near_refs, sources, _, targets, buffers, out_buffers, out_sems, sems = groups
        sources = [
            r if s is None else r.at[pl.ds(s[0], s[1] - s[0])] for r, s in zip(sources, spans)
        ]
        fetched = [Fetched(*f) for f in zip(sources, buffers, sems, pieces)]
        for i in range(max(pieces)):
            for f in fetched:
                f.start(i)
        stored = [Stored(*t) for t in zip(targets, out_buffers, out_sems)]
        body(scalar_refs, near_refs, fetched, stored, *refs)
        for out in stored:
            if not out.copies:
                out.send()
        for out in stored:
            for copy in out.copies:
                copy.wait()

    far = pl.BlockSpec(memory_space=pl.ANY)
    moved = sum(math.prod(a.shape) * jnp.dtype(a.dtype).itemsize for a in held)
    return pl.pallas_call(
        kernel,
        name=name,
        out_shape=[o for o, _ in outs],
        in_specs=[SMEM] * len(scalars) + [VMEM] * len(near) + [far] * (len(ins) + len(after)),
        out_specs=[far] * len(outs),
        scratch_shapes=[pltpu.VMEM(a.shape, a.dtype) for a in held]
        + [pltpu.SemaphoreType.DMA((pieces,)) for _, pieces in outs]
        + [pltpu.SemaphoreType.DMA((count,)) for count in pieces]
        + list(scratch),
        compiler_params=pltpu.CompilerParams(vmem_limit_bytes=VMEM_LIMIT),
        cost_estimate=COSTS.get(name, SHORT),
    )(*scalars, *near, *ins, *after)


def gate(value, after):
    if not after:
        return value
    return pl.pallas_call(
        lambda *refs: None,
        name="gate",
        out_shape=shape(value.shape, value.dtype),
        in_specs=[pl.BlockSpec(memory_space=pl.ANY)] * (1 + len(after)),
        out_specs=pl.BlockSpec(memory_space=pl.ANY),
        input_output_aliases={0: 0},
    )(value, *after)


def row_scale(stream):
    return lax.rsqrt(jnp.mean(stream * stream, axis=-1, keepdims=True) + NORM_EPS)


def swap(value, axis, size, bit):
    return lax.ppermute(value, axis, [(i, i ^ bit) for i in range(size)])


def bits_down(size):
    return [1 << b for b in reversed(range(size.bit_length() - 1))]


def gather_relative(value, axis, size, hold=None):
    parts = {0: value}
    for bit in bits_down(size):
        moved = {0: swap(value, axis, size, bit)}
        if bit == 1 and hold:
            after = hold(parts[0], moved[0])
            parts.update({j: gate(v, after) for j, v in parts.items() if j})
        moved.update({j: swap(v, axis, size, bit) for j, v in parts.items() if j})
        parts.update({j | bit: v for j, v in moved.items()})
    return [parts[j] for j in range(size)]


def fold_body(scalars, near, ins, outs):
    rows = outs[0].ref.shape[0]
    step = min(rows, 128)
    for row in range(0, rows, step):
        at = slice(row, row + step)
        outs[0].ref[at, :] = sum(t.tile(row, step).astype(F32) for t in ins).astype(BF16)
        outs[0].send(at)


def fold(terms, after=()):
    pieces = max(1, terms[0].shape[0] // 128)
    outs = [(shape(terms[0].shape, BF16), pieces)]
    return far_call(fold_body, "fold", [], [], [(t, pieces) for t in terms], outs, after=after)[0]


def sum_relative(parts, axis, size, after=(), first_after=(), fold_after=()):
    parts = dict(enumerate([[p] for p in parts]))
    bit, sent = 1, []
    while bit < size:
        kept = {}
        for j in sorted((j for j in parts if not j & bit), reverse=True):
            away = parts[j | bit]
            if len(away) > 1:
                away = gate(fold(away, fold_after), after)
                sent.append(away)
            else:
                away = gate(away[0], first_after)
            kept[j] = parts[j] + [swap(away, axis, size, bit)]
        parts = kept
        bit *= 2
    return parts[0], sent


def sum_near(parts, after=()):
    third = swap(gate(parts[3], after), "head", 4, 1)
    return [parts[0], swap(parts[1], "head", 4, 1)], [parts[2], third]


def sum_far(terms, away, after=(), fold_after=()):
    sent = gate(fold(away, fold_after), after)
    return [*terms, swap(sent, "head", 4, 2)], sent


def exchange_relative(parts, axis, size):
    return [p if j == 0 else swap(p, axis, size, j) for j, p in enumerate(parts)]


def exchange_pair(parts, axis):
    own, near, pair = parts
    pair = swap(pair, "head", 4, 2)
    second = lax.slice_in_dim(pair, pair.shape[axis] // 2, pair.shape[axis], axis=axis)
    return [own, swap(near, "head", 4, 1), pair, swap(second, "head", 4, 1)]


def sum_all(value, axis, size):
    return sum((swap(value, axis, size, j) for j in range(1, size)), value)


def column_orders(size):
    bits = bits_down(size)
    return [bits, bits[-1:] + bits[:-1]]


def ring_sources(dp, size):
    line = size // 2
    place = dp // 2 ^ dp // 4
    held = [jnp.remainder(place - k, line) for k in range(line)]
    held = [2 * (p ^ p // 2) for p in held]
    return jnp.stack([h + (dp & 1) for h in held] + [h + 1 - (dp & 1) for h in held])


def ring_step(value, size):
    line = size // 2
    ring = [p ^ p // 2 for p in range(line)]
    pairs = [(2 * ring[p] + i, 2 * ring[(p + 1) % line] + i) for p in range(line) for i in range(2)]
    return lax.ppermute(value, "dp", pairs)


def gather_columns(rows, size):
    held, other = [rows], []
    for step in range(size // 2):
        if step:
            held[step] = gate(held[step], other[-1:])
        other.append(swap(held[step], "dp", size, 1))
        if step + 1 < size // 2:
            held.append(ring_step(held[step], size))
    return held + other


def column_places(size, bits):
    places = [0]
    for bit in reversed(bits):
        places = places + [j | bit for j in places]
    return places


def join_columns(from_ref, parts, outs):
    for i, part in enumerate(parts):
        part = part.ref
        lanes = part.shape[1]
        at = slice(None)
        if len(parts) > 1:
            at = pl.ds(pl.multiple_of(from_ref[i] * lanes, 128), lanes)
        for row, rows, out in outs:
            out[:, at] = part[row : row + rows, :]


def project_body(n, tile, scalars, near, ins, outs):
    me_ref, from_ref = scalars
    gain_ref, cos_ref, sin_ref = near
    count = len(ins) - 2 * n
    parts, xs, fvs = ins[:count], ins[count : count + n], ins[count + n :]
    q_out, k_out, kt_out, v_out, vt_out, w_out, wo_out = outs
    width = q_out.ref.shape[0]
    shard = xs[0].buffer.shape[0]
    w_ref = w_out.ref
    join_columns(from_ref, parts, [(0, 3 * width, w_ref), (3 * width, width, wo_out.ref)])
    w_out.send()
    wo_out.send()
    for j in range(n):
        x_ref, fv_ref = xs[j].ref, fvs[j].ref
        base = pl.multiple_of((me_ref[0] ^ j) * shard, shard)
        for t in range(0, shard, tile):
            at = pl.ds(pl.multiple_of(base + t, tile), tile)
            stream = x_ref[t : t + tile, :].astype(F32)
            normed = (stream * row_scale(stream) * gain_ref[...]).astype(BF16)
            qk = dot_nt(w_ref[: 2 * width, :], normed)
            cos, sin = cos_ref[:, at], sin_ref[:, at]
            turned = []
            for row in range(0, 2 * width, HEAD_DIM):
                first, second = qk[row : row + HALF], qk[row + HALF : row + HEAD_DIM]
                turned += [first * cos - second * sin, second * cos + first * sin]
            turned = jnp.concatenate(turned, axis=0)
            q_out.ref[:, at] = (turned[:width] * HEAD_DIM ** (-0.5)).astype(BF16)
            keys = turned[width:]
            kt_out.ref[:, at] = keys.astype(BF16)
            k_out.ref[at, :] = keys.T.astype(BF16)
            first_values = fv_ref[t : t + tile, :width].astype(F32)
            values = 0.5 * dot_nt(normed, w_ref[2 * width :, :]) + 0.5 * first_values
            v_out.ref[at, :] = values.astype(BF16)
            vt_out.ref[:, at] = values.T.astype(BF16)
        at = pl.ds(base, shard)
        for out in (q_out, kt_out, vt_out):
            out.send(slice(None), at)
        for out in (k_out, v_out):
            out.send(at, slice(None))


def doc_of(len_ref, token):
    run, first, last = jnp.int32(0), jnp.int32(0), jnp.int32(SEQ)
    for doc in range(NDOC):
        end = run + len_ref[0, doc]
        inside = (token >= run) & (token < end)
        first, last = jnp.where(inside, run, first), jnp.where(inside, end, last)
        run = end
    return first, last


def attend_kernel(bq, per, heads, skip, len_ref, me_ref, q_ref, k_ref, vt_ref, start_ref, *refs):
    *ctx_refs, ot_ref, lse_ref, s_ref = refs[skip:]
    bk = bq
    block = pl.program_id(0)
    first, _ = doc_of(len_ref, block * bq)
    starts = start_ref[...]

    def score(kb, tops, diagonal):
        at = pl.ds(pl.multiple_of(kb * bk, bk), bk)
        key_index = lax.broadcasted_iota(jnp.int32, (bk, bq), 0) + kb * bk
        allowed = key_index >= starts
        if diagonal:
            allowed &= key_index <= lax.broadcasted_iota(jnp.int32, (bk, bq), 1) + block * bq
        out = []
        for h in range(heads):
            rows = slice(h * HEAD_DIM, (h + 1) * HEAD_DIM)
            scores = jnp.where(allowed, dot(k_ref[at, rows], q_ref[rows, :]), NEG)
            s_ref[h, at, :] = scores
            out.append(jnp.maximum(tops[h], jnp.max(scores.reshape(bk // 8, 8, bq), axis=0)))
        return tuple(out)

    tops = score(block, tuple(jnp.full((8, bq), NEG, F32) for _ in range(heads)), True)
    tops = lax.fori_loop(first // bk, block, lambda kb, c: score(kb, c, False), tops)
    tops = [jnp.max(t, axis=0, keepdims=True) for t in tops]

    def gather(kb, carry):
        at = pl.ds(pl.multiple_of(kb * bk, bk), bk)
        out = []
        for h in range(heads):
            rows = slice(h * HEAD_DIM, (h + 1) * HEAD_DIM)
            total, acc = carry[h]
            probs = jnp.exp(s_ref[h, at, :] - tops[h])
            total = total + jnp.sum(probs.reshape(bk // 8, 8, bq), axis=0)
            out.append((total, acc + dot(vt_ref[rows, at], probs.astype(BF16))))
        return tuple(out)

    zero = tuple((jnp.zeros((8, bq), F32), jnp.zeros((HEAD_DIM, bq), F32)) for _ in range(heads))
    sums = lax.fori_loop(first // bk, block + 1, gather, zero)
    outs = []
    for h in range(heads):
        total = jnp.sum(sums[h][0], axis=0, keepdims=True)
        outs.append(sums[h][1] * (1.0 / total))
        lse_ref[h : h + 1, :] = tops[h] + jnp.log(total)
    out = jnp.concatenate(outs, axis=0)
    ot_ref[...] = out.astype(BF16)
    out = out.T.astype(BF16)
    width = out.shape[1]
    paired = 3 * (len(ctx_refs) == 3)
    for j in range(paired + 1 if paired else len(ctx_refs)):
        ref = ctx_refs[min(j, 2)] if paired else ctx_refs[j]
        at = slice(width, 2 * width) if paired and j == 3 else slice(0, width)

        @pl.when((block // per) ^ me_ref[0] == j)
        def _(ref=ref, at=at):
            ref[pl.ds(pl.multiple_of((block % per) * bq, bq), bq), at] = out


def attend(lengths, me, q_t, keys, v_t, starts, shard, after):
    width = q_t.shape[0]
    heads = width // HEAD_DIM
    bq = min(512, shard)
    per = shard // bq
    n = SEQ // shard
    widths = [width, width, 2 * width] if n == 4 else [width] * n
    spec = pltpu.PrefetchScalarGridSpec(
        num_scalar_prefetch=2,
        grid=(SEQ // bq,),
        in_specs=[
            pl.BlockSpec((width, bq), lambda i, l, h: (0, i)),
            pl.BlockSpec((SEQ, width), lambda i, l, h: (0, 0)),
            pl.BlockSpec((width, SEQ), lambda i, l, h: (0, 0)),
            pl.BlockSpec((1, bq), lambda i, l, h: (0, i)),
        ]
        + [pl.BlockSpec(memory_space=pl.ANY)] * len(after),
        out_specs=[
            *[pl.BlockSpec((shard, w), lambda i, l, h: (0, 0)) for w in widths],
            pl.BlockSpec((width, bq), lambda i, l, h: (0, i)),
            pl.BlockSpec((heads, bq), lambda i, l, h: (0, i)),
        ],
        scratch_shapes=[pltpu.VMEM((heads, SEQ, bq), F32)],
    )
    return pl.pallas_call(
        functools.partial(attend_kernel, bq, per, heads, len(after)),
        name="attend",
        grid_spec=spec,
        out_shape=[
            *[shape((shard, w), BF16) for w in widths],
            shape((width, SEQ), BF16),
            shape((heads, SEQ), F32),
        ],
        compiler_params=pltpu.CompilerParams(vmem_limit_bytes=VMEM_LIMIT),
        cost_estimate=MOST,
    )(lengths, me, q_t, keys, v_t, starts, *after)


def attend_back_body(n, block, scalars, near, ins, outs, *scratch):
    len_ref, me_ref = scalars
    lse_ref, start_ref, cos_ref, sin_ref = near
    dos, (ot_in, *rest) = ins[:n], ins[n:]
    gp_out, *firsts = outs
    out_ref = gp_out.ref
    dq_ref, dk_ref, dv_ref, do_ref, delta_ref = scratch
    width = dq_ref.shape[0]
    heads = width // HEAD_DIM
    shard = SEQ // n
    ot_ref = ot_in.ref
    for j in range(n):
        at = pl.ds(pl.multiple_of((me_ref[0] ^ j) * shard, shard), shard)
        grad = dos[j].ref[:width, :]
        do_ref[:, at] = grad
        product = grad.astype(F32) * ot_ref[:, at].astype(F32)
        for h in range(heads):
            delta_ref[h : h + 1, at] = jnp.sum(
                product[h * HEAD_DIM : (h + 1) * HEAD_DIM], axis=0, keepdims=True
            )
    dq_ref[...] = jnp.zeros_like(dq_ref)
    dk_ref[...] = jnp.zeros_like(dk_ref)
    dv_ref[...] = jnp.zeros_like(dv_ref)
    q_ref, k_ref, kt_ref, v_ref = (r.ref for r in rest)

    def pair(kb, qb, diagonal):
        k_at = pl.ds(pl.multiple_of(kb * block, block), block)
        q_at = pl.ds(pl.multiple_of(qb * block, block), block)
        key_index = lax.broadcasted_iota(jnp.int32, (block, block), 0) + kb * block
        allowed = key_index >= start_ref[:, q_at]
        if diagonal:
            allowed &= key_index <= lax.broadcasted_iota(jnp.int32, (block, block), 1) + qb * block
        every = range(heads)
        rows = [slice(h * HEAD_DIM, (h + 1) * HEAD_DIM) for h in every]
        q_t = [q_ref[r, q_at] for r in rows]
        do_t = [do_ref[r, q_at] for r in rows]
        scores = [dot(k_ref[k_at, r], q_t[h]) for h, r in enumerate(rows)]
        dprobs = [dot(v_ref[k_at, r], do_t[h]) for h, r in enumerate(rows)]
        probs = [
            jnp.exp(jnp.where(allowed, scores[h], NEG) - lse_ref[h : h + 1, q_at]) for h in every
        ]
        dscores = [
            (probs[h] * (dprobs[h] - delta_ref[h : h + 1, q_at])).astype(BF16) for h in every
        ]
        probs = [p.astype(BF16) for p in probs]
        dv = [dot_nt(do_t[h], probs[h]) for h in every]
        dk = [dot_nt(q_t[h], dscores[h]) for h in every]
        dq = [dot(kt_ref[rows[h], k_at], dscores[h]) for h in every]
        for h in every:
            dv_ref[rows[h], k_at] += dv[h]
            dk_ref[rows[h], k_at] += dk[h]
            dq_ref[rows[h], q_at] += dq[h]

    def outer(kb, carry):
        _, end = doc_of(len_ref, kb * block + block - 1)
        pair(kb, kb, True)

        def inner(qb, c):
            pair(kb, qb, False)
            return c

        lax.fori_loop(kb + 1, (end - 1) // block + 1, inner, 0)
        return carry

    lax.fori_loop(0, SEQ // block, outer, 0)
    for j in range(n):
        at = pl.ds(pl.multiple_of((me_ref[0] ^ j) * shard, shard), shard)
        grad = 0.5 * dv_ref[:, at]
        out_ref[2 * width :, at] = grad.astype(BF16)
        first = firsts[j] if len(firsts) == n else firsts[min(j, 2)]
        cols = slice(width, 2 * width) if len(firsts) != n and j == 3 else slice(0, width)
        first.ref[:, cols] = grad.T.astype(BF16)
    for first in firsts:
        first.send()
    gp_out.send(slice(2 * width, 3 * width))
    cos, sin = cos_ref[...], sin_ref[...]
    for base, ref, scale in ((0, dq_ref, HEAD_DIM ** (-0.5)), (width, dk_ref, 1.0)):
        for row in range(0, width, HEAD_DIM):
            first = ref[row : row + HALF, :] * scale
            second = ref[row + HALF : row + HEAD_DIM, :] * scale
            out_ref[base + row : base + row + HALF, :] = (first * cos + second * sin).astype(BF16)
            out_ref[base + row + HALF : base + row + HEAD_DIM, :] = (
                second * cos - first * sin
            ).astype(BF16)
        gp_out.send(slice(base, base + width))


def join_body(n, tile, scalars, near, ins, outs):
    (gain_ref,) = near
    ctx, x_in, w_out = ins[:n], ins[n], ins[n + 1 :]
    mid, *normeds = outs
    for row in range(0, x_in.buffer.shape[0], tile):
        at = slice(row, row + tile)
        total = x_in.tile(row, tile).astype(F32)
        for c, w in zip(ctx, w_out):
            total = total + dot(c.tile(row, tile)[:, : w.buffer.shape[0]], w.ref[...])
        rows = (total * row_scale(total) * gain_ref[...]).astype(BF16)
        for normed in normeds:
            normed.ref[at, :] = rows
            normed.send(at)
        mid.ref[at, :] = total
        mid.send(at)


def mlp_body(n, tile, scalars, near, ins, outs):
    (from_ref,) = scalars
    count = len(ins) - 2 * n
    parts, normed, grads = ins[:count], ins[count : count + n], ins[count + n :]
    mixed, dgate_out, dup_out, *gns = outs
    hidden = mixed.ref.shape[1]
    shard = normed[0].buffer.shape[0]
    if count > 1:
        *gns, made = gns
        w_ref = made.ref
        join_columns(from_ref, parts, [(0, 3 * hidden, w_ref)])
        made.send()
    else:
        w_ref = parts[0].ref
    w_gate, w_up, w_down = (w_ref.at[i * hidden : (i + 1) * hidden, :] for i in range(3))
    for j in reversed(range(n)):
        tokens_ref, og_ref = normed[j].ref, grads[j].ref

        def step(t, carry, tokens_ref=tokens_ref, og_ref=og_ref, j=j):
            rows = pl.ds(pl.multiple_of(t * tile, tile), tile)
            at = pl.ds(pl.multiple_of(j * shard + t * tile, tile), tile)
            tokens = tokens_ref[rows, :]
            gate = dot_nt(tokens, w_gate[...])
            up = dot_nt(tokens, w_up[...])
            gm = dot_nt(og_ref[rows, :], w_down[...])
            sig = 1.0 / (1.0 + jnp.exp(-gate))
            act = gate * sig
            mixed.ref[at, :] = (act * up).astype(BF16)
            dup = (gm * act).astype(BF16)
            dgate = (gm * up * sig * (1.0 + gate * (1.0 - sig))).astype(BF16)
            dup_out.ref[at, :] = dup
            dgate_out.ref[at, :] = dgate
            gns[j].ref[rows, :] = (dot(dgate, w_gate[...]) + dot(dup, w_up[...])).astype(BF16)
            return carry

        lax.fori_loop(0, shard // tile, step, 0)
        gns[j].send()
        for out in (mixed, dgate_out, dup_out):
            out.send(slice(j * shard, (j + 1) * shard))


def mlp_rest_body(n, tile, orders, scalars, near, ins, outs, acc_ref):
    w_in, mixeds, ogs = ins[0], ins[1:3], ins[3 : 3 + n]
    dgates, normed, dups = ins[3 + n : 5 + n], ins[5 + n : 5 + 2 * n], ins[5 + 2 * n :]
    parts, grads = outs[:n], outs[n:]
    half = n // 2
    hidden = acc_ref.shape[0]
    lanes = grads[0].ref.shape[2]
    shard = normed[0].buffer.shape[0]
    w_down = w_in.ref.at[2 * hidden :, :]
    for j in reversed(range(n)):
        mixed_ref = mixeds[j // half].ref
        for t in range(0, shard, tile):
            rows = mixed_ref[j % half * shard + t : j % half * shard + t + tile, :]
            parts[j].ref[t : t + tile, :] = dot(rows, w_down[...]).astype(BF16)
        parts[j].send()
    for which, (lefts, rights) in ((2, (mixeds, ogs)), (0, (dgates, normed)), (1, (dups, normed))):
        for j in range(n):
            left = lefts[j // half].ref[j % half * shard : (j % half + 1) * shard, :]
            part = dot_tn(left, rights[j].ref[...])
            if j == 0:
                acc_ref[...] = part
            else:
                acc_ref[...] += part
        cut_columns(scalars, orders, acc_ref, which * hidden, grads, lanes)


def cut_columns(scalars, orders, acc_ref, first, outs, lanes):
    count = acc_ref.shape[0]
    if orders is None:
        for i in range(outs[0].ref.shape[0]):
            outs[0].ref[i, first : first + count, :] = acc_ref[
                :, i * lanes : (i + 1) * lanes
            ].astype(BF16)
        return
    rows = outs[0].ref.shape[1]
    for half, places in enumerate(orders):
        low, high = max(first, half * rows), min(first + count, (half + 1) * rows)
        if low >= high:
            continue
        to = slice(low - half * rows, high - half * rows)
        for i, j in reversed(list(enumerate(places))):
            at = pl.ds(pl.multiple_of((scalars[-1][0] ^ j) * lanes, 128), lanes)
            out = outs[2 * half + i // (len(places) // 2)]
            out.ref[i % (len(places) // 2), to, :] = acc_ref[low - first : high - first, at].astype(
                BF16
            )


def middle_back_body(n, tile, scalars, near, ins, outs):
    (gain_ref,) = near
    mid_in, og_in, *terms = ins[:-n]
    w_out = ins[-n:]
    gmid_out, ga_out, gain_out, *gctx = outs
    for row in range(0, mid_in.buffer.shape[0], tile):
        at = slice(row, row + tile)
        mid = mid_in.tile(row, tile)
        grad = sum(t.tile(row, tile).astype(F32) for t in terms)
        scale = row_scale(mid)
        normed = mid * scale
        scaled = grad * gain_ref[...]
        back = scale * (scaled - normed * jnp.mean(scaled * normed, axis=-1, keepdims=True))
        total = jnp.sum(grad * normed, axis=0, keepdims=True)
        gain_out.ref[...] = total if row == 0 else gain_out.ref[...] + total
        gmid = og_in.tile(row, tile).astype(F32) + back
        ga = gmid.astype(BF16)
        for j, w in reversed(list(enumerate(w_out))):
            wide = w.buffer.shape[0]
            out, first = (gctx[j], 0) if len(gctx) == n else (gctx[min(j, 2)], wide * (j == 3))
            out.ref[first : first + wide, at] = dot_nt(w.ref[...], ga).astype(BF16)
            if first == 0:
                out.send(slice(None), at)
        ga_out.ref[at, :] = ga
        ga_out.send(at)
        gmid_out.ref[at, :] = gmid
        gmid_out.send(at)


def out_weight_body(n, scalars, near, ins, outs):
    *ctx, ga = ins
    for c, out in reversed(list(zip(ctx, outs))):
        out.ref[...] = dot_tn(c.ref[:, : out.ref.shape[0]], ga.ref[...]).astype(BF16)
        out.send()


def unproject_body(n, tile, scalars, near, ins, outs):
    (me_ref,) = scalars
    w_ref, gp_ref = (i.ref for i in ins)
    shard = outs[0].ref.shape[0]
    for j in reversed(range(n)):
        base = (me_ref[0] ^ j) * shard
        for t in range(0, shard, tile):
            at = pl.ds(pl.multiple_of(base + t, tile), tile)
            outs[j].ref[t : t + tile, :] = dot_tn(gp_ref[:, at], w_ref[...]).astype(BF16)
        outs[j].send()


def qkv_weight_body(n, orders, scalars, near, ins, outs, acc_ref):
    me_ref, dp_ref = scalars
    gain_ref, gain_two_ref = near
    gp_in, w_in, xs, terms = ins[0], ins[1], ins[2 : 2 + n], ins[2 + n :]
    *outs, gains = outs
    shard = xs[0].buffer.shape[0]
    lanes = outs[0].ref.shape[2]
    gp_ref = gp_in.ref
    wide = gp_ref.shape[0]
    for j in range(n):
        at = pl.ds(pl.multiple_of((me_ref[0] ^ j) * shard, shard), shard)
        stream = xs[j].ref[...].astype(F32)
        normed = (stream * row_scale(stream) * gain_ref[...]).astype(BF16)
        part = dot(gp_ref[:, at], normed)
        if j == 0:
            acc_ref[:wide, :] = part
        else:
            acc_ref[:wide, :] += part
    acc_ref[wide:, :] = sum(t.ref[...].astype(F32) for t in terms)
    cut_columns(scalars, orders, acc_ref, 0, outs, lanes)
    for out in outs:
        out.send()
    gain = 0.0
    for row in range(0, wide, 64):
        at = slice(row, row + 64)
        gain = gain + jnp.sum(acc_ref[at, :] * w_in.ref[at, :].astype(F32), axis=0, keepdims=True)
    gain = gain / gain_ref[...]
    both = [gain, gain_two_ref[...]]
    pieces = [g[:, c : c + 128] for g in both for c in range(0, gain.shape[1], 128)]
    gains.ref[...] = jnp.concatenate(pieces, axis=0)


def gain_rows(gains):
    high = gains.astype(BF16)
    return high, (gains - high.astype(F32)).astype(BF16)


def scatter_body(halves, scalars, near, ins, outs):
    first, second = ins[: halves[0]], ins[halves[0] : sum(halves)]
    gains_in = ins[sum(halves) :]
    rows = second[0].buffer.shape[1]
    count = second[0].buffer.shape[0]
    if gains_in:
        outs, gains_out = outs[:2], outs[2:]
        gains = gains_in[0].ref[...]
        last = first[-1].ref
        if last.shape[1] > rows:
            gains = gains + sum(
                last[i, row : row + 16, :].astype(F32)
                for i in range(last.shape[0])
                for row in range(rows, last.shape[1], 16)
            )
        each = gains.shape[0] // len(gains_out)
        for i, out in enumerate(gains_out):
            out.ref[...] = gains[i * each : (i + 1) * each]

    def total(terms, i, low, high):
        return sum(
            t.ref[i + t.buffer.shape[0] - count, low:high, :].astype(F32) for t in terms
        )

    if len(first) == 4:
        top, rest = outs
        cut = 2 * rows - rest.ref.shape[0]
        top_rows = [(first, 0, rows, 0), (second, 0, cut - rows, rows)]
        if len(top.ref.shape) == 3:
            wide = top.ref.shape[2]
            for terms, low, high, base in top_rows:
                for row in range(low, high, wide):
                    top.ref[(base + row) // wide] = total(terms, 0, row, row + wide).T
        else:
            for terms, low, high, base in top_rows:
                top.ref[base + low : base + high, :] = total(terms, 0, low, high)
        rest.ref[...] = total(second, 0, cut - rows, rows)
        return
    if gains_in:
        extra = outs[0].ref.shape[1] - rows
        for i, part in enumerate(gain_rows(gains)):
            row = rows if extra == 16 else rows + 16 * i
            outs[0].ref[i if extra == 16 else 0, row : row + 16, :] = part
    for terms, out in zip((first, second), outs):
        for i in range(count):
            out.ref[i, :rows, :] = total(terms, i, 0, rows).astype(BF16)
        out.send()


def scatter_start(parts, size, orders):
    return [
        [parts[2 * i], swap(parts[2 * i + 1], "dp", size, bits[0])] for i, bits in enumerate(orders)
    ]


def scatter_terms(held, first, last, gains):
    terms = []
    for half, parts in enumerate(held):
        for i, part in enumerate(parts):
            all_of_it = gains and half == 0 and i == len(parts) - 1 and i > 1
            terms.append((part, 1, 0 if all_of_it else first, last))
    return terms + gains


def scatter_kernel(held, gains, after=()):
    steps = len(held[0])
    rows, lanes = held[1][0].shape[1:]
    half = held[0][0].shape[0] >> (steps - 1)
    extra = 32 // half if gains else 0
    return far_call(
        functools.partial(scatter_body, [len(h) for h in held]),
        "scatter",
        [],
        [],
        scatter_terms(held, half, 2 * half, gains),
        [(shape((half, rows + extra, lanes), BF16), 1), (shape((half, rows, lanes), BF16), 1)]
        + [(shape(g.shape, F32), 1) for g in gains],
        after=after,
    )


def scatter_swap(held, sent, size, orders):
    return [
        [*parts, swap(out, "dp", size, bits[len(parts) - 1])]
        for parts, out, bits in zip(held, sent, orders)
    ]


def scatter_end(held, gains, cut, after=()):
    rows, lanes = held[1][0].shape[1:]
    return far_call(
        functools.partial(scatter_body, [len(h) for h in held]),
        "scatter",
        [],
        [],
        scatter_terms(held, 0, 1, gains),
        [(shape((3, lanes, cut // 3) if gains else (cut, lanes), F32), 1)]
        + [(shape((2 * rows - cut, lanes), F32), 1)]
        + [(shape((g.shape[0] // 2, *g.shape[1:]), F32), 1) for g in gains for _ in range(2)],
        after=after,
    )


def layer_out_body(tile, scalars, near, ins, outs):
    for row in range(0, ins[0].buffer.shape[0], tile):
        at = slice(row, row + tile)
        outs[0].ref[at, :] = sum(t.tile(row, tile).astype(F32) for t in ins).astype(BF16)
        outs[0].send(at)


def first_grad_body(scalars, near, ins, outs):
    width = outs[0].ref.shape[1] // len(ins)
    for j, dv in enumerate(ins):
        at = pl.ds(pl.multiple_of((scalars[0][0] ^ j) * width, 128), width)
        outs[0].ref[:, at] = dv.ref[:, :width].astype(F32)


def input_back_body(tile, scalars, near, ins, outs):
    (gain_ref,) = near
    x_in, gmid_in, *terms = ins
    for row in range(0, x_in.buffer.shape[0], tile):
        at = slice(row, row + tile)
        stream = x_in.tile(row, tile).astype(F32)
        scale = row_scale(stream)
        normed = stream * scale
        scaled = sum(t.tile(row, tile).astype(F32) for t in terms) * gain_ref[...]
        back = scale * (scaled - normed * jnp.mean(scaled * normed, axis=-1, keepdims=True))
        outs[0].ref[at, :] = gmid_in.tile(row, tile) + back
        outs[0].send(at)


def doc_tables(lengths):
    index = jnp.arange(SEQ, dtype=jnp.int32)
    ends = jnp.cumsum(lengths)
    begins = ends - lengths
    starts = jnp.max(jnp.where(begins[:, None] <= index[None, :], begins[:, None], 0), axis=0)
    inverse = jnp.exp(jnp.arange(HALF, dtype=F32) * (-2.0 * math.log(10000.0) / HEAD_DIM))
    angles = (index - starts).astype(F32)[None, :] * inverse[:, None]
    return starts[None, :], jnp.cos(angles), jnp.sin(angles)


def local(
    n,
    n_dp,
    hidden_in,
    first_values,
    doc_lengths,
    out_grad,
    qkv_weight,
    out_weight,
    gate_up_weight,
    down_weight,
    attn_gain,
    mlp_gain,
):
    shard, width = hidden_in.shape[1], qkv_weight.shape[2]
    hidden = down_weight.shape[0]
    lanes = qkv_weight.shape[0]
    dim = hidden_in.shape[2]
    tile = min(256, shard)
    me = lax.axis_index("head").reshape(1).astype(jnp.int32)
    dp = lax.axis_index("dp").reshape(1).astype(jnp.int32)
    x_own, og_own = hidden_in[0], out_grad[0]
    gain_one, gain_two = attn_gain[None, :], mlp_gain[None, :]

    per = shard // tile
    rows = jnp.concatenate(
        [qkv_weight.transpose(1, 2, 0).reshape(3 * width, lanes), out_weight], axis=0
    )
    mlp_rows = jnp.concatenate(
        [gate_up_weight.transpose(1, 2, 0).reshape(2 * hidden, lanes), down_weight], axis=0
    )
    fv_parts = [
        lax.dynamic_slice(first_values[0], (0, (me[0] ^ j) * width), (shard, width))
        for j in range(n)
    ]
    sources = ring_sources(dp[0], n_dp)
    line = n_dp // 2
    ringed = n == 4 and n_dp == 8 and lanes % 128 == 0
    if ringed:
        fv_near = swap(fv_parts[1], "head", n, 1)
        fv_far = swap(jnp.concatenate(fv_parts[2:], axis=1), "head", n, 2)
        parts = gather_columns(rows, n_dp)
        fv_far = gate(fv_far, [parts[line - 1]])
        xs = gather_relative(x_own, "head", n, lambda *x: [parts[line - 1]])
    else:
        parts = [lax.all_gather(rows, "dp", axis=1, tiled=True)]
        xs = gather_relative(x_own, "head", n)
        fvs = exchange_relative(fv_parts, "head", n)
        mlp_columns = [lax.all_gather(mlp_rows, "dp", axis=1, tiled=True)]
    starts, cos, sin = doc_tables(doc_lengths[0])

    def project(fvs, after=()):
        return far_call(
            functools.partial(project_body, n, tile),
            "project",
            [me, sources],
            [gain_one, cos, sin],
            [*parts, *xs, *fvs],
            [
                (shape((width, SEQ), BF16), n),
                (shape((SEQ, width), BF16), n),
                (shape((width, SEQ), BF16), n),
                (shape((SEQ, width), BF16), n),
                (shape((width, SEQ), BF16), n),
                (shape((3 * width, dim), BF16), 1),
                (shape((width, dim), BF16), 1),
            ],
            flops=6 * SEQ * dim * width,
            after=after,
        )

    if ringed:
        held = [gate(mlp_rows, [parts[line - 1], cos, sin, xs[1], fv_near, fv_far])]
        held.append(ring_step(held[0], n_dp))
        other = [swap(held[0], "dp", n_dp, 1)]
        og_near, og_far = swap(og_own, "head", n, 1), swap(og_own, "head", n, 2)
        fv_last = swap(fv_far[:, width:], "head", n, 1)
        projected = project([fv_parts[0], fv_near, fv_far, fv_last])
        w_near, far = swap(projected[-1], "head", n, 1), swap(projected[-1], "head", n, 2)
        held[1] = gate(held[1], [projected[0], other[0]])
        other.append(swap(held[1], "dp", n_dp, 1))
        held.append(ring_step(held[1], n_dp))
        early = [held[1]]
    else:
        projected, early = project(fvs), []
    q_t, keys, k_t, values, v_t, w_qkv, w_out = projected
    *ctx, o_t, lse = attend(doc_lengths, me, q_t, keys, v_t, starts, shard, early)
    if ringed:
        held[2] = gate(held[2], [o_t, other[1], far])
        other.append(swap(held[2], "dp", n_dp, 1))
        held.append(ring_step(held[2], n_dp))
        other.append(swap(held[3], "dp", n_dp, 1))
        far = gate(far, [o_t])
        w_outs = [w_out, w_near, far, swap(far, "head", n, 1)]
        mlp_columns = held + other
    else:
        w_outs = gather_relative(w_out, "head", n, lambda *w: [o_t])

    ctxs = exchange_pair(ctx, 1) if n == 4 else exchange_relative(ctx, "head", n)
    if not ringed:
        ogs = gather_relative(og_own, "head", n)
    middle, normed_two, normed_near = far_call(
        functools.partial(join_body, n, tile),
        "join",
        [],
        [gain_two],
        [*[(a, per) for a in (*ctxs, x_own)], *w_outs],
        [(shape((shard, dim), F32), per)] + [(shape((shard, dim), BF16), per)] * 2,
        flops=2 * shard * dim * dim,
        after=[og_far, held[3], other[2]] if ringed else ogs[1:],
    )

    if ringed:
        og_far = gate(og_far, [normed_near])
        ogs = [og_own, og_near, og_far, swap(og_far, "head", n, 1)]
    half = n // 2
    groups = []

    def mlp(tokens, lo, weights):
        hiddens = [(shape((half * shard, hidden), BF16), half)] * 3
        made = [(shape((3 * hidden, dim), BF16), 1)] if len(weights) > 1 else []
        out = far_call(
            functools.partial(mlp_body, half, tile),
            "mlp",
            [sources],
            [],
            [*weights, *tokens, *ogs[lo : lo + half]],
            hiddens + [(shape((shard, dim), BF16), 1)] * half + made,
            flops=10 * half * shard * dim * hidden,
        )
        groups.append(out)
        return [out[3]]

    if ringed:
        near = swap(gate(normed_near, other[3:]), "head", n, 1)
        pair = swap(normed_two, "head", n, 2)
        pair = gate(pair, mlp([normed_two, near], 0, mlp_columns))
        normed = [normed_two, near, pair, swap(pair, "head", n, 1)]
    else:
        normed = gather_relative(normed_two, "head", n)
        mlp(normed[:half], 0, mlp_columns)
    w_mlp = groups[0][-1] if ringed else mlp_columns[0]
    mlp(normed[half:], half, [w_mlp])
    gn_parts = [p for g in groups for p in g[3 : 3 + half]]
    if n == 4:
        gn_two, *gn_sent = sum_far(*sum_near(gn_parts))
    else:
        gn_two, gn_sent = sum_relative(gn_parts, "head", n)

    orders, grad_outs = None, lambda rows: [(shape((n_dp, rows, lanes), BF16), 3)]
    if ringed:
        bit_orders = [bits[::-1] for bits in column_orders(n_dp)]
        orders = [column_places(n_dp, bits) for bits in bit_orders]
        grad_outs = lambda rows: [(shape((n_dp // 2, rows // 2, lanes), BF16), 1)] * 4
    rest = far_call(
        functools.partial(mlp_rest_body, n, tile, orders),
        "mlp_rest",
        [dp],
        [],
        [w_mlp, groups[0][0], groups[1][0], *ogs]
        + [groups[0][1], groups[1][1], *normed, groups[0][2], groups[1][2]],
        [(shape((shard, dim), BF16), 1)] * n + grad_outs(3 * hidden),
        [pltpu.VMEM((hidden, dim), F32)],
        flops=8 * SEQ * dim * hidden,
        after=[*gn_sent, gn_two[1]],
    )
    mlp_parts, mlp_grads = rest[:n], rest[n:]
    layer_near = sum_near(mlp_parts) if n == 4 else ([mlp_parts[0]] * 2,) * 2
    if ringed:
        mlp_held = scatter_start(mlp_grads, n_dp, bit_orders)
    else:
        mlp_grads = lax.psum_scatter(mlp_grads[0], "dp", scatter_dimension=0, tiled=False)

    widths = [width, width, 2 * width] if n == 4 else [width] * n
    mlp_sent, third_sums = [], []
    grad_middle, ga, gain_two_part, *gctx = far_call(
        functools.partial(middle_back_body, n, tile),
        "middle_back",
        [],
        [gain_two],
        [*[(a, per) for a in (middle, og_own, *gn_two)], *w_outs],
        [
            (shape((shard, dim), F32), per),
            (shape((shard, dim), BF16), per),
            (shape((1, dim), F32), 1),
        ]
        + [(shape((w, shard), BF16), per) for w in widths],
        flops=2 * shard * dim * dim,
        after=mlp_parts[:1],
    )
    dos = exchange_pair(gctx, 0) if n == 4 else exchange_relative(gctx, "head", n)
    out_parts = far_call(
        functools.partial(out_weight_body, n),
        "out_weight",
        [],
        [],
        [*ctxs, ga],
        [(shape((width, dim), BF16), 1)] * n,
        flops=2 * shard * dim * dim,
        after=[t[1] for t in layer_near],
    )
    if n == 4:
        out_near = sum_near(out_parts, dos[2:3])
        layer_terms, layer_sent = sum_far(*layer_near, after=dos[2:3])
        out_terms, out_sent = sum_far(*out_near, after=dos[2:3])
        sums_sent = [layer_sent, out_sent, out_terms[1]]
    else:
        layer_terms, _ = sum_relative(mlp_parts, "head", n)
        out_terms, sums_sent = sum_relative(out_parts, "head", n)
    first_sums, second_sums = [], []
    if ringed:
        first_sums = scatter_kernel(mlp_held, [], after=out_parts[:1])
        mlp_held = scatter_swap(mlp_held, first_sums, n_dp, bit_orders)
        second_sums = [h[-1] for h in mlp_held]
    gp_t, *dv = far_call(
        functools.partial(attend_back_body, n, min(256, shard)),
        "attend_back",
        [doc_lengths, me],
        [lse, starts, cos, sin],
        [*dos, o_t, q_t, keys, k_t, values],
        [(shape((3 * width, SEQ), BF16), 3)] + [(shape((shard, w), BF16), 1) for w in widths],
        [pltpu.VMEM((width, SEQ), F32)] * 3
        + [pltpu.VMEM((width, SEQ), BF16), pltpu.VMEM((width // HEAD_DIM, SEQ), F32)],
        flops=20 * SEQ * SEQ * width,
        after=[*sums_sent, *first_sums],
    )
    dvs = exchange_pair(dv, 1) if n == 4 else exchange_relative(dv, "head", n)

    if ringed:
        mlp_sent = scatter_kernel(mlp_held, [], after=[gp_t])
        mlp_held = scatter_swap(mlp_held, mlp_sent, n_dp, bit_orders)
        third_sums = [h[-1] for h in mlp_held]
    *grads, gains = far_call(
        functools.partial(qkv_weight_body, n, orders),
        "qkv_weight",
        [me, dp],
        [gain_one, gain_two_part],
        [gp_t, w_qkv, *xs, *out_terms],
        grad_outs(4 * width) + [(shape((2 * dim // 128, 128), F32), 1)],
        [pltpu.VMEM((4 * width, dim), F32)],
        after=[*layer_terms[1:], *mlp_sent],
    )
    if n == 4:
        gains = gains + swap(gains, "head", n, 1)
        gains = gains + swap(gains, "head", n, 2)
    else:
        gains = sum_all(gains, "head", n)
    if ringed:
        held = scatter_start(grads, n_dp, bit_orders)
    gn_parts = far_call(
        functools.partial(unproject_body, n, tile),
        "unproject",
        [me],
        [],
        [w_qkv, gp_t],
        [(shape((shard, dim), BF16), 1)] * n,
        after=[*grads[:1], *third_sums, *dvs[1:3]],
    )
    (layer_out,) = far_call(
        functools.partial(layer_out_body, tile),
        "layer_out",
        [],
        [],
        [(a, per) for a in (middle, *layer_terms)],
        [(shape((shard, dim), BF16), per)],
        after=gn_parts[:1],
    )
    first_grad = None

    def first_grad_of(after):
        return far_call(
            first_grad_body, "first_grad", [me], [], dvs, [(shape((shard, dim), F32), 1)], after=after
        )[0]

    if ringed:
        sent = scatter_kernel(held, [])
        gn_near = sum_near(gn_parts, [gains, layer_out, *[h[-1] for h in held]])
        gn_one, gn_sent = sum_far(*gn_near, fold_after=sent)
        held = scatter_swap(held, sent, n_dp, bit_orders)
        gains = gate(gains, [gn_sent, gn_one[1]])
        gains = gains + swap(gains, "dp", n_dp, bit_orders[0][0])
        first_grad = first_grad_of([gains])
        mlp_gu, mlp_down = scatter_end(mlp_held, [], 2 * hidden, after=[gains])
        gains = gate(gains, [first_grad, mlp_down])
        gains = gains + swap(gains, "dp", n_dp, bit_orders[0][1])
        *sent, gains = scatter_kernel(held, [gains])
        held = scatter_swap(held, sent, n_dp, bit_orders)
    else:
        gn_one, _ = sum_relative(gn_parts, "head", n)
        gains = sum_all(gains, "dp", n_dp)
        grads = lax.psum_scatter(grads[0], "dp", scatter_dimension=0, tiled=False).astype(F32)
        qkv_grad, out_grad_w = grads[: 3 * width], grads[3 * width :]
        mlp_grads = mlp_grads.astype(F32)
        mlp_gu, mlp_down = mlp_grads[: 2 * hidden], mlp_grads[2 * hidden :]
    (input_grad,) = far_call(
        functools.partial(input_back_body, tile),
        "input_back",
        [],
        [gain_one],
        [(a, per) for a in (x_own, grad_middle, *gn_one)],
        [(shape((shard, dim), F32), per)],
    )
    if ringed:
        qkv_grad, out_grad_w, gain_one_grad, gain_two_grad = scatter_end(
            held, [gains], 3 * width, after=[input_grad]
        )
        qkv_grad = qkv_grad.transpose(1, 0, 2)
    else:
        qkv_grad = qkv_grad.reshape(3, width, lanes).transpose(2, 0, 1)
        gain_one_grad, gain_two_grad = gains.reshape(2, dim)
    if first_grad is None:
        stacked = jnp.stack(dvs)
        placed = [
            lax.dynamic_index_in_dim(stacked, me[0] ^ i, keepdims=False) for i in range(n)
        ]
        first_grad = jnp.concatenate(placed, axis=1).astype(F32)
    return (
        layer_out[None],
        input_grad[None],
        first_grad[None],
        qkv_grad,
        out_grad_w,
        mlp_gu.reshape(2, hidden, lanes).transpose(2, 0, 1),
        mlp_down,
        gain_one_grad.reshape(dim),
        gain_two_grad.reshape(dim),
    )


def solution(mesh):
    tokens = P("dp", "head", None)
    columns = P("dp", None, "head")
    rows = P("head", "dp")
    return jax.shard_map(
        functools.partial(local, mesh.shape["head"], mesh.shape["dp"]),
        mesh=mesh,
        in_specs=(tokens, tokens, P("dp", None), tokens, columns, rows, columns, rows, P(), P()),
        out_specs=(tokens, tokens, tokens, columns, rows, columns, rows, P(), P()),
        check_vma=False,
    )
```

```python
import functools
import math

import jax
import jax.numpy as jnp
from jax import lax
from jax.experimental import pallas as pl
from jax.experimental.pallas import tpu as pltpu
from jax.sharding import PartitionSpec as P

HEAD_DIM = 64
HALF = HEAD_DIM // 2
SEQ = 2048
NDOC = 16
NORM_EPS = 1e-06
NEG = -1e30
F32 = jnp.float32
BF16 = jnp.bfloat16
VMEM_LIMIT = 65280 << 10
SHORT, SMALL, MIDDLE, MOST, LONG = (
    pl.CostEstimate(flops=f << 30, bytes_accessed=1, transcendentals=0) for f in (0, 1, 3, 6, 12)
)
COSTS = {
    "project": MOST,
    **dict.fromkeys(("mlp", "mlp_rest", "middle_back"), LONG),
    **dict.fromkeys(("attend_back", "unproject", "qkv_weight"), LONG),
    **dict.fromkeys(("fold", "out_weight"), MIDDLE),
    **dict.fromkeys(("first_grad", "layer_out", "collect"), SMALL),
}

VMEM = pl.BlockSpec(memory_space=pltpu.VMEM)
SMEM = pl.BlockSpec(memory_space=pltpu.SMEM)


def shape(dims, dtype):
    return jax.ShapeDtypeStruct(dims, dtype)


def dot(a, b):
    return jnp.dot(a, b, preferred_element_type=F32)


def dot_nt(a, b):
    return lax.dot_general(a, b, (((1,), (1,)), ((), ())), preferred_element_type=F32)


def dot_tn(a, b):
    return lax.dot_general(a, b, (((0,), (0,)), ((), ())), preferred_element_type=F32)


class Fetched:
    def __init__(self, source, buffer, sems, pieces):
        self.buffer, self.waiting, self.begun = buffer, {}, set()
        self.rows = buffer.shape[0] // pieces
        for i in range(pieces):
            at = (pl.ds(i * self.rows, self.rows),) if pieces > 1 else ()
            src, dst = (source.at[at], buffer.at[at]) if at else (source, buffer)
            self.waiting[i] = pltpu.make_async_copy(src, dst, sems.at[i])

    def start(self, i):
        if i in self.waiting and i not in self.begun:
            self.begun.add(i)
            self.waiting[i].start()

    def begin(self):
        for i in list(self.waiting):
            self.start(i)

    def finish(self, i):
        self.start(i)
        self.waiting.pop(i).wait()

    def tile(self, first, rows):
        for i in list(self.waiting):
            if first < (i + 1) * self.rows and first + rows > i * self.rows:
                self.finish(i)
        return self.buffer[first : first + rows, :]

    @property
    def ref(self):
        for i in list(self.waiting):
            self.finish(i)
        return self.buffer


class Stored:
    def __init__(self, target, buffer, sems):
        self.target, self.ref, self.sems, self.copies = target, buffer, sems, []

    def send(self, *at):
        copy = pltpu.make_async_copy(
            self.ref.at[at], self.target.at[at], self.sems.at[len(self.copies)]
        )
        copy.start()
        self.copies.append(copy)


def far_call(body, name, scalars, near, ins, outs, scratch=(), flops=0, after=(), lazy=()):
    pieces = [i[1] if isinstance(i, tuple) else 1 for i in ins]
    spans = [i[2:] if isinstance(i, tuple) and len(i) > 2 else None for i in ins]
    ins = [i[0] if isinstance(i, tuple) else i for i in ins]
    held_in = [
        a if s is None else shape((s[1] - s[0], *a.shape[1:]), a.dtype) for a, s in zip(ins, spans)
    ]
    counts = [len(scalars), len(near), len(ins), len(after), len(outs)]
    held = [*held_in, *[o for o, _ in outs]]

    def kernel(*refs):
        groups = []
        for count in (*counts, len(ins), len(outs), len(outs), len(ins)):
            groups.append(refs[:count])
            refs = refs[count:]
        scalar_refs, near_refs, sources, _, targets, buffers, out_buffers, out_sems, sems = groups
        sources = [
            r if s is None else r.at[pl.ds(s[0], s[1] - s[0])] for r, s in zip(sources, spans)
        ]
        fetched = [Fetched(*f) for f in zip(sources, buffers, sems, pieces)]
        for i in range(max(pieces)):
            for k, f in enumerate(fetched):
                if k not in lazy:
                    f.start(i)
        stored = [Stored(*t) for t in zip(targets, out_buffers, out_sems)]
        body(scalar_refs, near_refs, fetched, stored, *refs)
        for out in stored:
            if not out.copies:
                out.send()
        for out in stored:
            for copy in out.copies:
                copy.wait()

    far = pl.BlockSpec(memory_space=pl.ANY)
    moved = sum(math.prod(a.shape) * jnp.dtype(a.dtype).itemsize for a in held)
    return pl.pallas_call(
        kernel,
        name=name,
        out_shape=[o for o, _ in outs],
        in_specs=[SMEM] * len(scalars) + [VMEM] * len(near) + [far] * (len(ins) + len(after)),
        out_specs=[far] * len(outs),
        scratch_shapes=[pltpu.VMEM(a.shape, a.dtype) for a in held]
        + [pltpu.SemaphoreType.DMA((pieces,)) for _, pieces in outs]
        + [pltpu.SemaphoreType.DMA((count,)) for count in pieces]
        + list(scratch),
        compiler_params=pltpu.CompilerParams(vmem_limit_bytes=VMEM_LIMIT),
        cost_estimate=COSTS.get(name, SHORT),
    )(*scalars, *near, *ins, *after)


def gate(value, after):
    if not after:
        return value
    return pl.pallas_call(
        lambda *refs: None,
        name="gate",
        out_shape=shape(value.shape, value.dtype),
        in_specs=[pl.BlockSpec(memory_space=pl.ANY)] * (1 + len(after)),
        out_specs=pl.BlockSpec(memory_space=pl.ANY),
        input_output_aliases={0: 0},
    )(value, *after)


def row_scale(stream):
    return lax.rsqrt(jnp.mean(stream * stream, axis=-1, keepdims=True) + NORM_EPS)


def swap(value, axis, size, bit):
    return lax.ppermute(value, axis, [(i, i ^ bit) for i in range(size)])


def bits_down(size):
    return [1 << b for b in reversed(range(size.bit_length() - 1))]


def gather_relative(value, axis, size, hold=None):
    parts = {0: value}
    for bit in bits_down(size):
        moved = {0: swap(value, axis, size, bit)}
        if bit == 1 and hold:
            after = hold(parts[0], moved[0])
            parts.update({j: gate(v, after) for j, v in parts.items() if j})
        moved.update({j: swap(v, axis, size, bit) for j, v in parts.items() if j})
        parts.update({j | bit: v for j, v in moved.items()})
    return [parts[j] for j in range(size)]


def fold_body(scalars, near, ins, outs):
    rows = outs[0].ref.shape[0]
    step = min(rows, 128)
    for row in range(0, rows, step):
        at = slice(row, row + step)
        outs[0].ref[at, :] = sum(t.tile(row, step).astype(F32) for t in ins).astype(BF16)
        outs[0].send(at)


def fold(terms, after=()):
    pieces = max(1, terms[0].shape[0] // 128)
    outs = [(shape(terms[0].shape, BF16), pieces)]
    return far_call(fold_body, "fold", [], [], [(t, pieces) for t in terms], outs, after=after)[0]


def sum_relative(parts, axis, size, after=(), first_after=(), fold_after=()):
    parts = dict(enumerate([[p] for p in parts]))
    bit, sent = 1, []
    while bit < size:
        kept = {}
        for j in sorted((j for j in parts if not j & bit), reverse=True):
            away = parts[j | bit]
            if len(away) > 1:
                away = gate(fold(away, fold_after), after)
                sent.append(away)
            else:
                away = gate(away[0], first_after)
            kept[j] = parts[j] + [swap(away, axis, size, bit)]
        parts = kept
        bit *= 2
    return parts[0], sent


def sum_near(parts, after=()):
    third = swap(gate(parts[3], after), "head", 4, 1)
    return [parts[0], swap(parts[1], "head", 4, 1)], [parts[2], third]


def sum_far(terms, away, after=(), fold_after=()):
    sent = gate(fold(away, fold_after), after)
    return [*terms, swap(sent, "head", 4, 2)], sent


def exchange_relative(parts, axis, size):
    return [p if j == 0 else swap(p, axis, size, j) for j, p in enumerate(parts)]


def exchange_pair(near, pair):
    pair = swap(pair, "head", 4, 2)
    return [swap(near, "head", 4, 1), pair, swap(pair, "head", 4, 1)]


def own_half(size, width, j):
    first = width if size == 2 * width and j == 3 else 0
    return slice(first, first + width)


def sum_all(value, axis, size):
    return sum((swap(value, axis, size, j) for j in range(1, size)), value)


def column_orders(size):
    bits = bits_down(size)
    return [bits, bits[-1:] + bits[:-1]]


def ring_sources(dp, size):
    line = size // 2
    place = dp // 2 ^ dp // 4
    held = [jnp.remainder(place - k, line) for k in range(line)]
    held = [2 * (p ^ p // 2) for p in held]
    return jnp.stack([h + (dp & 1) for h in held] + [h + 1 - (dp & 1) for h in held])


def ring_step(value, size):
    line = size // 2
    ring = [p ^ p // 2 for p in range(line)]
    pairs = [(2 * ring[p] + i, 2 * ring[(p + 1) % line] + i) for p in range(line) for i in range(2)]
    return lax.ppermute(value, "dp", pairs)


def gather_columns(rows, size):
    held, other = [rows], []
    for step in range(size // 2):
        if step:
            held[step] = gate(held[step], other[-1:])
        other.append(swap(held[step], "dp", size, 1))
        if step + 1 < size // 2:
            held.append(ring_step(held[step], size))
    return held + other


def column_places(size, bits):
    places = [0]
    for bit in reversed(bits):
        places = places + [j | bit for j in places]
    return places


def join_columns(from_ref, parts, outs):
    for i, part in enumerate(parts):
        part = part.ref
        lanes = part.shape[1]
        at = slice(None)
        if len(parts) > 1:
            at = pl.ds(pl.multiple_of(from_ref[i] * lanes, 128), lanes)
        for row, rows, out in outs:
            out[:, at] = part[row : row + rows, :]


def project_body(n, tile, scalars, near, ins, outs):
    me_ref, from_ref = scalars
    gain_ref, cos_ref, sin_ref = near
    count = len(ins) - 2 * n
    parts, xs, fvs = ins[:count], ins[count : count + n], ins[count + n :]
    q_out, k_out, kt_out, v_out, vt_out, w_out, wo_out = outs
    width = q_out.ref.shape[0]
    shard = xs[0].buffer.shape[0]
    w_ref = w_out.ref
    join_columns(from_ref, parts, [(0, 3 * width, w_ref), (3 * width, width, wo_out.ref)])
    w_out.send()
    wo_out.send()
    for j in range(n):
        x_ref, fv_ref = xs[j].ref, fvs[j].ref
        base = pl.multiple_of((me_ref[0] ^ j) * shard, shard)
        for t in range(0, shard, tile):
            at = pl.ds(pl.multiple_of(base + t, tile), tile)
            stream = x_ref[t : t + tile, :].astype(F32)
            normed = (stream * row_scale(stream) * gain_ref[...]).astype(BF16)
            qk = dot_nt(w_ref[: 2 * width, :], normed)
            cos, sin = cos_ref[:, at], sin_ref[:, at]
            turned = []
            for row in range(0, 2 * width, HEAD_DIM):
                first, second = qk[row : row + HALF], qk[row + HALF : row + HEAD_DIM]
                turned += [first * cos - second * sin, second * cos + first * sin]
            turned = jnp.concatenate(turned, axis=0)
            q_out.ref[:, at] = (turned[:width] * HEAD_DIM ** (-0.5)).astype(BF16)
            keys = turned[width:]
            kt_out.ref[:, at] = keys.astype(BF16)
            k_out.ref[at, :] = keys.T.astype(BF16)
            first_values = fv_ref[t : t + tile, :width].astype(F32)
            values = 0.5 * dot_nt(normed, w_ref[2 * width :, :]) + 0.5 * first_values
            v_out.ref[at, :] = values.astype(BF16)
            vt_out.ref[:, at] = values.T.astype(BF16)
        at = pl.ds(base, shard)
        for out in (q_out, kt_out, vt_out):
            out.send(slice(None), at)
        for out in (k_out, v_out):
            out.send(at, slice(None))


def doc_of(len_ref, token):
    run, first, last = jnp.int32(0), jnp.int32(0), jnp.int32(SEQ)
    for doc in range(NDOC):
        end = run + len_ref[0, doc]
        inside = (token >= run) & (token < end)
        first, last = jnp.where(inside, run, first), jnp.where(inside, end, last)
        run = end
    return first, last


def attend_kernel(
    bq, per, heads, skip, len_ref, me_ref, q_ref, k_ref, vt_ref, start_ref, *refs
):
    *ctx_refs, ot_ref, lse_ref, s_ref = refs[skip:]
    bk = bq
    step = pl.program_id(0)
    block = (step // per ^ me_ref[0]) * per + step % per
    first, _ = doc_of(len_ref, block * bq)
    starts = start_ref[...]

    def score(kb, tops, diagonal):
        at = pl.ds(pl.multiple_of(kb * bk, bk), bk)
        key_index = lax.broadcasted_iota(jnp.int32, (bk, bq), 0) + kb * bk
        allowed = key_index >= starts
        if diagonal:
            allowed &= key_index <= lax.broadcasted_iota(jnp.int32, (bk, bq), 1) + block * bq
        out = []
        for h in range(heads):
            rows = slice(h * HEAD_DIM, (h + 1) * HEAD_DIM)
            scores = jnp.where(allowed, dot(k_ref[at, rows], q_ref[rows, :]), NEG)
            s_ref[h, at, :] = scores
            out.append(jnp.maximum(tops[h], jnp.max(scores.reshape(bk // 8, 8, bq), axis=0)))
        return tuple(out)

    tops = score(block, tuple(jnp.full((8, bq), NEG, F32) for _ in range(heads)), True)
    tops = lax.fori_loop(first // bk, block, lambda kb, c: score(kb, c, False), tops)
    tops = [jnp.max(t, axis=0, keepdims=True) for t in tops]

    def gather(kb, carry):
        at = pl.ds(pl.multiple_of(kb * bk, bk), bk)
        out = []
        for h in range(heads):
            rows = slice(h * HEAD_DIM, (h + 1) * HEAD_DIM)
            total, acc = carry[h]
            probs = jnp.exp(s_ref[h, at, :] - tops[h])
            total = total + jnp.sum(probs.reshape(bk // 8, 8, bq), axis=0)
            out.append((total, acc + dot(vt_ref[rows, at], probs.astype(BF16))))
        return tuple(out)

    zero = tuple((jnp.zeros((8, bq), F32), jnp.zeros((HEAD_DIM, bq), F32)) for _ in range(heads))
    sums = lax.fori_loop(first // bk, block + 1, gather, zero)
    outs = []
    for h in range(heads):
        total = jnp.sum(sums[h][0], axis=0, keepdims=True)
        outs.append(sums[h][1] * (1.0 / total))
        lse_ref[h : h + 1, :] = tops[h] + jnp.log(total)
    out = jnp.concatenate(outs, axis=0)
    ot_ref[...] = out.astype(BF16)
    out = out.T.astype(BF16)
    width = out.shape[1]
    places = [(ref, c) for ref in ctx_refs for c in range(0, ref.shape[1], width)]
    for j, (ref, col) in enumerate(places):

        @pl.when(step // per == j)
        def _(ref=ref, col=col):
            rows = pl.ds(pl.multiple_of((step % per) * bq, bq), bq)
            ref[rows, col : col + width] = out


def attend(lengths, me, q_t, keys, v_t, starts, shard, widths, after=()):
    width = q_t.shape[0]
    heads = width // HEAD_DIM
    bq = min(512, shard)
    per = shard // bq
    at = lambda i, l, m: (0, (i // per ^ m[0]) * per + i % per)
    whole = lambda i, l, m: (0, 0)
    spec = pltpu.PrefetchScalarGridSpec(
        num_scalar_prefetch=2,
        grid=(SEQ // bq,),
        in_specs=[
            pl.BlockSpec((width, bq), at),
            pl.BlockSpec((SEQ, width), whole),
            pl.BlockSpec((width, SEQ), whole),
            pl.BlockSpec((1, bq), at),
        ]
        + [pl.BlockSpec(memory_space=pl.ANY)] * len(after),
        out_specs=[
            *[pl.BlockSpec((shard, w), whole) for w in widths],
            pl.BlockSpec((width, bq), at),
            pl.BlockSpec((heads, bq), at),
        ],
        scratch_shapes=[pltpu.VMEM((heads, SEQ, bq), F32)],
    )
    return pl.pallas_call(
        functools.partial(attend_kernel, bq, per, heads, len(after)),
        name="attend",
        grid_spec=spec,
        out_shape=[
            *[shape((shard, w), BF16) for w in widths],
            shape((width, SEQ), BF16),
            shape((heads, SEQ), F32),
        ],
        compiler_params=pltpu.CompilerParams(vmem_limit_bytes=VMEM_LIMIT),
        cost_estimate=MOST,
    )(lengths, me, q_t, keys, v_t, starts, *after)


def attend_back_body(n, block, scalars, near, ins, outs, *scratch):
    len_ref, me_ref = scalars
    lse_ref, start_ref, cos_ref, sin_ref = near
    dos, (ot_in, *rest) = ins[:n], ins[n:]
    gp_out, *firsts = outs
    out_ref = gp_out.ref
    dq_ref, dk_ref, dv_ref, do_ref, delta_ref = scratch
    width = dq_ref.shape[0]
    heads = width // HEAD_DIM
    shard = SEQ // n
    ot_ref = ot_in.ref
    for j in range(n):
        at = pl.ds(pl.multiple_of((me_ref[0] ^ j) * shard, shard), shard)
        grad = dos[j].ref[own_half(dos[j].buffer.shape[0], width, j), :]
        do_ref[:, at] = grad
        product = grad.astype(F32) * ot_ref[:, at].astype(F32)
        for h in range(heads):
            delta_ref[h : h + 1, at] = jnp.sum(
                product[h * HEAD_DIM : (h + 1) * HEAD_DIM], axis=0, keepdims=True
            )
    dq_ref[...] = jnp.zeros_like(dq_ref)
    dk_ref[...] = jnp.zeros_like(dk_ref)
    dv_ref[...] = jnp.zeros_like(dv_ref)
    q_ref, k_ref, kt_ref, v_ref = (r.ref for r in rest)

    def pair(kb, qb, diagonal):
        k_at = pl.ds(pl.multiple_of(kb * block, block), block)
        q_at = pl.ds(pl.multiple_of(qb * block, block), block)
        key_index = lax.broadcasted_iota(jnp.int32, (block, block), 0) + kb * block
        allowed = key_index >= start_ref[:, q_at]
        if diagonal:
            allowed &= key_index <= lax.broadcasted_iota(jnp.int32, (block, block), 1) + qb * block
        every = range(heads)
        rows = [slice(h * HEAD_DIM, (h + 1) * HEAD_DIM) for h in every]
        q_t = [q_ref[r, q_at] for r in rows]
        do_t = [do_ref[r, q_at] for r in rows]
        scores = [dot(k_ref[k_at, r], q_t[h]) for h, r in enumerate(rows)]
        dprobs = [dot(v_ref[k_at, r], do_t[h]) for h, r in enumerate(rows)]
        probs = [
            jnp.exp(jnp.where(allowed, scores[h], NEG) - lse_ref[h : h + 1, q_at]) for h in every
        ]
        dscores = [
            (probs[h] * (dprobs[h] - delta_ref[h : h + 1, q_at])).astype(BF16) for h in every
        ]
        probs = [p.astype(BF16) for p in probs]
        dv = [dot_nt(do_t[h], probs[h]) for h in every]
        dk = [dot_nt(q_t[h], dscores[h]) for h in every]
        dq = [dot(kt_ref[rows[h], k_at], dscores[h]) for h in every]
        for h in every:
            dv_ref[rows[h], k_at] += dv[h]
            dk_ref[rows[h], k_at] += dk[h]
            dq_ref[rows[h], q_at] += dq[h]

    def outer(kb, carry):
        _, end = doc_of(len_ref, kb * block + block - 1)
        pair(kb, kb, True)

        def inner(qb, c):
            pair(kb, qb, False)
            return c

        lax.fori_loop(kb + 1, (end - 1) // block + 1, inner, 0)
        return carry

    lax.fori_loop(0, SEQ // block, outer, 0)
    for j in range(n):
        at = pl.ds(pl.multiple_of((me_ref[0] ^ j) * shard, shard), shard)
        grad = 0.5 * dv_ref[:, at]
        out_ref[2 * width :, at] = grad.astype(BF16)
        first = firsts[j] if len(firsts) == n else firsts[min(j, 2)]
        cols = slice(width, 2 * width) if len(firsts) != n and j == 3 else slice(0, width)
        first.ref[:, cols] = grad.T.astype(BF16)
    for first in firsts:
        first.send()
    gp_out.send(slice(2 * width, 3 * width))
    cos, sin = cos_ref[...], sin_ref[...]
    for base, ref, scale in ((0, dq_ref, HEAD_DIM ** (-0.5)), (width, dk_ref, 1.0)):
        for row in range(0, width, HEAD_DIM):
            first = ref[row : row + HALF, :] * scale
            second = ref[row + HALF : row + HEAD_DIM, :] * scale
            out_ref[base + row : base + row + HALF, :] = (first * cos + second * sin).astype(BF16)
            out_ref[base + row + HALF : base + row + HEAD_DIM, :] = (
                second * cos - first * sin
            ).astype(BF16)
        gp_out.send(slice(base, base + width))


def join_body(n, tile, scalars, near, ins, outs):
    (gain_ref,) = near
    ctx, x_in, w_out = ins[:n], ins[n], ins[n + 1 :]
    mid, *normeds = outs
    for row in range(0, x_in.buffer.shape[0], tile):
        at = slice(row, row + tile)
        total = x_in.tile(row, tile).astype(F32)
        for j, (c, w) in enumerate(zip(ctx, w_out)):
            cols = own_half(c.buffer.shape[1], w.buffer.shape[0], j)
            total = total + dot(c.tile(row, tile)[:, cols], w.ref[...])
        rows = (total * row_scale(total) * gain_ref[...]).astype(BF16)
        for normed in normeds:
            normed.ref[at, :] = rows
            normed.send(at)
        mid.ref[at, :] = total
        mid.send(at)


def mlp_body(n, tile, scalars, near, ins, outs):
    (from_ref,) = scalars
    count = len(ins) - 2 * n
    parts, normed, grads = ins[:count], ins[count : count + n], ins[count + n :]
    mixed, dgate_out, dup_out, *gns = outs
    hidden = mixed.ref.shape[1]
    shard = normed[0].buffer.shape[0]
    if count > 1:
        *gns, made = gns
        w_ref = made.ref
        join_columns(from_ref, parts, [(0, 3 * hidden, w_ref)])
        made.send()
    else:
        w_ref = parts[0].ref
    w_gate, w_up, w_down = (w_ref.at[i * hidden : (i + 1) * hidden, :] for i in range(3))
    for j in reversed(range(n)):
        tokens_ref, og_ref = normed[j].ref, grads[j].ref
        for later in (*normed[:j][-1:], *grads[:j][-1:]):
            later.begin()

        def step(t, carry, tokens_ref=tokens_ref, og_ref=og_ref, j=j):
            rows = pl.ds(pl.multiple_of(t * tile, tile), tile)
            at = pl.ds(pl.multiple_of(j * shard + t * tile, tile), tile)
            tokens = tokens_ref[rows, :]
            gate = dot_nt(tokens, w_gate[...])
            up = dot_nt(tokens, w_up[...])
            gm = dot_nt(og_ref[rows, :], w_down[...])
            sig = 1.0 / (1.0 + jnp.exp(-gate))
            act = gate * sig
            mixed.ref[at, :] = (act * up).astype(BF16)
            dup = (gm * act).astype(BF16)
            dgate = (gm * up * sig * (1.0 + gate * (1.0 - sig))).astype(BF16)
            dup_out.ref[at, :] = dup
            dgate_out.ref[at, :] = dgate
            gns[j].ref[rows, :] = (dot(dgate, w_gate[...]) + dot(dup, w_up[...])).astype(BF16)
            return carry

        lax.fori_loop(0, shard // tile, step, 0)
        gns[j].send()
        for out in (mixed, dgate_out, dup_out):
            out.send(slice(j * shard, (j + 1) * shard))


def mlp_rest_body(n, tile, orders, scalars, near, ins, outs, acc_ref):
    w_in, mixeds, ogs = ins[0], ins[1:3], ins[3 : 3 + n]
    dgates, normed, dups = ins[3 + n : 5 + n], ins[5 + n : 5 + 2 * n], ins[5 + 2 * n :]
    parts, grads = outs[:n], outs[n:]
    half = n // 2
    hidden = acc_ref.shape[0]
    lanes = grads[0].ref.shape[2]
    shard = normed[0].buffer.shape[0]
    w_down = w_in.ref
    for load in (*mixeds, *dgates, *normed):
        load.begin()
    for j in reversed(range(n)):
        mixed_ref = mixeds[j // half].ref
        for t in range(0, shard, tile):
            rows = mixed_ref[j % half * shard + t : j % half * shard + t + tile, :]
            parts[j].ref[t : t + tile, :] = dot(rows, w_down[...]).astype(BF16)
        parts[j].send()
    for which, (lefts, rights) in ((0, (dgates, normed)), (1, (dups, normed)), (2, (mixeds, ogs))):
        for load in (*dups, *ogs) if which == 0 else ():
            load.begin()
        for j in range(n):
            left = lefts[j // half].ref[j % half * shard : (j % half + 1) * shard, :]
            part = dot_tn(left, rights[j].ref[...])
            if j == 0:
                acc_ref[...] = part
            else:
                acc_ref[...] += part
        cut_columns(scalars, orders, acc_ref, which * hidden, grads, lanes)


def cut_columns(scalars, orders, acc_ref, first, outs, lanes):
    count = acc_ref.shape[0]
    if orders is None:
        for i in range(outs[0].ref.shape[0]):
            outs[0].ref[i, first : first + count, :] = acc_ref[
                :, i * lanes : (i + 1) * lanes
            ].astype(BF16)
        return
    rows = outs[0].ref.shape[1]
    for half, places in enumerate(orders):
        low, high = max(first, half * rows), min(first + count, (half + 1) * rows)
        if low >= high:
            continue
        to = slice(low - half * rows, high - half * rows)
        for i, j in reversed(list(enumerate(places))):
            at = pl.ds(pl.multiple_of((scalars[-1][0] ^ j) * lanes, 128), lanes)
            out = outs[2 * half + i // (len(places) // 2)]
            out.ref[i % (len(places) // 2), to, :] = acc_ref[low - first : high - first, at].astype(
                BF16
            )


def middle_back_body(n, tile, scalars, near, ins, outs):
    (gain_ref,) = near
    mid_in, og_in, *terms = ins[:-n]
    w_out = ins[-n:]
    gmid_out, ga_out, gain_out, *gctx = outs
    for row in range(0, mid_in.buffer.shape[0], tile):
        at = slice(row, row + tile)
        mid = mid_in.tile(row, tile)
        grad = sum(t.tile(row, tile).astype(F32) for t in terms)
        scale = row_scale(mid)
        normed = mid * scale
        scaled = grad * gain_ref[...]
        back = scale * (scaled - normed * jnp.mean(scaled * normed, axis=-1, keepdims=True))
        total = jnp.sum(grad * normed, axis=0, keepdims=True)
        gain_out.ref[...] = total if row == 0 else gain_out.ref[...] + total
        gmid = og_in.tile(row, tile).astype(F32) + back
        ga = gmid.astype(BF16)
        for j, w in reversed(list(enumerate(w_out))):
            wide = w.buffer.shape[0]
            out, first = (gctx[j], 0) if len(gctx) == n else (gctx[min(j, 2)], wide * (j == 3))
            out.ref[first : first + wide, at] = dot_nt(w.ref[...], ga).astype(BF16)
            if first == 0:
                out.send(slice(None), at)
        ga_out.ref[at, :] = ga
        ga_out.send(at)
        gmid_out.ref[at, :] = gmid
        gmid_out.send(at)


def out_weight_body(n, scalars, near, ins, outs):
    *ctx, ga = ins
    for j, (c, out) in reversed(list(enumerate(zip(ctx, outs)))):
        cols = own_half(c.buffer.shape[1], out.ref.shape[0], j)
        out.ref[...] = dot_tn(c.ref[:, cols], ga.ref[...]).astype(BF16)
        out.send()


def unproject_body(n, tile, scalars, near, ins, outs):
    (me_ref,) = scalars
    w_ref, gp_ref = (i.ref for i in ins)
    shard = outs[0].ref.shape[0]
    for j in reversed(range(n)):
        base = (me_ref[0] ^ j) * shard
        for t in range(0, shard, tile):
            at = pl.ds(pl.multiple_of(base + t, tile), tile)
            outs[j].ref[t : t + tile, :] = dot_tn(gp_ref[:, at], w_ref[...]).astype(BF16)
        outs[j].send()


def qkv_weight_body(n, orders, scalars, near, ins, outs, acc_ref):
    me_ref, dp_ref = scalars
    gain_ref, gain_two_ref = near
    gp_in, w_in, xs, terms = ins[0], ins[1], ins[2 : 2 + n], ins[2 + n :]
    *outs, gains = outs
    shard = xs[0].buffer.shape[0]
    lanes = outs[0].ref.shape[2]
    gp_ref = gp_in.ref
    wide = gp_ref.shape[0]
    for j in range(n):
        at = pl.ds(pl.multiple_of((me_ref[0] ^ j) * shard, shard), shard)
        x_ref = xs[j].ref
        for later in xs[j + 1 : j + 2] if j + 1 < n else (w_in, *terms):
            later.begin()
        stream = x_ref[...].astype(F32)
        normed = (stream * row_scale(stream) * gain_ref[...]).astype(BF16)
        part = dot(gp_ref[:, at], normed)
        if j == 0:
            acc_ref[:wide, :] = part
        else:
            acc_ref[:wide, :] += part
    acc_ref[wide:, :] = sum(t.ref[...].astype(F32) for t in terms)
    cut_columns(scalars, orders, acc_ref, 0, outs, lanes)
    for out in outs:
        out.send()
    gain = 0.0
    for row in range(0, wide, 64):
        at = slice(row, row + 64)
        gain = gain + jnp.sum(acc_ref[at, :] * w_in.ref[at, :].astype(F32), axis=0, keepdims=True)
    gain = gain / gain_ref[...]
    both = [gain, gain_two_ref[...]]
    pieces = [g[:, c : c + 128] for g in both for c in range(0, gain.shape[1], 128)]
    gains.ref[...] = jnp.concatenate(pieces, axis=0)


def gain_rows(gains):
    high = gains.astype(BF16)
    return high, (gains - high.astype(F32)).astype(BF16)


def scatter_body(halves, scalars, near, ins, outs):
    first, second = ins[: halves[0]], ins[halves[0] : sum(halves)]
    gains_in = ins[sum(halves) :]
    rows = second[0].buffer.shape[1]
    count = second[0].buffer.shape[0]
    if gains_in:
        outs, gains_out = outs[:2], outs[2:]
        gains = gains_in[0].ref[...]
        last = first[-1].ref
        if last.shape[1] > rows:
            gains = gains + sum(
                last[i, row : row + 16, :].astype(F32)
                for i in range(last.shape[0])
                for row in range(rows, last.shape[1], 16)
            )
        each = gains.shape[0] // len(gains_out)
        for i, out in enumerate(gains_out):
            out.ref[...] = gains[i * each : (i + 1) * each]

    def total(terms, i, low, high):
        return sum(
            t.ref[i + t.buffer.shape[0] - count, low:high, :].astype(F32) for t in terms
        )

    if len(first) == 4:
        top, rest = outs
        cut = 2 * rows - rest.ref.shape[0]
        top_rows = [(first, 0, rows, 0), (second, 0, cut - rows, rows)]
        if len(top.ref.shape) == 3:
            wide = top.ref.shape[2]
            for terms, low, high, base in top_rows:
                for row in range(low, high, wide):
                    top.ref[(base + row) // wide] = total(terms, 0, row, row + wide).T
        else:
            for terms, low, high, base in top_rows:
                top.ref[base + low : base + high, :] = total(terms, 0, low, high)
        rest.ref[...] = total(second, 0, cut - rows, rows)
        return
    if gains_in:
        extra = outs[0].ref.shape[1] - rows
        for i, part in enumerate(gain_rows(gains)):
            row = rows if extra == 16 else rows + 16 * i
            outs[0].ref[i if extra == 16 else 0, row : row + 16, :] = part
    for terms, out in zip((first, second), outs):
        for i in range(count):
            out.ref[i, :rows, :] = total(terms, i, 0, rows).astype(BF16)
        out.send()


def scatter_start(parts, size, orders):
    return [
        [parts[2 * i], swap(parts[2 * i + 1], "dp", size, bits[0])] for i, bits in enumerate(orders)
    ]


def scatter_terms(held, first, last, gains):
    terms = []
    for half, parts in enumerate(held):
        for i, part in enumerate(parts):
            all_of_it = gains and half == 0 and i == len(parts) - 1 and i > 1
            terms.append((part, 1, 0 if all_of_it else first, last))
    return terms + gains


def scatter_kernel(held, gains, after=()):
    steps = len(held[0])
    rows, lanes = held[1][0].shape[1:]
    half = held[0][0].shape[0] >> (steps - 1)
    extra = 32 // half if gains else 0
    return far_call(
        functools.partial(scatter_body, [len(h) for h in held]),
        "scatter",
        [],
        [],
        scatter_terms(held, half, 2 * half, gains),
        [(shape((half, rows + extra, lanes), BF16), 1), (shape((half, rows, lanes), BF16), 1)]
        + [(shape(g.shape, F32), 1) for g in gains],
        after=after,
    )


def scatter_swap(held, sent, size, orders):
    return [
        [*parts, swap(out, "dp", size, bits[len(parts) - 1])]
        for parts, out, bits in zip(held, sent, orders)
    ]


def scatter_end(held, gains, cut, after=()):
    rows, lanes = held[1][0].shape[1:]
    return far_call(
        functools.partial(scatter_body, [len(h) for h in held]),
        "collect",
        [],
        [],
        scatter_terms(held, 0, 1, gains),
        [(shape((3, lanes, cut // 3) if gains else (cut, lanes), F32), 1)]
        + [(shape((2 * rows - cut, lanes), F32), 1)]
        + [(shape((g.shape[0] // 2, *g.shape[1:]), F32), 1) for g in gains for _ in range(2)],
        after=after,
    )


def layer_out_body(tile, scalars, near, ins, outs):
    for row in range(0, ins[0].buffer.shape[0], tile):
        at = slice(row, row + tile)
        outs[0].ref[at, :] = sum(t.tile(row, tile).astype(F32) for t in ins).astype(BF16)
        outs[0].send(at)


def first_grad_body(scalars, near, ins, outs):
    width = outs[0].ref.shape[1] // len(ins)
    for j, dv in enumerate(ins):
        at = pl.ds(pl.multiple_of((scalars[0][0] ^ j) * width, 128), width)
        outs[0].ref[:, at] = dv.ref[
            :, own_half(dv.buffer.shape[1], width, j)
        ].astype(F32)


def input_back_body(tile, scalars, near, ins, outs):
    (gain_ref,) = near
    x_in, gmid_in, *terms = ins
    for row in range(0, x_in.buffer.shape[0], tile):
        at = slice(row, row + tile)
        stream = x_in.tile(row, tile).astype(F32)
        scale = row_scale(stream)
        normed = stream * scale
        scaled = sum(t.tile(row, tile).astype(F32) for t in terms) * gain_ref[...]
        back = scale * (scaled - normed * jnp.mean(scaled * normed, axis=-1, keepdims=True))
        outs[0].ref[at, :] = gmid_in.tile(row, tile) + back
        outs[0].send(at)


def doc_tables(lengths):
    index = jnp.arange(SEQ, dtype=jnp.int32)
    ends = jnp.cumsum(lengths)
    begins = ends - lengths
    starts = jnp.max(jnp.where(begins[:, None] <= index[None, :], begins[:, None], 0), axis=0)
    inverse = jnp.exp(jnp.arange(HALF, dtype=F32) * (-2.0 * math.log(10000.0) / HEAD_DIM))
    angles = (index - starts).astype(F32)[None, :] * inverse[:, None]
    return starts[None, :], jnp.cos(angles), jnp.sin(angles)


def local(
    n,
    n_dp,
    hidden_in,
    first_values,
    doc_lengths,
    out_grad,
    qkv_weight,
    out_weight,
    gate_up_weight,
    down_weight,
    attn_gain,
    mlp_gain,
):
    shard, width = hidden_in.shape[1], qkv_weight.shape[2]
    hidden = down_weight.shape[0]
    lanes = qkv_weight.shape[0]
    dim = hidden_in.shape[2]
    tile = min(256, shard)
    me = lax.axis_index("head").reshape(1).astype(jnp.int32)
    dp = lax.axis_index("dp").reshape(1).astype(jnp.int32)
    x_own, og_own = hidden_in[0], out_grad[0]
    gain_one, gain_two = attn_gain[None, :], mlp_gain[None, :]

    per = shard // tile
    rows = jnp.concatenate(
        [qkv_weight.transpose(1, 2, 0).reshape(3 * width, lanes), out_weight], axis=0
    )
    mlp_rows = jnp.concatenate(
        [gate_up_weight.transpose(1, 2, 0).reshape(2 * hidden, lanes), down_weight], axis=0
    )
    fv_parts = [
        lax.dynamic_slice(first_values[0], (0, (me[0] ^ j) * width), (shard, width))
        for j in range(n)
    ]
    sources = ring_sources(dp[0], n_dp)
    line = n_dp // 2
    ringed = n == 4 and n_dp == 8 and lanes % 128 == 0
    if ringed:
        fv_near = swap(fv_parts[1], "head", n, 1)
        fv_far = swap(jnp.concatenate(fv_parts[2:], axis=1), "head", n, 2)
        parts = gather_columns(rows, n_dp)
        fv_far = gate(fv_far, [parts[line - 1]])
        xs = gather_relative(x_own, "head", n, lambda *x: [parts[line - 1]])
    else:
        parts = [lax.all_gather(rows, "dp", axis=1, tiled=True)]
        xs = gather_relative(x_own, "head", n)
        fvs = exchange_relative(fv_parts, "head", n)
        mlp_columns = [lax.all_gather(mlp_rows, "dp", axis=1, tiled=True)]
    starts, cos, sin = doc_tables(doc_lengths[0])

    def project(fvs, after=()):
        return far_call(
            functools.partial(project_body, n, tile),
            "project",
            [me, sources],
            [gain_one, cos, sin],
            [*parts, *xs, *fvs],
            [
                (shape((width, SEQ), BF16), n),
                (shape((SEQ, width), BF16), n),
                (shape((width, SEQ), BF16), n),
                (shape((SEQ, width), BF16), n),
                (shape((width, SEQ), BF16), n),
                (shape((3 * width, dim), BF16), 1),
                (shape((width, dim), BF16), 1),
            ],
            flops=6 * SEQ * dim * width,
            after=after,
        )

    if ringed:
        held = [gate(mlp_rows, [parts[line - 1], cos, sin, xs[1], fv_near, fv_far])]
        held.append(ring_step(held[0], n_dp))
        other = [swap(held[0], "dp", n_dp, 1)]
        og_near, og_far = swap(og_own, "head", n, 1), swap(og_own, "head", n, 2)
        fv_last = swap(fv_far[:, width:], "head", n, 1)
        projected = project([fv_parts[0], fv_near, fv_far, fv_last])
        w_near, far = swap(projected[-1], "head", n, 1), swap(projected[-1], "head", n, 2)
        held[1] = gate(held[1], [projected[0], other[0]])
        other.append(swap(held[1], "dp", n_dp, 1))
        held.append(ring_step(held[1], n_dp))
        early = [held[1]]
    else:
        projected = project(fvs)
    q_t, keys, k_t, values, v_t, w_qkv, w_out = projected
    look = functools.partial(attend, doc_lengths, me, q_t, keys, v_t, starts, shard)
    if ringed:
        ctx_own, ctx_near, ctx_far, o_t, lse = look([width, width, 2 * width], early)
        held[2] = gate(held[2], [ctx_own, other[1], far])
        other.append(swap(held[2], "dp", n_dp, 1))
        held.append(ring_step(held[2], n_dp))
        other.append(swap(held[3], "dp", n_dp, 1))
        ctxs = [ctx_own, *exchange_pair(ctx_near, ctx_far)]
        far = gate(far, [ctx_near])
        w_outs = [w_out, w_near, far, swap(far, "head", n, 1)]
        mlp_columns = held + other
    else:
        *ctx, o_t, lse = look([width] * n)
        w_outs = gather_relative(w_out, "head", n, lambda *w: [o_t])
        ctxs = exchange_relative(ctx, "head", n)

    if not ringed:
        ogs = gather_relative(og_own, "head", n)
    middle, normed_two, normed_near = far_call(
        functools.partial(join_body, n, tile),
        "join",
        [],
        [gain_two],
        [*[(a, per) for a in (*ctxs, x_own)], *w_outs],
        [(shape((shard, dim), F32), per)] + [(shape((shard, dim), BF16), per)] * 2,
        flops=2 * shard * dim * dim,
        after=[og_far, held[3], other[2]] if ringed else ogs[1:],
    )

    if ringed:
        og_far = gate(og_far, [normed_near])
        ogs = [og_own, og_near, og_far, swap(og_far, "head", n, 1)]
    half = n // 2
    groups = []

    def mlp(tokens, lo, weights):
        hiddens = [(shape((half * shard, hidden), BF16), half)] * 3
        made = [(shape((3 * hidden, dim), BF16), 1)] if len(weights) > 1 else []
        out = far_call(
            functools.partial(mlp_body, half, tile),
            "mlp",
            [sources],
            [],
            [*weights, *tokens, *ogs[lo : lo + half]],
            hiddens + [(shape((shard, dim), BF16), 1)] * half + made,
            flops=10 * half * shard * dim * hidden,
            lazy=[len(weights) + j + k for j in range(half - 1) for k in (0, half)],
        )
        groups.append(out)
        return [out[3]]

    if ringed:
        near = swap(gate(normed_near, other[3:]), "head", n, 1)
        pair = swap(normed_two, "head", n, 2)
        pair = gate(pair, mlp([normed_two, near], 0, mlp_columns))
        normed = [normed_two, near, pair, swap(pair, "head", n, 1)]
    else:
        normed = gather_relative(normed_two, "head", n)
        mlp(normed[:half], 0, mlp_columns)
    w_mlp = groups[0][-1] if ringed else mlp_columns[0]
    mlp(normed[half:], half, [w_mlp])
    gn_parts = [p for g in groups for p in g[3 : 3 + half]]
    if n == 4:
        gn_two, *gn_sent = sum_far(*sum_near(gn_parts))
    else:
        gn_two, gn_sent = sum_relative(gn_parts, "head", n)

    orders, grad_outs = None, lambda rows: [(shape((n_dp, rows, lanes), BF16), 3)]
    if ringed:
        bit_orders = [bits[::-1] for bits in column_orders(n_dp)]
        orders = [column_places(n_dp, bits) for bits in bit_orders]
        grad_outs = lambda rows: [(shape((n_dp // 2, rows // 2, lanes), BF16), 1)] * 4
    rest = far_call(
        functools.partial(mlp_rest_body, n, tile, orders),
        "mlp_rest",
        [dp],
        [],
        [(w_mlp, 1, 2 * hidden, 3 * hidden), groups[0][0], groups[1][0], *ogs]
        + [groups[0][1], groups[1][1], *normed, groups[0][2], groups[1][2]],
        [(shape((shard, dim), BF16), 1)] * n + grad_outs(3 * hidden),
        [pltpu.VMEM((hidden, dim), F32)],
        flops=8 * SEQ * dim * hidden,
        lazy=range(3, 7 + 2 * n),
        after=[*gn_sent, gn_two[1]],
    )
    mlp_parts, mlp_grads = rest[:n], rest[n:]
    layer_near = sum_near(mlp_parts) if n == 4 else ([mlp_parts[0]] * 2,) * 2
    if ringed:
        mlp_held = scatter_start(mlp_grads, n_dp, bit_orders)
    else:
        mlp_grads = lax.psum_scatter(mlp_grads[0], "dp", scatter_dimension=0, tiled=False)

    widths = [width, width, 2 * width] if n == 4 else [width] * n
    grad_middle, ga, gain_two_part, *gctx = far_call(
        functools.partial(middle_back_body, n, tile),
        "middle_back",
        [],
        [gain_two],
        [*[(a, per) for a in (middle, og_own, *gn_two)], *w_outs],
        [
            (shape((shard, dim), F32), per),
            (shape((shard, dim), BF16), per),
            (shape((1, dim), F32), 1),
        ]
        + [(shape((w, shard), BF16), per) for w in widths],
        flops=2 * shard * dim * dim,
        after=mlp_parts[:1],
    )
    if n == 4:
        dos = [gctx[0], *exchange_pair(*gctx[1:])]
    else:
        dos = exchange_relative(gctx, "head", n)
    layer_folded = [fold(layer_near[1], layer_near[0][1:])] if n == 4 else []
    out_parts = far_call(
        functools.partial(out_weight_body, n),
        "out_weight",
        [],
        [],
        [*ctxs, ga],
        [(shape((width, dim), BF16), 1)] * n,
        flops=2 * shard * dim * dim,
        after=layer_folded,
    )
    if n == 4:
        out_near = sum_near(out_parts, dos[2:3])
        layer_sent = gate(layer_folded[0], dos[2:3])
        layer_terms = [*layer_near[0], swap(layer_sent, "head", n, 2)]
        out_terms, out_sent = sum_far(*out_near, after=dos[2:3])
        sums_sent = [layer_sent, out_sent, out_terms[1]]
    else:
        layer_terms, _ = sum_relative(mlp_parts, "head", n)
        out_terms, sums_sent = sum_relative(out_parts, "head", n)
    first_sums, second_sums = [], []
    if ringed:
        first_sums = scatter_kernel(mlp_held, [], after=out_parts[:1])
        mlp_held = scatter_swap(mlp_held, first_sums, n_dp, bit_orders)
        second_sums = [h[-1] for h in mlp_held]
    gp_t, *dv = far_call(
        functools.partial(attend_back_body, n, min(256, shard)),
        "attend_back",
        [doc_lengths, me],
        [lse, starts, cos, sin],
        [*dos, o_t, q_t, keys, k_t, values],
        [(shape((3 * width, SEQ), BF16), 3)] + [(shape((shard, w), BF16), 1) for w in widths],
        [pltpu.VMEM((width, SEQ), F32)] * 3
        + [pltpu.VMEM((width, SEQ), BF16), pltpu.VMEM((width // HEAD_DIM, SEQ), F32)],
        flops=20 * SEQ * SEQ * width,
        after=[*sums_sent, *first_sums],
    )
    dvs = [dv[0], *exchange_pair(*dv[1:])] if n == 4 else exchange_relative(dv, "head", n)

    mlp_sent, third_sums = [], []
    if ringed:
        mlp_sent = scatter_kernel(mlp_held, [], after=[gp_t])
        mlp_held = scatter_swap(mlp_held, mlp_sent, n_dp, bit_orders)
        third_sums = [h[-1] for h in mlp_held]
    *grads, gains = far_call(
        functools.partial(qkv_weight_body, n, orders),
        "qkv_weight",
        [me, dp],
        [gain_one, gain_two_part],
        [gp_t, w_qkv, *xs, *out_terms],
        grad_outs(4 * width) + [(shape((2 * dim // 128, 128), F32), 1)],
        [pltpu.VMEM((4 * width, dim), F32)],
        after=[*layer_terms[1:], *mlp_sent],
        lazy=[1, *range(3, 2 + n + len(out_terms))],
    )
    if n == 4:
        gains_far = swap(gains, "head", n, 2)
        gains = gains + gains_far
    if ringed:
        held = scatter_start(grads, n_dp, bit_orders)
    gn_parts = far_call(
        functools.partial(unproject_body, n, tile),
        "unproject",
        [me],
        [],
        [w_qkv, gp_t],
        [(shape((shard, dim), BF16), 1)] * n,
        after=[*grads[:1], *third_sums, *dvs[1:3]],
    )
    first_grad = None

    def first_grad_of(after):
        return far_call(
            first_grad_body, "first_grad", [me], [], dvs, [(shape((shard, dim), F32), 1)], after=after
        )[0]

    if n == 4:
        gains = gate(gains, gn_parts[:1])
        gains = gains + swap(gains, "head", n, 1)
    else:
        gains = sum_all(gains, "head", n)
    def layer_out_of(after):
        return far_call(
            functools.partial(layer_out_body, tile),
            "layer_out",
            [],
            [],
            [(a, per) for a in (middle, *layer_terms)],
            [(shape((shard, dim), BF16), per)],
            after=after,
        )[0]

    def input_grad_of():
        return far_call(
            functools.partial(input_back_body, tile),
            "input_back",
            [],
            [gain_one],
            [(a, per) for a in (x_own, grad_middle, *gn_one)],
            [(shape((shard, dim), F32), per)],
        )[0]

    if ringed:
        layer_out = layer_out_of(gn_parts[:1])
        sent = scatter_kernel(held, [])
        gn_near = sum_near(gn_parts, [gains_far, layer_out, *[h[-1] for h in held]])
        gn_one, gn_sent = sum_far(*gn_near, fold_after=sent)
        held = scatter_swap(held, sent, n_dp, bit_orders)
        gains = gate(gains, [gn_sent, gn_one[1]])
        gains = gains + swap(gains, "dp", n_dp, bit_orders[0][0])
        first_grad = first_grad_of([gn_sent])
        mlp_gu, mlp_down = scatter_end(mlp_held, [], 2 * hidden, after=[gn_sent])
        gains = gate(gains, [first_grad, mlp_down])
        gains = gains + swap(gains, "dp", n_dp, bit_orders[0][1])
        input_grad = input_grad_of()
        *sent, gains = scatter_kernel(held, [gains])
        held = scatter_swap(held, sent, n_dp, bit_orders)
    else:
        gn_one, _ = sum_relative(gn_parts, "head", n)
        layer_out, input_grad = layer_out_of([]), input_grad_of()
        gains = sum_all(gains, "dp", n_dp)
        grads = lax.psum_scatter(grads[0], "dp", scatter_dimension=0, tiled=False).astype(F32)
        qkv_grad, out_grad_w = grads[: 3 * width], grads[3 * width :]
        mlp_grads = mlp_grads.astype(F32)
        mlp_gu, mlp_down = mlp_grads[: 2 * hidden], mlp_grads[2 * hidden :]
    if ringed:
        qkv_grad, out_grad_w, gain_one_grad, gain_two_grad = scatter_end(
            held, [gains], 3 * width, after=[input_grad]
        )
        qkv_grad = qkv_grad.transpose(1, 0, 2)
    else:
        qkv_grad = qkv_grad.reshape(3, width, lanes).transpose(2, 0, 1)
        gain_one_grad, gain_two_grad = gains.reshape(2, dim)
    if first_grad is None:
        stacked = jnp.stack(dvs)
        placed = [
            lax.dynamic_index_in_dim(stacked, me[0] ^ i, keepdims=False) for i in range(n)
        ]
        first_grad = jnp.concatenate(placed, axis=1).astype(F32)
    return (
        layer_out[None],
        input_grad[None],
        first_grad[None],
        qkv_grad,
        out_grad_w,
        mlp_gu.reshape(2, hidden, lanes).transpose(2, 0, 1),
        mlp_down,
        gain_one_grad.reshape(dim),
        gain_two_grad.reshape(dim),
    )


def solution(mesh):
    tokens = P("dp", "head", None)
    columns = P("dp", None, "head")
    rows = P("head", "dp")
    return jax.shard_map(
        functools.partial(local, mesh.shape["head"], mesh.shape["dp"]),
        mesh=mesh,
        in_specs=(tokens, tokens, P("dp", None), tokens, columns, rows, columns, rows, P(), P()),
        out_specs=(tokens, tokens, tokens, columns, rows, columns, rows, P(), P()),
        check_vma=False,
    )
```

```python
import functools
import math

import jax
import jax.numpy as jnp
from jax import lax
from jax.experimental import pallas as pl
from jax.experimental.pallas import tpu as pltpu
from jax.sharding import PartitionSpec as P

HEAD_DIM = 64
HALF = HEAD_DIM // 2
SEQ = 2048
NDOC = 16
NORM_EPS = 1e-06
NEG = -1e30
F32 = jnp.float32
BF16 = jnp.bfloat16
VMEM_LIMIT = 65280 << 10
SHORT, SMALL, MIDDLE, MOST, LONG = (
    pl.CostEstimate(flops=f << 30, bytes_accessed=1, transcendentals=0) for f in (0, 1, 3, 6, 12)
)
COSTS = {
    "project": MOST,
    **dict.fromkeys(("mlp", "mlp_rest", "middle_back"), LONG),
    **dict.fromkeys(("attend_back", "unproject", "qkv_weight"), LONG),
    **dict.fromkeys(("fold", "out_weight"), MIDDLE),
    **dict.fromkeys(("first_grad", "layer_out", "collect"), SMALL),
}

VMEM = pl.BlockSpec(memory_space=pltpu.VMEM)
SMEM = pl.BlockSpec(memory_space=pltpu.SMEM)


def shape(dims, dtype):
    return jax.ShapeDtypeStruct(dims, dtype)


def dot(a, b):
    return jnp.dot(a, b, preferred_element_type=F32)


def dot_nt(a, b):
    return lax.dot_general(a, b, (((1,), (1,)), ((), ())), preferred_element_type=F32)


def dot_tn(a, b):
    return lax.dot_general(a, b, (((0,), (0,)), ((), ())), preferred_element_type=F32)


class Fetched:
    def __init__(self, source, buffer, sems, pieces):
        self.buffer, self.waiting, self.begun = buffer, {}, set()
        self.rows = buffer.shape[0] // pieces
        for i in range(pieces):
            at = (pl.ds(i * self.rows, self.rows),) if pieces > 1 else ()
            src, dst = (source.at[at], buffer.at[at]) if at else (source, buffer)
            self.waiting[i] = pltpu.make_async_copy(src, dst, sems.at[i])

    def start(self, i):
        if i in self.waiting and i not in self.begun:
            self.begun.add(i)
            self.waiting[i].start()

    def begin(self):
        for i in list(self.waiting):
            self.start(i)

    def finish(self, i):
        self.start(i)
        self.waiting.pop(i).wait()

    def tile(self, first, rows):
        for i in list(self.waiting):
            if first < (i + 1) * self.rows and first + rows > i * self.rows:
                self.finish(i)
        return self.buffer[first : first + rows, :]

    @property
    def ref(self):
        for i in list(self.waiting):
            self.finish(i)
        return self.buffer


class Stored:
    def __init__(self, target, buffer, sems):
        self.target, self.ref, self.sems, self.copies = target, buffer, sems, []

    def send(self, *at):
        copy = pltpu.make_async_copy(
            self.ref.at[at], self.target.at[at], self.sems.at[len(self.copies)]
        )
        copy.start()
        self.copies.append(copy)


def far_call(body, name, scalars, near, ins, outs, scratch=(), flops=0, after=(), lazy=()):
    pieces = [i[1] if isinstance(i, tuple) else 1 for i in ins]
    spans = [i[2:] if isinstance(i, tuple) and len(i) > 2 else None for i in ins]
    ins = [i[0] if isinstance(i, tuple) else i for i in ins]
    held_in = [
        a if s is None else shape((s[1] - s[0], *a.shape[1:]), a.dtype) for a, s in zip(ins, spans)
    ]
    counts = [len(scalars), len(near), len(ins), len(after), len(outs)]
    held = [*held_in, *[o for o, _ in outs]]

    def kernel(*refs):
        groups = []
        for count in (*counts, len(ins), len(outs), len(outs), len(ins)):
            groups.append(refs[:count])
            refs = refs[count:]
        scalar_refs, near_refs, sources, _, targets, buffers, out_buffers, out_sems, sems = groups
        sources = [
            r if s is None else r.at[pl.ds(s[0], s[1] - s[0])] for r, s in zip(sources, spans)
        ]
        fetched = [Fetched(*f) for f in zip(sources, buffers, sems, pieces)]
        for i in range(max(pieces)):
            for k, f in enumerate(fetched):
                if k not in lazy:
                    f.start(i)
        stored = [Stored(*t) for t in zip(targets, out_buffers, out_sems)]
        body(scalar_refs, near_refs, fetched, stored, *refs)
        for out in stored:
            if not out.copies:
                out.send()
        for out in stored:
            for copy in out.copies:
                copy.wait()

    far = pl.BlockSpec(memory_space=pl.ANY)
    moved = sum(math.prod(a.shape) * jnp.dtype(a.dtype).itemsize for a in held)
    return pl.pallas_call(
        kernel,
        name=name,
        out_shape=[o for o, _ in outs],
        in_specs=[SMEM] * len(scalars) + [VMEM] * len(near) + [far] * (len(ins) + len(after)),
        out_specs=[far] * len(outs),
        scratch_shapes=[pltpu.VMEM(a.shape, a.dtype) for a in held]
        + [pltpu.SemaphoreType.DMA((pieces,)) for _, pieces in outs]
        + [pltpu.SemaphoreType.DMA((count,)) for count in pieces]
        + list(scratch),
        compiler_params=pltpu.CompilerParams(vmem_limit_bytes=VMEM_LIMIT),
        cost_estimate=COSTS.get(name, SHORT),
    )(*scalars, *near, *ins, *after)


def gate(value, after):
    if not after:
        return value
    return pl.pallas_call(
        lambda *refs: None,
        name="gate",
        out_shape=shape(value.shape, value.dtype),
        in_specs=[pl.BlockSpec(memory_space=pl.ANY)] * (1 + len(after)),
        out_specs=pl.BlockSpec(memory_space=pl.ANY),
        input_output_aliases={0: 0},
    )(value, *after)


def row_scale(stream):
    return lax.rsqrt(jnp.mean(stream * stream, axis=-1, keepdims=True) + NORM_EPS)


def swap(value, axis, size, bit):
    return lax.ppermute(value, axis, [(i, i ^ bit) for i in range(size)])


def bits_down(size):
    return [1 << b for b in reversed(range(size.bit_length() - 1))]


def gather_relative(value, axis, size, hold=None):
    parts = {0: value}
    for bit in bits_down(size):
        moved = {0: swap(value, axis, size, bit)}
        if bit == 1 and hold:
            after = hold(parts[0], moved[0])
            parts.update({j: gate(v, after) for j, v in parts.items() if j})
        moved.update({j: swap(v, axis, size, bit) for j, v in parts.items() if j})
        parts.update({j | bit: v for j, v in moved.items()})
    return [parts[j] for j in range(size)]


def fold_body(scalars, near, ins, outs):
    rows = outs[0].ref.shape[0]
    step = min(rows, 128)
    for row in range(0, rows, step):
        at = slice(row, row + step)
        outs[0].ref[at, :] = sum(t.tile(row, step).astype(F32) for t in ins).astype(BF16)
        outs[0].send(at)


def fold(terms, after=()):
    pieces = max(1, terms[0].shape[0] // 128)
    outs = [(shape(terms[0].shape, BF16), pieces)]
    return far_call(fold_body, "fold", [], [], [(t, pieces) for t in terms], outs, after=after)[0]


def sum_relative(parts, axis, size, after=(), first_after=(), fold_after=()):
    parts = dict(enumerate([[p] for p in parts]))
    bit, sent = 1, []
    while bit < size:
        kept = {}
        for j in sorted((j for j in parts if not j & bit), reverse=True):
            away = parts[j | bit]
            if len(away) > 1:
                away = gate(fold(away, fold_after), after)
                sent.append(away)
            else:
                away = gate(away[0], first_after)
            kept[j] = parts[j] + [swap(away, axis, size, bit)]
        parts = kept
        bit *= 2
    return parts[0], sent


def sum_near(parts, after=()):
    third = swap(gate(parts[3], after), "head", 4, 1)
    return [parts[0], swap(parts[1], "head", 4, 1)], [parts[2], third]


def sum_far(terms, away, after=(), fold_after=()):
    sent = gate(fold(away, fold_after), after)
    return [*terms, swap(sent, "head", 4, 2)], sent


def exchange_relative(parts, axis, size):
    return [p if j == 0 else swap(p, axis, size, j) for j, p in enumerate(parts)]


def exchange_pair(near, pair):
    pair = swap(pair, "head", 4, 2)
    return [swap(near, "head", 4, 1), pair, swap(pair, "head", 4, 1)]


def own_half(size, width, j):
    first = width if size == 2 * width and j == 3 else 0
    return slice(first, first + width)


def sum_all(value, axis, size):
    return sum((swap(value, axis, size, j) for j in range(1, size)), value)


def column_orders(size):
    bits = bits_down(size)
    return [bits, bits[-1:] + bits[:-1]]


def ring_sources(dp, size):
    line = size // 2
    place = dp // 2 ^ dp // 4
    held = [jnp.remainder(place - k, line) for k in range(line)]
    held = [2 * (p ^ p // 2) for p in held]
    return jnp.stack([h + (dp & 1) for h in held] + [h + 1 - (dp & 1) for h in held])


def ring_step(value, size):
    line = size // 2
    ring = [p ^ p // 2 for p in range(line)]
    pairs = [(2 * ring[p] + i, 2 * ring[(p + 1) % line] + i) for p in range(line) for i in range(2)]
    return lax.ppermute(value, "dp", pairs)


def gather_columns(rows, size):
    held, other = [rows], []
    for step in range(size // 2):
        if step:
            held[step] = gate(held[step], other[-1:])
        other.append(swap(held[step], "dp", size, 1))
        if step + 1 < size // 2:
            held.append(ring_step(held[step], size))
    return held + other


def column_places(size, bits):
    places = [0]
    for bit in reversed(bits):
        places = places + [j | bit for j in places]
    return places


def join_columns(from_ref, parts, outs):
    for i, part in enumerate(parts):
        part = part.ref
        lanes = part.shape[1]
        at = slice(None)
        if len(parts) > 1:
            at = pl.ds(pl.multiple_of(from_ref[i] * lanes, 128), lanes)
        for row, rows, out in outs:
            out[:, at] = part[row : row + rows, :]


def project_body(n, tile, scalars, near, ins, outs):
    me_ref, from_ref = scalars
    gain_ref, cos_ref, sin_ref = near
    count = len(ins) - 2 * n
    parts, xs, fvs = ins[:count], ins[count : count + n], ins[count + n :]
    q_out, k_out, kt_out, v_out, vt_out, w_out, wo_out = outs
    width = q_out.ref.shape[0]
    shard = xs[0].buffer.shape[0]
    w_ref = w_out.ref
    join_columns(from_ref, parts, [(0, 3 * width, w_ref), (3 * width, width, wo_out.ref)])
    w_out.send()
    wo_out.send()
    for j in range(n):
        x_ref, fv_ref = xs[j].ref, fvs[j].ref
        base = pl.multiple_of((me_ref[0] ^ j) * shard, shard)
        for t in range(0, shard, tile):
            at = pl.ds(pl.multiple_of(base + t, tile), tile)
            stream = x_ref[t : t + tile, :].astype(F32)
            normed = (stream * row_scale(stream) * gain_ref[...]).astype(BF16)
            qk = dot_nt(w_ref[: 2 * width, :], normed)
            cos, sin = cos_ref[:, at], sin_ref[:, at]
            turned = []
            for row in range(0, 2 * width, HEAD_DIM):
                first, second = qk[row : row + HALF], qk[row + HALF : row + HEAD_DIM]
                turned += [first * cos - second * sin, second * cos + first * sin]
            turned = jnp.concatenate(turned, axis=0)
            q_out.ref[:, at] = (turned[:width] * HEAD_DIM ** (-0.5)).astype(BF16)
            keys = turned[width:]
            kt_out.ref[:, at] = keys.astype(BF16)
            k_out.ref[at, :] = keys.T.astype(BF16)
            first_values = fv_ref[t : t + tile, :width].astype(F32)
            values = 0.5 * dot_nt(normed, w_ref[2 * width :, :]) + 0.5 * first_values
            v_out.ref[at, :] = values.astype(BF16)
            vt_out.ref[:, at] = values.T.astype(BF16)
        at = pl.ds(base, shard)
        for out in (q_out, kt_out, vt_out):
            out.send(slice(None), at)
        for out in (k_out, v_out):
            out.send(at, slice(None))


def doc_of(len_ref, token):
    run, first, last = jnp.int32(0), jnp.int32(0), jnp.int32(SEQ)
    for doc in range(NDOC):
        end = run + len_ref[0, doc]
        inside = (token >= run) & (token < end)
        first, last = jnp.where(inside, run, first), jnp.where(inside, end, last)
        run = end
    return first, last


def attend_kernel(
    bq, per, heads, skip, len_ref, me_ref, q_ref, k_ref, vt_ref, start_ref, *refs
):
    *ctx_refs, ot_ref, lse_ref, s_ref = refs[skip:]
    bk = bq
    step = pl.program_id(0)
    block = (step // per ^ me_ref[0]) * per + step % per
    first, _ = doc_of(len_ref, block * bq)
    starts = start_ref[...]

    heads_rows = [slice(h * HEAD_DIM, (h + 1) * HEAD_DIM) for h in range(heads)]
    half = bq // 2 if bq % 256 == 0 else bq
    halves = [(col, col + half, col + half) for col in range(0, bq, half)]

    def own_keys(count):
        return pl.ds(pl.multiple_of(block * bk, bk), count)

    def top_of(scores):
        return jnp.max(scores.reshape(scores.shape[0] // 8, 8, scores.shape[1]), axis=0)

    def score(kb, tops):
        at = pl.ds(pl.multiple_of(kb * bk, bk), bk)
        allowed = lax.broadcasted_iota(jnp.int32, (bk, bq), 0) + kb * bk >= starts
        out = []
        for h, rows in enumerate(heads_rows):
            scores = jnp.where(allowed, dot(k_ref[at, rows], q_ref[rows, :]), NEG)
            s_ref[h, at, :] = scores
            out.append(jnp.maximum(tops[h], top_of(scores)))
        return tuple(out)

    parts = [[] for _ in range(heads)]
    for low, high, count in halves:
        key_index = lax.broadcasted_iota(jnp.int32, (count, high - low), 0)
        allowed = key_index + block * bk >= starts[:, low:high]
        allowed &= key_index <= lax.broadcasted_iota(jnp.int32, (count, high - low), 1) + low
        for h, rows in enumerate(heads_rows):
            scores = dot(k_ref[own_keys(count), rows], q_ref[rows, low:high])
            scores = jnp.where(allowed, scores, NEG)
            s_ref[h, own_keys(count), low:high] = scores
            parts[h].append(top_of(scores))
    tops = tuple(jnp.concatenate(p, axis=1) for p in parts)
    tops = lax.fori_loop(first // bk, block, score, tops)
    tops = [jnp.max(t, axis=0, keepdims=True) for t in tops]

    def weigh(h, at, cols):
        probs = jnp.exp(s_ref[h, at, cols] - tops[h][:, cols])
        total = jnp.sum(probs.reshape(probs.shape[0] // 8, 8, probs.shape[1]), axis=0)
        return total, dot(vt_ref[heads_rows[h], at], probs.astype(BF16))

    def gather(kb, carry):
        at = pl.ds(pl.multiple_of(kb * bk, bk), bk)
        out = []
        for h in range(heads):
            total, acc = weigh(h, at, slice(None))
            out.append((carry[h][0] + total, carry[h][1] + acc))
        return tuple(out)

    sums = []
    for h in range(heads):
        pairs = [weigh(h, own_keys(count), slice(low, high)) for low, high, count in halves]
        sums.append(tuple(jnp.concatenate(p, axis=1) for p in zip(*pairs)))
    sums = lax.fori_loop(first // bk, block, gather, tuple(sums))
    outs = []
    for h in range(heads):
        total = jnp.sum(sums[h][0], axis=0, keepdims=True)
        outs.append(sums[h][1] * (1.0 / total))
        lse_ref[h : h + 1, :] = tops[h] + jnp.log(total)
    out = jnp.concatenate(outs, axis=0)
    ot_ref[...] = out.astype(BF16)
    out = out.T.astype(BF16)
    width = out.shape[1]
    places = [(ref, c) for ref in ctx_refs for c in range(0, ref.shape[1], width)]
    for j, (ref, col) in enumerate(places):

        @pl.when(step // per == j)
        def _(ref=ref, col=col):
            rows = pl.ds(pl.multiple_of((step % per) * bq, bq), bq)
            ref[rows, col : col + width] = out


def attend(lengths, me, q_t, keys, v_t, starts, shard, widths, after=()):
    width = q_t.shape[0]
    heads = width // HEAD_DIM
    bq = min(512, shard)
    per = shard // bq
    at = lambda i, l, m: (0, (i // per ^ m[0]) * per + i % per)
    whole = lambda i, l, m: (0, 0)
    spec = pltpu.PrefetchScalarGridSpec(
        num_scalar_prefetch=2,
        grid=(SEQ // bq,),
        in_specs=[
            pl.BlockSpec((width, bq), at),
            pl.BlockSpec((SEQ, width), whole),
            pl.BlockSpec((width, SEQ), whole),
            pl.BlockSpec((1, bq), at),
        ]
        + [pl.BlockSpec(memory_space=pl.ANY)] * len(after),
        out_specs=[
            *[pl.BlockSpec((shard, w), whole) for w in widths],
            pl.BlockSpec((width, bq), at),
            pl.BlockSpec((heads, bq), at),
        ],
        scratch_shapes=[pltpu.VMEM((heads, SEQ, bq), F32)],
    )
    return pl.pallas_call(
        functools.partial(attend_kernel, bq, per, heads, len(after)),
        name="attend",
        grid_spec=spec,
        out_shape=[
            *[shape((shard, w), BF16) for w in widths],
            shape((width, SEQ), BF16),
            shape((heads, SEQ), F32),
        ],
        compiler_params=pltpu.CompilerParams(vmem_limit_bytes=VMEM_LIMIT),
        cost_estimate=MOST,
    )(lengths, me, q_t, keys, v_t, starts, *after)


def attend_back_body(n, block, scalars, near, ins, outs, *scratch):
    len_ref, me_ref = scalars
    lse_ref, start_ref, cos_ref, sin_ref = near
    dos, (ot_in, *rest) = ins[:n], ins[n:]
    gp_out, *firsts = outs
    out_ref = gp_out.ref
    dq_ref, dk_ref, dv_ref, do_ref, delta_ref = scratch
    width = dq_ref.shape[0]
    heads = width // HEAD_DIM
    shard = SEQ // n
    ot_ref = ot_in.ref
    for j in range(n):
        at = pl.ds(pl.multiple_of((me_ref[0] ^ j) * shard, shard), shard)
        grad = dos[j].ref[own_half(dos[j].buffer.shape[0], width, j), :]
        do_ref[:, at] = grad
        product = grad.astype(F32) * ot_ref[:, at].astype(F32)
        for h in range(heads):
            delta_ref[h : h + 1, at] = jnp.sum(
                product[h * HEAD_DIM : (h + 1) * HEAD_DIM], axis=0, keepdims=True
            )
    dq_ref[...] = jnp.zeros_like(dq_ref)
    dk_ref[...] = jnp.zeros_like(dk_ref)
    dv_ref[...] = jnp.zeros_like(dv_ref)
    q_ref, k_ref, kt_ref, v_ref = (r.ref for r in rest)

    def pair(kb, qb, diagonal):
        k_at = pl.ds(pl.multiple_of(kb * block, block), block)
        q_at = pl.ds(pl.multiple_of(qb * block, block), block)
        key_index = lax.broadcasted_iota(jnp.int32, (block, block), 0) + kb * block
        allowed = key_index >= start_ref[:, q_at]
        if diagonal:
            allowed &= key_index <= lax.broadcasted_iota(jnp.int32, (block, block), 1) + qb * block
        every = range(heads)
        rows = [slice(h * HEAD_DIM, (h + 1) * HEAD_DIM) for h in every]
        q_t = [q_ref[r, q_at] for r in rows]
        do_t = [do_ref[r, q_at] for r in rows]
        scores = [dot(k_ref[k_at, r], q_t[h]) for h, r in enumerate(rows)]
        dprobs = [dot(v_ref[k_at, r], do_t[h]) for h, r in enumerate(rows)]
        probs = [
            jnp.exp(jnp.where(allowed, scores[h], NEG) - lse_ref[h : h + 1, q_at]) for h in every
        ]
        dscores = [
            (probs[h] * (dprobs[h] - delta_ref[h : h + 1, q_at])).astype(BF16) for h in every
        ]
        probs = [p.astype(BF16) for p in probs]
        dv = [dot_nt(do_t[h], probs[h]) for h in every]
        dk = [dot_nt(q_t[h], dscores[h]) for h in every]
        dq = [dot(kt_ref[rows[h], k_at], dscores[h]) for h in every]
        for h in every:
            dv_ref[rows[h], k_at] += dv[h]
            dk_ref[rows[h], k_at] += dk[h]
            dq_ref[rows[h], q_at] += dq[h]

    def outer(kb, carry):
        _, end = doc_of(len_ref, kb * block + block - 1)
        pair(kb, kb, True)

        def inner(qb, c):
            pair(kb, qb, False)
            return c

        lax.fori_loop(kb + 1, (end - 1) // block + 1, inner, 0)
        return carry

    lax.fori_loop(0, SEQ // block, outer, 0)
    for j in range(n):
        at = pl.ds(pl.multiple_of((me_ref[0] ^ j) * shard, shard), shard)
        grad = 0.5 * dv_ref[:, at]
        out_ref[2 * width :, at] = grad.astype(BF16)
        first = firsts[j] if len(firsts) == n else firsts[min(j, 2)]
        cols = slice(width, 2 * width) if len(firsts) != n and j == 3 else slice(0, width)
        first.ref[:, cols] = grad.T.astype(BF16)
    for first in firsts:
        first.send()
    gp_out.send(slice(2 * width, 3 * width))
    cos, sin = cos_ref[...], sin_ref[...]
    for base, ref, scale in ((0, dq_ref, HEAD_DIM ** (-0.5)), (width, dk_ref, 1.0)):
        for row in range(0, width, HEAD_DIM):
            first = ref[row : row + HALF, :] * scale
            second = ref[row + HALF : row + HEAD_DIM, :] * scale
            out_ref[base + row : base + row + HALF, :] = (first * cos + second * sin).astype(BF16)
            out_ref[base + row + HALF : base + row + HEAD_DIM, :] = (
                second * cos - first * sin
            ).astype(BF16)
        gp_out.send(slice(base, base + width))


def join_body(n, tile, scalars, near, ins, outs):
    (gain_ref,) = near
    ctx, x_in, w_out = ins[:n], ins[n], ins[n + 1 :]
    mid, *normeds = outs
    for row in range(0, x_in.buffer.shape[0], tile):
        at = slice(row, row + tile)
        total = x_in.tile(row, tile).astype(F32)
        for j, (c, w) in enumerate(zip(ctx, w_out)):
            cols = own_half(c.buffer.shape[1], w.buffer.shape[0], j)
            total = total + dot(c.tile(row, tile)[:, cols], w.ref[...])
        rows = (total * row_scale(total) * gain_ref[...]).astype(BF16)
        for normed in normeds:
            normed.ref[at, :] = rows
            normed.send(at)
        mid.ref[at, :] = total
        mid.send(at)


def mlp_body(n, tile, scalars, near, ins, outs):
    (from_ref,) = scalars
    count = len(ins) - 2 * n
    parts, normed, grads = ins[:count], ins[count : count + n], ins[count + n :]
    mixed, dgate_out, dup_out, *gns = outs
    hidden = mixed.ref.shape[1]
    shard = normed[0].buffer.shape[0]
    if count > 1:
        *gns, made = gns
        w_ref = made.ref
        join_columns(from_ref, parts, [(0, 3 * hidden, w_ref)])
        made.send()
    else:
        w_ref = parts[0].ref
    w_gate, w_up, w_down = (w_ref.at[i * hidden : (i + 1) * hidden, :] for i in range(3))
    for j in reversed(range(n)):
        tokens_ref, og_ref = normed[j].ref, grads[j].ref
        for later in (*normed[:j][-1:], *grads[:j][-1:]):
            later.begin()

        def step(t, carry, tokens_ref=tokens_ref, og_ref=og_ref, j=j):
            rows = pl.ds(pl.multiple_of(t * tile, tile), tile)
            at = pl.ds(pl.multiple_of(j * shard + t * tile, tile), tile)
            tokens = tokens_ref[rows, :]
            gate = dot_nt(tokens, w_gate[...])
            up = dot_nt(tokens, w_up[...])
            gm = dot_nt(og_ref[rows, :], w_down[...])
            sig = 1.0 / (1.0 + jnp.exp(-gate))
            act = gate * sig
            mixed.ref[at, :] = (act * up).astype(BF16)
            dup = (gm * act).astype(BF16)
            dgate = (gm * up * sig * (1.0 + gate * (1.0 - sig))).astype(BF16)
            dup_out.ref[at, :] = dup
            dgate_out.ref[at, :] = dgate
            gns[j].ref[rows, :] = (dot(dgate, w_gate[...]) + dot(dup, w_up[...])).astype(BF16)
            return carry

        lax.fori_loop(0, shard // tile, step, 0)
        gns[j].send()
        for out in (mixed, dgate_out, dup_out):
            out.send(slice(j * shard, (j + 1) * shard))


def mlp_rest_body(n, tile, orders, scalars, near, ins, outs, acc_ref):
    w_in, mixeds, ogs = ins[0], ins[1:3], ins[3 : 3 + n]
    dgates, normed, dups = ins[3 + n : 5 + n], ins[5 + n : 5 + 2 * n], ins[5 + 2 * n :]
    parts, grads = outs[:n], outs[n:]
    half = n // 2
    hidden = acc_ref.shape[0]
    lanes = grads[0].ref.shape[2]
    shard = normed[0].buffer.shape[0]
    w_down = w_in.ref
    for load in (*mixeds, *dgates, *normed):
        load.begin()
    for j in reversed(range(n)):
        mixed_ref = mixeds[j // half].ref
        for t in range(0, shard, tile):
            rows = mixed_ref[j % half * shard + t : j % half * shard + t + tile, :]
            parts[j].ref[t : t + tile, :] = dot(rows, w_down[...]).astype(BF16)
        parts[j].send()
    for which, (lefts, rights) in ((0, (dgates, normed)), (1, (dups, normed)), (2, (mixeds, ogs))):
        for load in (*dups, *ogs) if which == 0 else ():
            load.begin()
        for j in range(n):
            left = lefts[j // half].ref[j % half * shard : (j % half + 1) * shard, :]
            part = dot_tn(left, rights[j].ref[...])
            if j == 0:
                acc_ref[...] = part
            else:
                acc_ref[...] += part
        cut_columns(scalars, orders, acc_ref, which * hidden, grads, lanes)


def cut_columns(scalars, orders, acc_ref, first, outs, lanes):
    count = acc_ref.shape[0]
    if orders is None:
        for i in range(outs[0].ref.shape[0]):
            outs[0].ref[i, first : first + count, :] = acc_ref[
                :, i * lanes : (i + 1) * lanes
            ].astype(BF16)
        return
    rows = outs[0].ref.shape[1]
    for half, places in enumerate(orders):
        low, high = max(first, half * rows), min(first + count, (half + 1) * rows)
        if low >= high:
            continue
        to = slice(low - half * rows, high - half * rows)
        for i, j in reversed(list(enumerate(places))):
            at = pl.ds(pl.multiple_of((scalars[-1][0] ^ j) * lanes, 128), lanes)
            out = outs[2 * half + i // (len(places) // 2)]
            out.ref[i % (len(places) // 2), to, :] = acc_ref[low - first : high - first, at].astype(
                BF16
            )


def middle_back_body(n, tile, scalars, near, ins, outs):
    (gain_ref,) = near
    mid_in, og_in, *terms = ins[:-n]
    w_out = ins[-n:]
    gmid_out, ga_out, gain_out, *gctx = outs
    for row in range(0, mid_in.buffer.shape[0], tile):
        at = slice(row, row + tile)
        mid = mid_in.tile(row, tile)
        grad = sum(t.tile(row, tile).astype(F32) for t in terms)
        scale = row_scale(mid)
        normed = mid * scale
        scaled = grad * gain_ref[...]
        back = scale * (scaled - normed * jnp.mean(scaled * normed, axis=-1, keepdims=True))
        total = jnp.sum(grad * normed, axis=0, keepdims=True)
        gain_out.ref[...] = total if row == 0 else gain_out.ref[...] + total
        gmid = og_in.tile(row, tile).astype(F32) + back
        ga = gmid.astype(BF16)
        for j, w in reversed(list(enumerate(w_out))):
            wide = w.buffer.shape[0]
            out, first = (gctx[j], 0) if len(gctx) == n else (gctx[min(j, 2)], wide * (j == 3))
            out.ref[first : first + wide, at] = dot_nt(w.ref[...], ga).astype(BF16)
            if first == 0:
                out.send(slice(None), at)
        ga_out.ref[at, :] = ga
        ga_out.send(at)
        gmid_out.ref[at, :] = gmid
        gmid_out.send(at)


def out_weight_body(n, scalars, near, ins, outs):
    *ctx, ga = ins
    for j, (c, out) in reversed(list(enumerate(zip(ctx, outs)))):
        cols = own_half(c.buffer.shape[1], out.ref.shape[0], j)
        out.ref[...] = dot_tn(c.ref[:, cols], ga.ref[...]).astype(BF16)
        out.send()


def unproject_body(n, tile, scalars, near, ins, outs):
    (me_ref,) = scalars
    w_ref, gp_ref = (i.ref for i in ins)
    shard = outs[0].ref.shape[0]
    for j in reversed(range(n)):
        base = (me_ref[0] ^ j) * shard
        for t in range(0, shard, tile):
            at = pl.ds(pl.multiple_of(base + t, tile), tile)
            outs[j].ref[t : t + tile, :] = dot_tn(gp_ref[:, at], w_ref[...]).astype(BF16)
        outs[j].send()


def qkv_weight_body(n, orders, scalars, near, ins, outs, acc_ref):
    me_ref, dp_ref = scalars
    gain_ref, gain_two_ref = near
    gp_in, w_in, xs, terms = ins[0], ins[1], ins[2 : 2 + n], ins[2 + n :]
    *outs, gains = outs
    shard = xs[0].buffer.shape[0]
    lanes = outs[0].ref.shape[2]
    gp_ref = gp_in.ref
    wide = gp_ref.shape[0]
    for j in range(n):
        at = pl.ds(pl.multiple_of((me_ref[0] ^ j) * shard, shard), shard)
        x_ref = xs[j].ref
        for later in xs[j + 1 : j + 2] if j + 1 < n else (w_in, *terms):
            later.begin()
        stream = x_ref[...].astype(F32)
        normed = (stream * row_scale(stream) * gain_ref[...]).astype(BF16)
        part = dot(gp_ref[:, at], normed)
        if j == 0:
            acc_ref[:wide, :] = part
        else:
            acc_ref[:wide, :] += part
    acc_ref[wide:, :] = sum(t.ref[...].astype(F32) for t in terms)
    cut_columns(scalars, orders, acc_ref, 0, outs, lanes)
    for out in outs:
        out.send()
    gain = 0.0
    for row in range(0, wide, 64):
        at = slice(row, row + 64)
        gain = gain + jnp.sum(acc_ref[at, :] * w_in.ref[at, :].astype(F32), axis=0, keepdims=True)
    gain = gain / gain_ref[...]
    both = [gain, gain_two_ref[...]]
    pieces = [g[:, c : c + 128] for g in both for c in range(0, gain.shape[1], 128)]
    gains.ref[...] = jnp.concatenate(pieces, axis=0)


def gain_rows(gains):
    high = gains.astype(BF16)
    return high, (gains - high.astype(F32)).astype(BF16)


def scatter_body(halves, scalars, near, ins, outs):
    first, second = ins[: halves[0]], ins[halves[0] : sum(halves)]
    gains_in = ins[sum(halves) :]
    rows = second[0].buffer.shape[1]
    count = second[0].buffer.shape[0]
    if gains_in:
        outs, gains_out = outs[:2], outs[2:]
        gains = gains_in[0].ref[...]
        last = first[-1].ref
        if last.shape[1] > rows:
            gains = gains + sum(
                last[i, row : row + 16, :].astype(F32)
                for i in range(last.shape[0])
                for row in range(rows, last.shape[1], 16)
            )
        each = gains.shape[0] // len(gains_out)
        for i, out in enumerate(gains_out):
            out.ref[...] = gains[i * each : (i + 1) * each]

    def total(terms, i, low, high):
        return sum(
            t.ref[i + t.buffer.shape[0] - count, low:high, :].astype(F32) for t in terms
        )

    if len(first) == 4:
        top, rest = outs
        cut = 2 * rows - rest.ref.shape[0]
        top_rows = [(first, 0, rows, 0), (second, 0, cut - rows, rows)]
        if len(top.ref.shape) == 3:
            wide = top.ref.shape[2]
            for terms, low, high, base in top_rows:
                for row in range(low, high, wide):
                    top.ref[(base + row) // wide] = total(terms, 0, row, row + wide).T
        else:
            for terms, low, high, base in top_rows:
                top.ref[base + low : base + high, :] = total(terms, 0, low, high)
        rest.ref[...] = total(second, 0, cut - rows, rows)
        return
    if gains_in:
        extra = outs[0].ref.shape[1] - rows
        for i, part in enumerate(gain_rows(gains)):
            row = rows if extra == 16 else rows + 16 * i
            outs[0].ref[i if extra == 16 else 0, row : row + 16, :] = part
    for terms, out in zip((first, second), outs):
        for i in range(count):
            out.ref[i, :rows, :] = total(terms, i, 0, rows).astype(BF16)
        out.send()


def scatter_start(parts, size, orders):
    return [
        [parts[2 * i], swap(parts[2 * i + 1], "dp", size, bits[0])] for i, bits in enumerate(orders)
    ]


def scatter_terms(held, first, last, gains):
    terms = []
    for half, parts in enumerate(held):
        for i, part in enumerate(parts):
            all_of_it = gains and half == 0 and i == len(parts) - 1 and i > 1
            terms.append((part, 1, 0 if all_of_it else first, last))
    return terms + gains


def scatter_kernel(held, gains, after=()):
    steps = len(held[0])
    rows, lanes = held[1][0].shape[1:]
    half = held[0][0].shape[0] >> (steps - 1)
    extra = 32 // half if gains else 0
    return far_call(
        functools.partial(scatter_body, [len(h) for h in held]),
        "scatter",
        [],
        [],
        scatter_terms(held, half, 2 * half, gains),
        [(shape((half, rows + extra, lanes), BF16), 1), (shape((half, rows, lanes), BF16), 1)]
        + [(shape(g.shape, F32), 1) for g in gains],
        after=after,
    )


def scatter_swap(held, sent, size, orders):
    return [
        [*parts, swap(out, "dp", size, bits[len(parts) - 1])]
        for parts, out, bits in zip(held, sent, orders)
    ]


def scatter_end(held, gains, cut, after=()):
    rows, lanes = held[1][0].shape[1:]
    return far_call(
        functools.partial(scatter_body, [len(h) for h in held]),
        "collect",
        [],
        [],
        scatter_terms(held, 0, 1, gains),
        [(shape((3, lanes, cut // 3) if gains else (cut, lanes), F32), 1)]
        + [(shape((2 * rows - cut, lanes), F32), 1)]
        + [(shape((g.shape[0] // 2, *g.shape[1:]), F32), 1) for g in gains for _ in range(2)],
        after=after,
    )


def layer_out_body(tile, scalars, near, ins, outs):
    for row in range(0, ins[0].buffer.shape[0], tile):
        at = slice(row, row + tile)
        outs[0].ref[at, :] = sum(t.tile(row, tile).astype(F32) for t in ins).astype(BF16)
        outs[0].send(at)


def first_grad_body(scalars, near, ins, outs):
    width = outs[0].ref.shape[1] // len(ins)
    for j, dv in enumerate(ins):
        at = pl.ds(pl.multiple_of((scalars[0][0] ^ j) * width, 128), width)
        outs[0].ref[:, at] = dv.ref[
            :, own_half(dv.buffer.shape[1], width, j)
        ].astype(F32)


def input_back_body(tile, scalars, near, ins, outs):
    (gain_ref,) = near
    x_in, gmid_in, *terms = ins
    for row in range(0, x_in.buffer.shape[0], tile):
        at = slice(row, row + tile)
        stream = x_in.tile(row, tile).astype(F32)
        scale = row_scale(stream)
        normed = stream * scale
        scaled = sum(t.tile(row, tile).astype(F32) for t in terms) * gain_ref[...]
        back = scale * (scaled - normed * jnp.mean(scaled * normed, axis=-1, keepdims=True))
        outs[0].ref[at, :] = gmid_in.tile(row, tile) + back
        outs[0].send(at)


def doc_tables(lengths):
    index = jnp.arange(SEQ, dtype=jnp.int32)
    ends = jnp.cumsum(lengths)
    begins = ends - lengths
    starts = jnp.max(jnp.where(begins[:, None] <= index[None, :], begins[:, None], 0), axis=0)
    inverse = jnp.exp(jnp.arange(HALF, dtype=F32) * (-2.0 * math.log(10000.0) / HEAD_DIM))
    angles = (index - starts).astype(F32)[None, :] * inverse[:, None]
    return starts[None, :], jnp.cos(angles), jnp.sin(angles)


def local(
    n,
    n_dp,
    hidden_in,
    first_values,
    doc_lengths,
    out_grad,
    qkv_weight,
    out_weight,
    gate_up_weight,
    down_weight,
    attn_gain,
    mlp_gain,
):
    shard, width = hidden_in.shape[1], qkv_weight.shape[2]
    hidden = down_weight.shape[0]
    lanes = qkv_weight.shape[0]
    dim = hidden_in.shape[2]
    tile = min(256, shard)
    me = lax.axis_index("head").reshape(1).astype(jnp.int32)
    dp = lax.axis_index("dp").reshape(1).astype(jnp.int32)
    x_own, og_own = hidden_in[0], out_grad[0]
    gain_one, gain_two = attn_gain[None, :], mlp_gain[None, :]

    per = shard // tile
    rows = jnp.concatenate(
        [qkv_weight.transpose(1, 2, 0).reshape(3 * width, lanes), out_weight], axis=0
    )
    mlp_rows = jnp.concatenate(
        [gate_up_weight.transpose(1, 2, 0).reshape(2 * hidden, lanes), down_weight], axis=0
    )
    fv_parts = [
        lax.dynamic_slice(first_values[0], (0, (me[0] ^ j) * width), (shard, width))
        for j in range(n)
    ]
    sources = ring_sources(dp[0], n_dp)
    line = n_dp // 2
    ringed = n == 4 and n_dp == 8 and lanes % 128 == 0
    if ringed:
        fv_near = swap(fv_parts[1], "head", n, 1)
        fv_far = swap(jnp.concatenate(fv_parts[2:], axis=1), "head", n, 2)
        parts = gather_columns(rows, n_dp)
        fv_far = gate(fv_far, [parts[line - 1]])
        xs = gather_relative(x_own, "head", n, lambda *x: [parts[line - 1]])
    else:
        parts = [lax.all_gather(rows, "dp", axis=1, tiled=True)]
        xs = gather_relative(x_own, "head", n)
        fvs = exchange_relative(fv_parts, "head", n)
        mlp_columns = [lax.all_gather(mlp_rows, "dp", axis=1, tiled=True)]
    starts, cos, sin = doc_tables(doc_lengths[0])

    def project(fvs, after=()):
        return far_call(
            functools.partial(project_body, n, tile),
            "project",
            [me, sources],
            [gain_one, cos, sin],
            [*parts, *xs, *fvs],
            [
                (shape((width, SEQ), BF16), n),
                (shape((SEQ, width), BF16), n),
                (shape((width, SEQ), BF16), n),
                (shape((SEQ, width), BF16), n),
                (shape((width, SEQ), BF16), n),
                (shape((3 * width, dim), BF16), 1),
                (shape((width, dim), BF16), 1),
            ],
            flops=6 * SEQ * dim * width,
            after=after,
        )

    if ringed:
        held = [gate(mlp_rows, [parts[line - 1], cos, sin, xs[1], fv_near, fv_far])]
        held.append(ring_step(held[0], n_dp))
        other = [swap(held[0], "dp", n_dp, 1)]
        og_near, og_far = swap(og_own, "head", n, 1), swap(og_own, "head", n, 2)
        fv_last = swap(fv_far[:, width:], "head", n, 1)
        projected = project([fv_parts[0], fv_near, fv_far, fv_last])
        w_near, far = swap(projected[-1], "head", n, 1), swap(projected[-1], "head", n, 2)
        held[1] = gate(held[1], [projected[0], other[0]])
        other.append(swap(held[1], "dp", n_dp, 1))
        held.append(ring_step(held[1], n_dp))
        early = [held[1]]
    else:
        projected = project(fvs)
    q_t, keys, k_t, values, v_t, w_qkv, w_out = projected
    look = functools.partial(attend, doc_lengths, me, q_t, keys, v_t, starts, shard)
    if ringed:
        ctx_own, ctx_near, ctx_far, o_t, lse = look([width, width, 2 * width], early)
        held[2] = gate(held[2], [ctx_own, other[1], far])
        other.append(swap(held[2], "dp", n_dp, 1))
        held.append(ring_step(held[2], n_dp))
        other.append(swap(held[3], "dp", n_dp, 1))
        ctxs = [ctx_own, *exchange_pair(ctx_near, ctx_far)]
        far = gate(far, [ctx_near])
        w_outs = [w_out, w_near, far, swap(far, "head", n, 1)]
        mlp_columns = held + other
    else:
        *ctx, o_t, lse = look([width] * n)
        w_outs = gather_relative(w_out, "head", n, lambda *w: [o_t])
        ctxs = exchange_relative(ctx, "head", n)

    if not ringed:
        ogs = gather_relative(og_own, "head", n)
    middle, normed_two, normed_near = far_call(
        functools.partial(join_body, n, tile),
        "join",
        [],
        [gain_two],
        [*[(a, per) for a in (*ctxs, x_own)], *w_outs],
        [(shape((shard, dim), F32), per)] + [(shape((shard, dim), BF16), per)] * 2,
        flops=2 * shard * dim * dim,
        after=[og_far, held[3], other[2]] if ringed else ogs[1:],
    )

    if ringed:
        og_far = gate(og_far, [normed_near])
        ogs = [og_own, og_near, og_far, swap(og_far, "head", n, 1)]
    half = n // 2
    groups = []

    def mlp(tokens, lo, weights):
        hiddens = [(shape((half * shard, hidden), BF16), half)] * 3
        made = [(shape((3 * hidden, dim), BF16), 1)] if len(weights) > 1 else []
        out = far_call(
            functools.partial(mlp_body, half, tile),
            "mlp",
            [sources],
            [],
            [*weights, *tokens, *ogs[lo : lo + half]],
            hiddens + [(shape((shard, dim), BF16), 1)] * half + made,
            flops=10 * half * shard * dim * hidden,
            lazy=[len(weights) + j + k for j in range(half - 1) for k in (0, half)],
        )
        groups.append(out)
        return [out[3]]

    if ringed:
        near = swap(gate(normed_near, other[3:]), "head", n, 1)
        pair = swap(normed_two, "head", n, 2)
        pair = gate(pair, mlp([normed_two, near], 0, mlp_columns))
        normed = [normed_two, near, pair, swap(pair, "head", n, 1)]
    else:
        normed = gather_relative(normed_two, "head", n)
        mlp(normed[:half], 0, mlp_columns)
    w_mlp = groups[0][-1] if ringed else mlp_columns[0]
    mlp(normed[half:], half, [w_mlp])
    gn_parts = [p for g in groups for p in g[3 : 3 + half]]
    if n == 4:
        gn_two, *gn_sent = sum_far(*sum_near(gn_parts))
    else:
        gn_two, gn_sent = sum_relative(gn_parts, "head", n)

    orders, grad_outs = None, lambda rows: [(shape((n_dp, rows, lanes), BF16), 3)]
    if ringed:
        bit_orders = [bits[::-1] for bits in column_orders(n_dp)]
        orders = [column_places(n_dp, bits) for bits in bit_orders]
        grad_outs = lambda rows: [(shape((n_dp // 2, rows // 2, lanes), BF16), 1)] * 4
    rest = far_call(
        functools.partial(mlp_rest_body, n, tile, orders),
        "mlp_rest",
        [dp],
        [],
        [(w_mlp, 1, 2 * hidden, 3 * hidden), groups[0][0], groups[1][0], *ogs]
        + [groups[0][1], groups[1][1], *normed, groups[0][2], groups[1][2]],
        [(shape((shard, dim), BF16), 1)] * n + grad_outs(3 * hidden),
        [pltpu.VMEM((hidden, dim), F32)],
        flops=8 * SEQ * dim * hidden,
        lazy=range(3, 7 + 2 * n),
        after=[*gn_sent, gn_two[1]],
    )
    mlp_parts, mlp_grads = rest[:n], rest[n:]
    layer_near = sum_near(mlp_parts) if n == 4 else ([mlp_parts[0]] * 2,) * 2
    if ringed:
        mlp_held = scatter_start(mlp_grads, n_dp, bit_orders)
    else:
        mlp_grads = lax.psum_scatter(mlp_grads[0], "dp", scatter_dimension=0, tiled=False)

    widths = [width, width, 2 * width] if n == 4 else [width] * n
    grad_middle, ga, gain_two_part, *gctx = far_call(
        functools.partial(middle_back_body, n, tile),
        "middle_back",
        [],
        [gain_two],
        [*[(a, per) for a in (middle, og_own, *gn_two)], *w_outs],
        [
            (shape((shard, dim), F32), per),
            (shape((shard, dim), BF16), per),
            (shape((1, dim), F32), 1),
        ]
        + [(shape((w, shard), BF16), per) for w in widths],
        flops=2 * shard * dim * dim,
        after=mlp_parts[:1],
    )
    if n == 4:
        dos = [gctx[0], *exchange_pair(*gctx[1:])]
    else:
        dos = exchange_relative(gctx, "head", n)
    layer_folded = [fold(layer_near[1], layer_near[0][1:])] if n == 4 else []
    out_parts = far_call(
        functools.partial(out_weight_body, n),
        "out_weight",
        [],
        [],
        [*ctxs, ga],
        [(shape((width, dim), BF16), 1)] * n,
        flops=2 * shard * dim * dim,
        after=layer_folded,
    )
    if n == 4:
        out_near = sum_near(out_parts, dos[2:3])
        layer_sent = gate(layer_folded[0], dos[2:3])
        layer_terms = [*layer_near[0], swap(layer_sent, "head", n, 2)]
        out_terms, out_sent = sum_far(*out_near, after=dos[2:3])
        sums_sent = [layer_sent, out_sent, out_terms[1]]
    else:
        layer_terms, _ = sum_relative(mlp_parts, "head", n)
        out_terms, sums_sent = sum_relative(out_parts, "head", n)
    first_sums, second_sums = [], []
    if ringed:
        first_sums = scatter_kernel(mlp_held, [], after=out_parts[:1])
        mlp_held = scatter_swap(mlp_held, first_sums, n_dp, bit_orders)
        second_sums = [h[-1] for h in mlp_held]
    gp_t, *dv = far_call(
        functools.partial(attend_back_body, n, min(256, shard)),
        "attend_back",
        [doc_lengths, me],
        [lse, starts, cos, sin],
        [*dos, o_t, q_t, keys, k_t, values],
        [(shape((3 * width, SEQ), BF16), 3)] + [(shape((shard, w), BF16), 1) for w in widths],
        [pltpu.VMEM((width, SEQ), F32)] * 3
        + [pltpu.VMEM((width, SEQ), BF16), pltpu.VMEM((width // HEAD_DIM, SEQ), F32)],
        flops=20 * SEQ * SEQ * width,
        after=[*sums_sent, *first_sums],
    )
    dvs = [dv[0], *exchange_pair(*dv[1:])] if n == 4 else exchange_relative(dv, "head", n)

    mlp_sent, third_sums = [], []
    if ringed:
        mlp_sent = scatter_kernel(mlp_held, [], after=[gp_t])
        mlp_held = scatter_swap(mlp_held, mlp_sent, n_dp, bit_orders)
        third_sums = [h[-1] for h in mlp_held]
    *grads, gains = far_call(
        functools.partial(qkv_weight_body, n, orders),
        "qkv_weight",
        [me, dp],
        [gain_one, gain_two_part],
        [gp_t, w_qkv, *xs, *out_terms],
        grad_outs(4 * width) + [(shape((2 * dim // 128, 128), F32), 1)],
        [pltpu.VMEM((4 * width, dim), F32)],
        after=[*layer_terms[1:], *mlp_sent],
        lazy=[1, *range(3, 2 + n + len(out_terms))],
    )
    if n == 4:
        gains_far = swap(gains, "head", n, 2)
        gains = gains + gains_far
    if ringed:
        held = scatter_start(grads, n_dp, bit_orders)
    gn_parts = far_call(
        functools.partial(unproject_body, n, tile),
        "unproject",
        [me],
        [],
        [w_qkv, gp_t],
        [(shape((shard, dim), BF16), 1)] * n,
        after=[*grads[:1], *third_sums, *dvs[1:3]],
    )
    first_grad = None

    def first_grad_of(after):
        return far_call(
            first_grad_body, "first_grad", [me], [], dvs, [(shape((shard, dim), F32), 1)], after=after
        )[0]

    if n == 4:
        gains = gate(gains, gn_parts[:1])
        gains = gains + swap(gains, "head", n, 1)
    else:
        gains = sum_all(gains, "head", n)
    def layer_out_of(after):
        return far_call(
            functools.partial(layer_out_body, tile),
            "layer_out",
            [],
            [],
            [(a, per) for a in (middle, *layer_terms)],
            [(shape((shard, dim), BF16), per)],
            after=after,
        )[0]

    def input_grad_of():
        return far_call(
            functools.partial(input_back_body, tile),
            "input_back",
            [],
            [gain_one],
            [(a, per) for a in (x_own, grad_middle, *gn_one)],
            [(shape((shard, dim), F32), per)],
        )[0]

    if ringed:
        layer_out = layer_out_of(gn_parts[:1])
        sent = scatter_kernel(held, [])
        gn_near = sum_near(gn_parts, [gains_far, layer_out, *[h[-1] for h in held]])
        gn_one, gn_sent = sum_far(*gn_near, fold_after=sent)
        held = scatter_swap(held, sent, n_dp, bit_orders)
        gains = gate(gains, [gn_sent, gn_one[1]])
        gains = gains + swap(gains, "dp", n_dp, bit_orders[0][0])
        first_grad = first_grad_of([gn_sent])
        mlp_gu, mlp_down = scatter_end(mlp_held, [], 2 * hidden, after=[gn_sent])
        gains = gate(gains, [first_grad, mlp_down])
        gains = gains + swap(gains, "dp", n_dp, bit_orders[0][1])
        input_grad = input_grad_of()
        *sent, gains = scatter_kernel(held, [gains])
        held = scatter_swap(held, sent, n_dp, bit_orders)
    else:
        gn_one, _ = sum_relative(gn_parts, "head", n)
        layer_out, input_grad = layer_out_of([]), input_grad_of()
        gains = sum_all(gains, "dp", n_dp)
        grads = lax.psum_scatter(grads[0], "dp", scatter_dimension=0, tiled=False).astype(F32)
        qkv_grad, out_grad_w = grads[: 3 * width], grads[3 * width :]
        mlp_grads = mlp_grads.astype(F32)
        mlp_gu, mlp_down = mlp_grads[: 2 * hidden], mlp_grads[2 * hidden :]
    if ringed:
        qkv_grad, out_grad_w, gain_one_grad, gain_two_grad = scatter_end(
            held, [gains], 3 * width, after=[input_grad]
        )
        qkv_grad = qkv_grad.transpose(1, 0, 2)
    else:
        qkv_grad = qkv_grad.reshape(3, width, lanes).transpose(2, 0, 1)
        gain_one_grad, gain_two_grad = gains.reshape(2, dim)
    if first_grad is None:
        stacked = jnp.stack(dvs)
        placed = [
            lax.dynamic_index_in_dim(stacked, me[0] ^ i, keepdims=False) for i in range(n)
        ]
        first_grad = jnp.concatenate(placed, axis=1).astype(F32)
    return (
        layer_out[None],
        input_grad[None],
        first_grad[None],
        qkv_grad,
        out_grad_w,
        mlp_gu.reshape(2, hidden, lanes).transpose(2, 0, 1),
        mlp_down,
        gain_one_grad.reshape(dim),
        gain_two_grad.reshape(dim),
    )


def solution(mesh):
    tokens = P("dp", "head", None)
    columns = P("dp", None, "head")
    rows = P("head", "dp")
    return jax.shard_map(
        functools.partial(local, mesh.shape["head"], mesh.shape["dp"]),
        mesh=mesh,
        in_specs=(tokens, tokens, P("dp", None), tokens, columns, rows, columns, rows, P(), P()),
        out_specs=(tokens, tokens, tokens, columns, rows, columns, rows, P(), P()),
        check_vma=False,
    )
```

```python
import functools
import math

import jax
import jax.numpy as jnp
from jax import lax
from jax.experimental import pallas as pl
from jax.experimental.pallas import tpu as pltpu
from jax.sharding import PartitionSpec as P

HEAD_DIM = 64
HALF = HEAD_DIM // 2
SEQ = 2048
NDOC = 16
NORM_EPS = 1e-06
NEG = -1e30
F32 = jnp.float32
BF16 = jnp.bfloat16
VMEM_LIMIT = 65280 << 10
SHORT, SMALL, MIDDLE, MOST, LONG = (
    pl.CostEstimate(flops=f << 30, bytes_accessed=1, transcendentals=0) for f in (0, 1, 3, 6, 12)
)
COSTS = {
    "project": MOST,
    **dict.fromkeys(("mlp", "mlp_rest", "middle_back"), LONG),
    **dict.fromkeys(("attend_back", "unproject", "qkv_weight"), LONG),
    **dict.fromkeys(("fold", "out_weight"), MIDDLE),
    **dict.fromkeys(("first_grad", "layer_out", "collect"), SMALL),
}

VMEM = pl.BlockSpec(memory_space=pltpu.VMEM)
SMEM = pl.BlockSpec(memory_space=pltpu.SMEM)


def shape(dims, dtype):
    return jax.ShapeDtypeStruct(dims, dtype)


def dot(a, b):
    return jnp.dot(a, b, preferred_element_type=F32)


def dot_nt(a, b):
    return lax.dot_general(a, b, (((1,), (1,)), ((), ())), preferred_element_type=F32)


def dot_tn(a, b):
    return lax.dot_general(a, b, (((0,), (0,)), ((), ())), preferred_element_type=F32)


class Fetched:
    def __init__(self, source, buffer, sems, pieces):
        self.buffer, self.waiting, self.begun = buffer, {}, set()
        self.rows = buffer.shape[0] // pieces
        for i in range(pieces):
            at = (pl.ds(i * self.rows, self.rows),) if pieces > 1 else ()
            src, dst = (source.at[at], buffer.at[at]) if at else (source, buffer)
            self.waiting[i] = pltpu.make_async_copy(src, dst, sems.at[i])

    def start(self, i):
        if i in self.waiting and i not in self.begun:
            self.begun.add(i)
            self.waiting[i].start()

    def begin(self):
        for i in list(self.waiting):
            self.start(i)

    def finish(self, i):
        self.start(i)
        self.waiting.pop(i).wait()

    def tile(self, first, rows):
        for i in list(self.waiting):
            if first < (i + 1) * self.rows and first + rows > i * self.rows:
                self.finish(i)
        return self.buffer[first : first + rows, :]

    @property
    def ref(self):
        for i in list(self.waiting):
            self.finish(i)
        return self.buffer


class Stored:
    def __init__(self, target, buffer, sems):
        self.target, self.ref, self.sems, self.copies = target, buffer, sems, []

    def send(self, *at):
        copy = pltpu.make_async_copy(
            self.ref.at[at], self.target.at[at], self.sems.at[len(self.copies)]
        )
        copy.start()
        self.copies.append(copy)


def far_call(body, name, scalars, near, ins, outs, scratch=(), flops=0, after=(), lazy=()):
    pieces = [i[1] if isinstance(i, tuple) else 1 for i in ins]
    spans = [i[2:] if isinstance(i, tuple) and len(i) > 2 else None for i in ins]
    ins = [i[0] if isinstance(i, tuple) else i for i in ins]
    held_in = [
        a if s is None else shape((s[1] - s[0], *a.shape[1:]), a.dtype) for a, s in zip(ins, spans)
    ]
    counts = [len(scalars), len(near), len(ins), len(after), len(outs)]
    held = [*held_in, *[o for o, _ in outs]]

    def kernel(*refs):
        groups = []
        for count in (*counts, len(ins), len(outs), len(outs), len(ins)):
            groups.append(refs[:count])
            refs = refs[count:]
        scalar_refs, near_refs, sources, _, targets, buffers, out_buffers, out_sems, sems = groups
        sources = [
            r if s is None else r.at[pl.ds(s[0], s[1] - s[0])] for r, s in zip(sources, spans)
        ]
        fetched = [Fetched(*f) for f in zip(sources, buffers, sems, pieces)]
        for i in range(max(pieces)):
            for k, f in enumerate(fetched):
                if k not in lazy:
                    f.start(i)
        stored = [Stored(*t) for t in zip(targets, out_buffers, out_sems)]
        body(scalar_refs, near_refs, fetched, stored, *refs)
        for out in stored:
            if not out.copies:
                out.send()
        for out in stored:
            for copy in out.copies:
                copy.wait()

    far = pl.BlockSpec(memory_space=pl.ANY)
    moved = sum(math.prod(a.shape) * jnp.dtype(a.dtype).itemsize for a in held)
    return pl.pallas_call(
        kernel,
        name=name,
        out_shape=[o for o, _ in outs],
        in_specs=[SMEM] * len(scalars) + [VMEM] * len(near) + [far] * (len(ins) + len(after)),
        out_specs=[far] * len(outs),
        scratch_shapes=[pltpu.VMEM(a.shape, a.dtype) for a in held]
        + [pltpu.SemaphoreType.DMA((pieces,)) for _, pieces in outs]
        + [pltpu.SemaphoreType.DMA((count,)) for count in pieces]
        + list(scratch),
        compiler_params=pltpu.CompilerParams(vmem_limit_bytes=VMEM_LIMIT),
        cost_estimate=COSTS.get(name, SHORT),
    )(*scalars, *near, *ins, *after)


def gate(value, after):
    if not after:
        return value
    return pl.pallas_call(
        lambda *refs: None,
        name="gate",
        out_shape=shape(value.shape, value.dtype),
        in_specs=[pl.BlockSpec(memory_space=pl.ANY)] * (1 + len(after)),
        out_specs=pl.BlockSpec(memory_space=pl.ANY),
        input_output_aliases={0: 0},
    )(value, *after)


def row_scale(stream):
    return lax.rsqrt(jnp.mean(stream * stream, axis=-1, keepdims=True) + NORM_EPS)


def swap(value, axis, size, bit):
    return lax.ppermute(value, axis, [(i, i ^ bit) for i in range(size)])


def bits_down(size):
    return [1 << b for b in reversed(range(size.bit_length() - 1))]


def gather_relative(value, axis, size, hold=None):
    parts = {0: value}
    for bit in bits_down(size):
        moved = {0: swap(value, axis, size, bit)}
        if bit == 1 and hold:
            after = hold(parts[0], moved[0])
            parts.update({j: gate(v, after) for j, v in parts.items() if j})
        moved.update({j: swap(v, axis, size, bit) for j, v in parts.items() if j})
        parts.update({j | bit: v for j, v in moved.items()})
    return [parts[j] for j in range(size)]


def fold_body(scalars, near, ins, outs):
    rows = outs[0].ref.shape[0]
    step = min(rows, 128)
    for row in range(0, rows, step):
        at = slice(row, row + step)
        outs[0].ref[at, :] = sum(t.tile(row, step).astype(F32) for t in ins).astype(BF16)
        outs[0].send(at)


def fold(terms, after=()):
    pieces = max(1, terms[0].shape[0] // 128)
    outs = [(shape(terms[0].shape, BF16), pieces)]
    return far_call(fold_body, "fold", [], [], [(t, pieces) for t in terms], outs, after=after)[0]


def sum_relative(parts, axis, size, after=(), first_after=(), fold_after=()):
    parts = dict(enumerate([[p] for p in parts]))
    bit, sent = 1, []
    while bit < size:
        kept = {}
        for j in sorted((j for j in parts if not j & bit), reverse=True):
            away = parts[j | bit]
            if len(away) > 1:
                away = gate(fold(away, fold_after), after)
                sent.append(away)
            else:
                away = gate(away[0], first_after)
            kept[j] = parts[j] + [swap(away, axis, size, bit)]
        parts = kept
        bit *= 2
    return parts[0], sent


def sum_near(parts, after=()):
    third = swap(gate(parts[3], after), "head", 4, 1)
    return [parts[0], swap(parts[1], "head", 4, 1)], [parts[2], third]


def sum_far(terms, away, after=(), fold_after=()):
    sent = gate(fold(away, fold_after), after)
    return [*terms, swap(sent, "head", 4, 2)], sent


def exchange_relative(parts, axis, size):
    return [p if j == 0 else swap(p, axis, size, j) for j, p in enumerate(parts)]


def exchange_pair(near, pair):
    pair = swap(pair, "head", 4, 2)
    return [swap(near, "head", 4, 1), pair, swap(pair, "head", 4, 1)]


def own_half(size, width, j):
    first = width if size == 2 * width and j == 3 else 0
    return slice(first, first + width)


def sum_all(value, axis, size):
    return sum((swap(value, axis, size, j) for j in range(1, size)), value)


def column_orders(size):
    bits = bits_down(size)
    return [bits, bits[-1:] + bits[:-1]]


def ring_sources(dp, size):
    line = size // 2
    place = dp // 2 ^ dp // 4
    held = [jnp.remainder(place - k, line) for k in range(line)]
    held = [2 * (p ^ p // 2) for p in held]
    return jnp.stack([h + (dp & 1) for h in held] + [h + 1 - (dp & 1) for h in held])


def ring_step(value, size):
    line = size // 2
    ring = [p ^ p // 2 for p in range(line)]
    pairs = [(2 * ring[p] + i, 2 * ring[(p + 1) % line] + i) for p in range(line) for i in range(2)]
    return lax.ppermute(value, "dp", pairs)


def gather_columns(rows, size):
    held, other = [rows], []
    for step in range(size // 2):
        if step:
            held[step] = gate(held[step], other[-1:])
        other.append(swap(held[step], "dp", size, 1))
        if step + 1 < size // 2:
            held.append(ring_step(held[step], size))
    return held + other


def column_places(size, bits):
    places = [0]
    for bit in reversed(bits):
        places = places + [j | bit for j in places]
    return places


def join_columns(from_ref, parts, outs):
    for i, part in enumerate(parts):
        part = part.ref
        lanes = part.shape[1]
        at = slice(None)
        if len(parts) > 1:
            at = pl.ds(pl.multiple_of(from_ref[i] * lanes, 128), lanes)
        for row, rows, out in outs:
            out[:, at] = part[row : row + rows, :]


def project_body(n, tile, scalars, near, ins, outs):
    me_ref, from_ref = scalars
    gain_ref, cos_ref, sin_ref = near
    count = len(ins) - 2 * n
    parts, xs, fvs = ins[:count], ins[count : count + n], ins[count + n :]
    q_out, k_out, kt_out, v_out, vt_out, w_out, wo_out = outs
    width = q_out.ref.shape[0]
    shard = xs[0].buffer.shape[0]
    w_ref = w_out.ref
    join_columns(from_ref, parts, [(0, 3 * width, w_ref), (3 * width, width, wo_out.ref)])
    w_out.send()
    wo_out.send()
    for j in range(n):
        x_ref, fv_ref = xs[j].ref, fvs[j].ref
        base = pl.multiple_of((me_ref[0] ^ j) * shard, shard)
        for t in range(0, shard, tile):
            at = pl.ds(pl.multiple_of(base + t, tile), tile)
            stream = x_ref[t : t + tile, :].astype(F32)
            normed = (stream * row_scale(stream) * gain_ref[...]).astype(BF16)
            qk = dot_nt(w_ref[: 2 * width, :], normed)
            cos, sin = cos_ref[:, at], sin_ref[:, at]
            turned = []
            for row in range(0, 2 * width, HEAD_DIM):
                first, second = qk[row : row + HALF], qk[row + HALF : row + HEAD_DIM]
                turned += [first * cos - second * sin, second * cos + first * sin]
            turned = jnp.concatenate(turned, axis=0)
            q_out.ref[:, at] = (turned[:width] * HEAD_DIM ** (-0.5)).astype(BF16)
            keys = turned[width:]
            kt_out.ref[:, at] = keys.astype(BF16)
            k_out.ref[at, :] = keys.T.astype(BF16)
            first_values = fv_ref[t : t + tile, :width].astype(F32)
            values = 0.5 * dot_nt(normed, w_ref[2 * width :, :]) + 0.5 * first_values
            v_out.ref[at, :] = values.astype(BF16)
            vt_out.ref[:, at] = values.T.astype(BF16)
        at = pl.ds(base, shard)
        for out in (q_out, kt_out, vt_out):
            out.send(slice(None), at)
        for out in (k_out, v_out):
            out.send(at, slice(None))


def doc_of(len_ref, token):
    run, first, last = jnp.int32(0), jnp.int32(0), jnp.int32(SEQ)
    for doc in range(NDOC):
        end = run + len_ref[0, doc]
        inside = (token >= run) & (token < end)
        first, last = jnp.where(inside, run, first), jnp.where(inside, end, last)
        run = end
    return first, last


def attend_kernel(
    bq, per, heads, skip, len_ref, me_ref, q_ref, k_ref, vt_ref, start_ref, *refs
):
    *ctx_refs, ot_ref, lse_ref, s_ref = refs[skip:]
    bk = bq
    step = pl.program_id(0)
    block = (step // per ^ me_ref[0]) * per + step % per
    first, _ = doc_of(len_ref, block * bq)
    starts = start_ref[...]

    heads_rows = [slice(h * HEAD_DIM, (h + 1) * HEAD_DIM) for h in range(heads)]
    half = bq // 2 if bq % 256 == 0 else bq
    halves = [(col, col + half, col + half) for col in range(0, bq, half)]

    def own_keys(count):
        return pl.ds(pl.multiple_of(block * bk, bk), count)

    def top_of(scores):
        return jnp.max(scores.reshape(scores.shape[0] // 8, 8, scores.shape[1]), axis=0)

    def score(kb, tops):
        at = pl.ds(pl.multiple_of(kb * bk, bk), bk)
        allowed = lax.broadcasted_iota(jnp.int32, (bk, bq), 0) + kb * bk >= starts
        out = []
        for h, rows in enumerate(heads_rows):
            scores = jnp.where(allowed, dot(k_ref[at, rows], q_ref[rows, :]), NEG)
            s_ref[h, at, :] = scores
            out.append(jnp.maximum(tops[h], top_of(scores)))
        return tuple(out)

    parts = [[] for _ in range(heads)]
    for low, high, count in halves:
        key_index = lax.broadcasted_iota(jnp.int32, (count, high - low), 0)
        allowed = key_index + block * bk >= starts[:, low:high]
        allowed &= key_index <= lax.broadcasted_iota(jnp.int32, (count, high - low), 1) + low
        for h, rows in enumerate(heads_rows):
            scores = dot(k_ref[own_keys(count), rows], q_ref[rows, low:high])
            scores = jnp.where(allowed, scores, NEG)
            s_ref[h, own_keys(count), low:high] = scores
            parts[h].append(top_of(scores))
    tops = tuple(jnp.concatenate(p, axis=1) for p in parts)
    tops = lax.fori_loop(first // bk, block, score, tops)
    tops = [jnp.max(t, axis=0, keepdims=True) for t in tops]

    def weigh(h, at, cols):
        probs = jnp.exp(s_ref[h, at, cols] - tops[h][:, cols])
        total = jnp.sum(probs.reshape(probs.shape[0] // 8, 8, probs.shape[1]), axis=0)
        return total, dot(vt_ref[heads_rows[h], at], probs.astype(BF16))

    def gather(kb, carry):
        at = pl.ds(pl.multiple_of(kb * bk, bk), bk)
        out = []
        for h in range(heads):
            total, acc = weigh(h, at, slice(None))
            out.append((carry[h][0] + total, carry[h][1] + acc))
        return tuple(out)

    sums = []
    for h in range(heads):
        pairs = [weigh(h, own_keys(count), slice(low, high)) for low, high, count in halves]
        sums.append(tuple(jnp.concatenate(p, axis=1) for p in zip(*pairs)))
    sums = lax.fori_loop(first // bk, block, gather, tuple(sums))
    outs = []
    for h in range(heads):
        total = jnp.sum(sums[h][0], axis=0, keepdims=True)
        outs.append(sums[h][1] * (1.0 / total))
        lse_ref[h : h + 1, :] = tops[h] + jnp.log(total)
    out = jnp.concatenate(outs, axis=0)
    ot_ref[...] = out.astype(BF16)
    out = out.T.astype(BF16)
    width = out.shape[1]
    places = [(ref, c) for ref in ctx_refs for c in range(0, ref.shape[1], width)]
    for j, (ref, col) in enumerate(places):

        @pl.when(step // per == j)
        def _(ref=ref, col=col):
            rows = pl.ds(pl.multiple_of((step % per) * bq, bq), bq)
            ref[rows, col : col + width] = out


def attend(lengths, me, q_t, keys, v_t, starts, shard, widths, after=()):
    width = q_t.shape[0]
    heads = width // HEAD_DIM
    bq = min(512, shard)
    per = shard // bq
    at = lambda i, l, m: (0, (i // per ^ m[0]) * per + i % per)
    whole = lambda i, l, m: (0, 0)
    spec = pltpu.PrefetchScalarGridSpec(
        num_scalar_prefetch=2,
        grid=(SEQ // bq,),
        in_specs=[
            pl.BlockSpec((width, bq), at),
            pl.BlockSpec((SEQ, width), whole),
            pl.BlockSpec((width, SEQ), whole),
            pl.BlockSpec((1, bq), at),
        ]
        + [pl.BlockSpec(memory_space=pl.ANY)] * len(after),
        out_specs=[
            *[pl.BlockSpec((shard, w), whole) for w in widths],
            pl.BlockSpec((width, bq), at),
            pl.BlockSpec((heads, bq), at),
        ],
        scratch_shapes=[pltpu.VMEM((heads, SEQ, bq), F32)],
    )
    return pl.pallas_call(
        functools.partial(attend_kernel, bq, per, heads, len(after)),
        name="attend",
        grid_spec=spec,
        out_shape=[
            *[shape((shard, w), BF16) for w in widths],
            shape((width, SEQ), BF16),
            shape((heads, SEQ), F32),
        ],
        compiler_params=pltpu.CompilerParams(vmem_limit_bytes=VMEM_LIMIT),
        cost_estimate=MOST,
    )(lengths, me, q_t, keys, v_t, starts, *after)


def attend_back_body(n, block, scalars, near, ins, outs, *scratch):
    len_ref, me_ref = scalars
    lse_ref, start_ref, cos_ref, sin_ref = near
    dos, (ot_in, *rest) = ins[:n], ins[n:]
    gp_out, *firsts = outs
    out_ref = gp_out.ref
    dq_ref, dk_ref, dv_ref, do_ref, delta_ref = scratch
    width = dq_ref.shape[0]
    heads = width // HEAD_DIM
    shard = SEQ // n
    ot_ref = ot_in.ref
    for j in range(n):
        at = pl.ds(pl.multiple_of((me_ref[0] ^ j) * shard, shard), shard)
        grad = dos[j].ref[own_half(dos[j].buffer.shape[0], width, j), :]
        do_ref[:, at] = grad
        product = grad.astype(F32) * ot_ref[:, at].astype(F32)
        for h in range(heads):
            delta_ref[h : h + 1, at] = jnp.sum(
                product[h * HEAD_DIM : (h + 1) * HEAD_DIM], axis=0, keepdims=True
            )
    dq_ref[...] = jnp.zeros_like(dq_ref)
    dk_ref[...] = jnp.zeros_like(dk_ref)
    dv_ref[...] = jnp.zeros_like(dv_ref)
    q_ref, k_ref, kt_ref, v_ref = (r.ref for r in rest)

    def pair(kb, qb, diagonal):
        k_at = pl.ds(pl.multiple_of(kb * block, block), block)
        q_at = pl.ds(pl.multiple_of(qb * block, block), block)
        key_index = lax.broadcasted_iota(jnp.int32, (block, block), 0) + kb * block
        allowed = key_index >= start_ref[:, q_at]
        if diagonal:
            allowed &= key_index <= lax.broadcasted_iota(jnp.int32, (block, block), 1) + qb * block
        every = range(heads)
        rows = [slice(h * HEAD_DIM, (h + 1) * HEAD_DIM) for h in every]
        q_t = [q_ref[r, q_at] for r in rows]
        do_t = [do_ref[r, q_at] for r in rows]
        scores = [dot(k_ref[k_at, r], q_t[h]) for h, r in enumerate(rows)]
        dprobs = [dot(v_ref[k_at, r], do_t[h]) for h, r in enumerate(rows)]
        probs = [
            jnp.exp(jnp.where(allowed, scores[h], NEG) - lse_ref[h : h + 1, q_at]) for h in every
        ]
        dscores = [
            (probs[h] * (dprobs[h] - delta_ref[h : h + 1, q_at])).astype(BF16) for h in every
        ]
        probs = [p.astype(BF16) for p in probs]
        dv = [dot_nt(do_t[h], probs[h]) for h in every]
        dk = [dot_nt(q_t[h], dscores[h]) for h in every]
        dq = [dot(kt_ref[rows[h], k_at], dscores[h]) for h in every]
        for h in every:
            dv_ref[rows[h], k_at] += dv[h]
            dk_ref[rows[h], k_at] += dk[h]
            dq_ref[rows[h], q_at] += dq[h]

    def outer(kb, carry):
        _, end = doc_of(len_ref, kb * block + block - 1)
        pair(kb, kb, True)

        def inner(qb, c):
            pair(kb, qb, False)
            return c

        lax.fori_loop(kb + 1, (end - 1) // block + 1, inner, 0)
        return carry

    lax.fori_loop(0, SEQ // block, outer, 0)
    for j in range(n):
        at = pl.ds(pl.multiple_of((me_ref[0] ^ j) * shard, shard), shard)
        grad = 0.5 * dv_ref[:, at]
        out_ref[2 * width :, at] = grad.astype(BF16)
        first = firsts[j] if len(firsts) == n else firsts[min(j, 2)]
        cols = slice(width, 2 * width) if len(firsts) != n and j == 3 else slice(0, width)
        first.ref[:, cols] = grad.T.astype(BF16)
    for first in firsts:
        first.send()
    gp_out.send(slice(2 * width, 3 * width))
    cos, sin = cos_ref[...], sin_ref[...]
    for base, ref, scale in ((0, dq_ref, HEAD_DIM ** (-0.5)), (width, dk_ref, 1.0)):
        for row in range(0, width, HEAD_DIM):
            first = ref[row : row + HALF, :] * scale
            second = ref[row + HALF : row + HEAD_DIM, :] * scale
            out_ref[base + row : base + row + HALF, :] = (first * cos + second * sin).astype(BF16)
            out_ref[base + row + HALF : base + row + HEAD_DIM, :] = (
                second * cos - first * sin
            ).astype(BF16)
        gp_out.send(slice(base, base + width))


def join_body(n, tile, scalars, near, ins, outs):
    (gain_ref,) = near
    ctx, x_in, w_out = ins[:n], ins[n], ins[n + 1 :]
    mid, *normeds = outs
    for row in range(0, x_in.buffer.shape[0], tile):
        at = slice(row, row + tile)
        total = x_in.tile(row, tile).astype(F32)
        for j, (c, w) in enumerate(zip(ctx, w_out)):
            cols = own_half(c.buffer.shape[1], w.buffer.shape[0], j)
            total = total + dot(c.tile(row, tile)[:, cols], w.ref[...])
        rows = (total * row_scale(total) * gain_ref[...]).astype(BF16)
        for normed in normeds:
            normed.ref[at, :] = rows
            normed.send(at)
        mid.ref[at, :] = total
        mid.send(at)


def mlp_body(n, tile, scalars, near, ins, outs):
    (from_ref,) = scalars
    count = len(ins) - 2 * n
    parts, normed, grads = ins[:count], ins[count : count + n], ins[count + n :]
    mixed, dgate_out, dup_out, *gns = outs
    hidden = mixed.ref.shape[1]
    shard = normed[0].buffer.shape[0]
    if count > 1:
        *gns, made = gns
        w_ref = made.ref
        join_columns(from_ref, parts, [(0, 3 * hidden, w_ref)])
        made.send()
    else:
        w_ref = parts[0].ref
    w_gate, w_up, w_down = (w_ref.at[i * hidden : (i + 1) * hidden, :] for i in range(3))
    for j in reversed(range(n)):
        tokens_ref, og_ref = normed[j].ref, grads[j].ref
        for later in (*normed[:j][-1:], *grads[:j][-1:]):
            later.begin()

        def step(t, carry, tokens_ref=tokens_ref, og_ref=og_ref, j=j):
            rows = pl.ds(pl.multiple_of(t * tile, tile), tile)
            at = pl.ds(pl.multiple_of(j * shard + t * tile, tile), tile)
            tokens = tokens_ref[rows, :]
            gate = dot_nt(tokens, w_gate[...])
            up = dot_nt(tokens, w_up[...])
            gm = dot_nt(og_ref[rows, :], w_down[...])
            sig = 1.0 / (1.0 + jnp.exp(-gate))
            act = gate * sig
            mixed.ref[at, :] = (act * up).astype(BF16)
            dup = (gm * act).astype(BF16)
            dgate = (gm * up * sig * (1.0 + gate * (1.0 - sig))).astype(BF16)
            dup_out.ref[at, :] = dup
            dgate_out.ref[at, :] = dgate
            gns[j].ref[rows, :] = (dot(dgate, w_gate[...]) + dot(dup, w_up[...])).astype(BF16)
            return carry

        lax.fori_loop(0, shard // tile, step, 0)
        gns[j].send()
        for out in (mixed, dgate_out, dup_out):
            out.send(slice(j * shard, (j + 1) * shard))


def mlp_rest_body(n, tile, orders, scalars, near, ins, outs, acc_ref):
    w_in, mixeds, ogs = ins[0], ins[1:3], ins[3 : 3 + n]
    dgates, normed, dups = ins[3 + n : 5 + n], ins[5 + n : 5 + 2 * n], ins[5 + 2 * n :]
    parts, grads = outs[:n], outs[n:]
    half = n // 2
    hidden = acc_ref.shape[0]
    lanes = grads[0].ref.shape[2]
    shard = normed[0].buffer.shape[0]
    w_down = w_in.ref
    for load in (*mixeds, *dgates, *normed):
        load.begin()
    for j in reversed(range(n)):
        mixed_ref = mixeds[j // half].ref
        for t in range(0, shard, tile):
            rows = mixed_ref[j % half * shard + t : j % half * shard + t + tile, :]
            parts[j].ref[t : t + tile, :] = dot(rows, w_down[...]).astype(BF16)
        parts[j].send()
    for which, (lefts, rights) in ((0, (dgates, normed)), (1, (dups, normed)), (2, (mixeds, ogs))):
        for load in (*dups, *ogs) if which == 0 else ():
            load.begin()
        for j in range(n):
            left = lefts[j // half].ref[j % half * shard : (j % half + 1) * shard, :]
            part = dot_tn(left, rights[j].ref[...])
            if j == 0:
                acc_ref[...] = part
            else:
                acc_ref[...] += part
        cut_columns(scalars, orders, acc_ref, which * hidden, grads, lanes)


def cut_columns(scalars, orders, acc_ref, first, outs, lanes):
    count = acc_ref.shape[0]
    if orders is None:
        for i in range(outs[0].ref.shape[0]):
            outs[0].ref[i, first : first + count, :] = acc_ref[
                :, i * lanes : (i + 1) * lanes
            ].astype(BF16)
        return
    rows = outs[0].ref.shape[1]
    for half, places in enumerate(orders):
        low, high = max(first, half * rows), min(first + count, (half + 1) * rows)
        if low >= high:
            continue
        to = slice(low - half * rows, high - half * rows)
        for i, j in reversed(list(enumerate(places))):
            at = pl.ds(pl.multiple_of((scalars[-1][0] ^ j) * lanes, 128), lanes)
            out = outs[2 * half + i // (len(places) // 2)]
            out.ref[i % (len(places) // 2), to, :] = acc_ref[low - first : high - first, at].astype(
                BF16
            )


def middle_back_body(n, tile, scalars, near, ins, outs):
    (gain_ref,) = near
    mid_in, og_in, *terms = ins[:-n]
    w_out = ins[-n:]
    gmid_out, ga_out, gain_out, *gctx = outs
    for row in range(0, mid_in.buffer.shape[0], tile):
        at = slice(row, row + tile)
        mid = mid_in.tile(row, tile)
        grad = sum(t.tile(row, tile).astype(F32) for t in terms)
        scale = row_scale(mid)
        normed = mid * scale
        scaled = grad * gain_ref[...]
        back = scale * (scaled - normed * jnp.mean(scaled * normed, axis=-1, keepdims=True))
        total = jnp.sum(grad * normed, axis=0, keepdims=True)
        gain_out.ref[...] = total if row == 0 else gain_out.ref[...] + total
        gmid = og_in.tile(row, tile).astype(F32) + back
        ga = gmid.astype(BF16)
        for j, w in reversed(list(enumerate(w_out))):
            wide = w.buffer.shape[0]
            out, first = (gctx[j], 0) if len(gctx) == n else (gctx[min(j, 2)], wide * (j == 3))
            out.ref[first : first + wide, at] = dot_nt(w.ref[...], ga).astype(BF16)
            if first == 0:
                out.send(slice(None), at)
        ga_out.ref[at, :] = ga
        ga_out.send(at)
        gmid_out.ref[at, :] = gmid
        gmid_out.send(at)


def out_weight_body(n, scalars, near, ins, outs):
    *ctx, ga = ins
    for j, (c, out) in reversed(list(enumerate(zip(ctx, outs)))):
        cols = own_half(c.buffer.shape[1], out.ref.shape[0], j)
        out.ref[...] = dot_tn(c.ref[:, cols], ga.ref[...]).astype(BF16)
        out.send()


def unproject_body(n, tile, scalars, near, ins, outs):
    (me_ref,) = scalars
    w_ref, gp_ref = (i.ref for i in ins)
    shard = outs[0].ref.shape[0]
    for j in reversed(range(n)):
        base = (me_ref[0] ^ j) * shard
        for t in range(0, shard, tile):
            at = pl.ds(pl.multiple_of(base + t, tile), tile)
            outs[j].ref[t : t + tile, :] = dot_tn(gp_ref[:, at], w_ref[...]).astype(BF16)
        outs[j].send()


def qkv_weight_body(n, orders, scalars, near, ins, outs, acc_ref):
    me_ref, dp_ref = scalars
    gain_ref, gain_two_ref = near
    gp_in, w_in, xs, terms = ins[0], ins[1], ins[2 : 2 + n], ins[2 + n :]
    *outs, gains = outs
    shard = xs[0].buffer.shape[0]
    lanes = outs[0].ref.shape[2]
    gp_ref = gp_in.ref
    wide = gp_ref.shape[0]
    for j in range(n):
        at = pl.ds(pl.multiple_of((me_ref[0] ^ j) * shard, shard), shard)
        x_ref = xs[j].ref
        for later in xs[j + 1 : j + 2] if j + 1 < n else (w_in, *terms):
            later.begin()
        stream = x_ref[...].astype(F32)
        normed = (stream * row_scale(stream) * gain_ref[...]).astype(BF16)
        part = dot(gp_ref[:, at], normed)
        if j == 0:
            acc_ref[:wide, :] = part
        else:
            acc_ref[:wide, :] += part
    acc_ref[wide:, :] = sum(t.ref[...].astype(F32) for t in terms)
    cut_columns(scalars, orders, acc_ref, 0, outs, lanes)
    for out in outs:
        out.send()
    gain = 0.0
    for row in range(0, wide, 64):
        at = slice(row, row + 64)
        gain = gain + jnp.sum(acc_ref[at, :] * w_in.ref[at, :].astype(F32), axis=0, keepdims=True)
    gain = gain / gain_ref[...]
    both = [gain, gain_two_ref[...]]
    pieces = [g[:, c : c + 128] for g in both for c in range(0, gain.shape[1], 128)]
    gains.ref[...] = jnp.concatenate(pieces, axis=0)


def gain_rows(gains):
    high = gains.astype(BF16)
    return high, (gains - high.astype(F32)).astype(BF16)


def scatter_body(halves, scalars, near, ins, outs):
    first, second = ins[: halves[0]], ins[halves[0] : sum(halves)]
    gains_in = ins[sum(halves) :]
    rows = second[0].buffer.shape[1]
    count = second[0].buffer.shape[0]
    if gains_in:
        outs, gains_out = outs[:2], outs[2:]
        gains = gains_in[0].ref[...]
        last = first[-1].ref
        if last.shape[1] > rows:
            gains = gains + sum(
                last[i, row : row + 16, :].astype(F32)
                for i in range(last.shape[0])
                for row in range(rows, last.shape[1], 16)
            )
        each = gains.shape[0] // len(gains_out)
        for i, out in enumerate(gains_out):
            out.ref[...] = gains[i * each : (i + 1) * each]

    def total(terms, i, low, high):
        return sum(
            t.ref[i + t.buffer.shape[0] - count, low:high, :].astype(F32) for t in terms
        )

    if len(first) == 4:
        top, rest = outs
        cut = 2 * rows - rest.ref.shape[0]
        top_rows = [(first, 0, rows, 0), (second, 0, cut - rows, rows)]
        if len(top.ref.shape) == 3:
            wide = top.ref.shape[2]
            for terms, low, high, base in top_rows:
                for row in range(low, high, wide):
                    top.ref[(base + row) // wide] = total(terms, 0, row, row + wide).T
        else:
            for terms, low, high, base in top_rows:
                top.ref[base + low : base + high, :] = total(terms, 0, low, high)
        rest.ref[...] = total(second, 0, cut - rows, rows)
        return
    if gains_in:
        extra = outs[0].ref.shape[1] - rows
        for i, part in enumerate(gain_rows(gains)):
            row = rows if extra == 16 else rows + 16 * i
            outs[0].ref[i if extra == 16 else 0, row : row + 16, :] = part
    for terms, out in zip((first, second), outs):
        for i in range(count):
            out.ref[i, :rows, :] = total(terms, i, 0, rows).astype(BF16)
        out.send()


def scatter_start(parts, size, orders):
    return [
        [parts[2 * i], swap(parts[2 * i + 1], "dp", size, bits[0])] for i, bits in enumerate(orders)
    ]


def scatter_terms(held, first, last, gains):
    terms = []
    for half, parts in enumerate(held):
        for i, part in enumerate(parts):
            all_of_it = gains and half == 0 and i == len(parts) - 1 and i > 1
            terms.append((part, 1, 0 if all_of_it else first, last))
    return terms + gains


def scatter_kernel(held, gains, after=()):
    steps = len(held[0])
    rows, lanes = held[1][0].shape[1:]
    half = held[0][0].shape[0] >> (steps - 1)
    extra = 32 // half if gains else 0
    return far_call(
        functools.partial(scatter_body, [len(h) for h in held]),
        "scatter",
        [],
        [],
        scatter_terms(held, half, 2 * half, gains),
        [(shape((half, rows + extra, lanes), BF16), 1), (shape((half, rows, lanes), BF16), 1)]
        + [(shape(g.shape, F32), 1) for g in gains],
        after=after,
    )


def fold_and_scatter_body(halves, scalars, near, ins, outs):
    fold_body(scalars, near, ins[:2], outs[:1])
    scatter_body(halves, scalars, near, ins[2:], outs[1:])


def fold_and_scatter(terms, held, after=()):
    rows, lanes = held[1][0].shape[1:]
    half = held[0][0].shape[0] >> (len(held[0]) - 1)
    pieces = terms[0].shape[0] // 128
    folded, *sent = far_call(
        functools.partial(fold_and_scatter_body, [len(h) for h in held]),
        "scatter",
        [],
        [],
        [(t, pieces) for t in terms] + scatter_terms(held, half, 2 * half, []),
        [(shape(terms[0].shape, BF16), pieces)] + [(shape((half, rows, lanes), BF16), 1)] * 2,
        after=after,
    )
    return folded, sent


def scatter_swap(held, sent, size, orders):
    return [
        [*parts, swap(out, "dp", size, bits[len(parts) - 1])]
        for parts, out, bits in zip(held, sent, orders)
    ]


def scatter_end(held, gains, cut, after=()):
    rows, lanes = held[1][0].shape[1:]
    return far_call(
        functools.partial(scatter_body, [len(h) for h in held]),
        "collect",
        [],
        [],
        scatter_terms(held, 0, 1, gains),
        [(shape((3, lanes, cut // 3) if gains else (cut, lanes), F32), 1)]
        + [(shape((2 * rows - cut, lanes), F32), 1)]
        + [(shape((g.shape[0] // 2, *g.shape[1:]), F32), 1) for g in gains for _ in range(2)],
        after=after,
    )


def layer_out_body(tile, scalars, near, ins, outs):
    for row in range(0, ins[0].buffer.shape[0], tile):
        at = slice(row, row + tile)
        outs[0].ref[at, :] = sum(t.tile(row, tile).astype(F32) for t in ins).astype(BF16)
        outs[0].send(at)


def first_grad_body(scalars, near, ins, outs):
    width = outs[0].ref.shape[1] // len(ins)
    for j, dv in enumerate(ins):
        at = pl.ds(pl.multiple_of((scalars[0][0] ^ j) * width, 128), width)
        outs[0].ref[:, at] = dv.ref[
            :, own_half(dv.buffer.shape[1], width, j)
        ].astype(F32)


def input_back_body(tile, scalars, near, ins, outs):
    (gain_ref,) = near
    x_in, gmid_in, *terms = ins
    for row in range(0, x_in.buffer.shape[0], tile):
        at = slice(row, row + tile)
        stream = x_in.tile(row, tile).astype(F32)
        scale = row_scale(stream)
        normed = stream * scale
        scaled = sum(t.tile(row, tile).astype(F32) for t in terms) * gain_ref[...]
        back = scale * (scaled - normed * jnp.mean(scaled * normed, axis=-1, keepdims=True))
        outs[0].ref[at, :] = gmid_in.tile(row, tile) + back
        outs[0].send(at)


def doc_tables(lengths):
    index = jnp.arange(SEQ, dtype=jnp.int32)
    ends = jnp.cumsum(lengths)
    begins = ends - lengths
    starts = jnp.max(jnp.where(begins[:, None] <= index[None, :], begins[:, None], 0), axis=0)
    inverse = jnp.exp(jnp.arange(HALF, dtype=F32) * (-2.0 * math.log(10000.0) / HEAD_DIM))
    angles = (index - starts).astype(F32)[None, :] * inverse[:, None]
    return starts[None, :], jnp.cos(angles), jnp.sin(angles)


def local(
    n,
    n_dp,
    hidden_in,
    first_values,
    doc_lengths,
    out_grad,
    qkv_weight,
    out_weight,
    gate_up_weight,
    down_weight,
    attn_gain,
    mlp_gain,
):
    shard, width = hidden_in.shape[1], qkv_weight.shape[2]
    hidden = down_weight.shape[0]
    lanes = qkv_weight.shape[0]
    dim = hidden_in.shape[2]
    tile = min(256, shard)
    me = lax.axis_index("head").reshape(1).astype(jnp.int32)
    dp = lax.axis_index("dp").reshape(1).astype(jnp.int32)
    x_own, og_own = hidden_in[0], out_grad[0]
    gain_one, gain_two = attn_gain[None, :], mlp_gain[None, :]

    per = shard // tile
    rows = jnp.concatenate(
        [qkv_weight.transpose(1, 2, 0).reshape(3 * width, lanes), out_weight], axis=0
    )
    mlp_rows = jnp.concatenate(
        [gate_up_weight.transpose(1, 2, 0).reshape(2 * hidden, lanes), down_weight], axis=0
    )
    fv_parts = [
        lax.dynamic_slice(first_values[0], (0, (me[0] ^ j) * width), (shard, width))
        for j in range(n)
    ]
    sources = ring_sources(dp[0], n_dp)
    line = n_dp // 2
    ringed = n == 4 and n_dp == 8 and lanes % 128 == 0
    if ringed:
        fv_near = swap(fv_parts[1], "head", n, 1)
        fv_far = swap(jnp.concatenate(fv_parts[2:], axis=1), "head", n, 2)
        parts = gather_columns(rows, n_dp)
        fv_far = gate(fv_far, [parts[line - 1]])
        xs = gather_relative(x_own, "head", n, lambda *x: [parts[line - 1]])
    else:
        parts = [lax.all_gather(rows, "dp", axis=1, tiled=True)]
        xs = gather_relative(x_own, "head", n)
        fvs = exchange_relative(fv_parts, "head", n)
        mlp_columns = [lax.all_gather(mlp_rows, "dp", axis=1, tiled=True)]
    starts, cos, sin = doc_tables(doc_lengths[0])

    def project(fvs, after=()):
        return far_call(
            functools.partial(project_body, n, tile),
            "project",
            [me, sources],
            [gain_one, cos, sin],
            [*parts, *xs, *fvs],
            [
                (shape((width, SEQ), BF16), n),
                (shape((SEQ, width), BF16), n),
                (shape((width, SEQ), BF16), n),
                (shape((SEQ, width), BF16), n),
                (shape((width, SEQ), BF16), n),
                (shape((3 * width, dim), BF16), 1),
                (shape((width, dim), BF16), 1),
            ],
            flops=6 * SEQ * dim * width,
            after=after,
        )

    if ringed:
        held = [gate(mlp_rows, [parts[line - 1], cos, sin, xs[1], fv_near, fv_far])]
        held.append(ring_step(held[0], n_dp))
        other = [swap(held[0], "dp", n_dp, 1)]
        og_near, og_far = swap(og_own, "head", n, 1), swap(og_own, "head", n, 2)
        fv_last = swap(fv_far[:, width:], "head", n, 1)
        projected = project([fv_parts[0], fv_near, fv_far, fv_last])
        w_near, far = swap(projected[-1], "head", n, 1), swap(projected[-1], "head", n, 2)
        held[1] = gate(held[1], [projected[0], other[0]])
        other.append(swap(held[1], "dp", n_dp, 1))
        held.append(ring_step(held[1], n_dp))
        early = [held[1]]
    else:
        projected = project(fvs)
    q_t, keys, k_t, values, v_t, w_qkv, w_out = projected
    look = functools.partial(attend, doc_lengths, me, q_t, keys, v_t, starts, shard)
    if ringed:
        ctx_own, ctx_near, ctx_far, o_t, lse = look([width, width, 2 * width], early)
        held[2] = gate(held[2], [ctx_own, other[1], far])
        other.append(swap(held[2], "dp", n_dp, 1))
        held.append(ring_step(held[2], n_dp))
        other.append(swap(held[3], "dp", n_dp, 1))
        ctxs = [ctx_own, *exchange_pair(ctx_near, ctx_far)]
        far = gate(far, [ctx_near])
        w_outs = [w_out, w_near, far, swap(far, "head", n, 1)]
        mlp_columns = held + other
    else:
        *ctx, o_t, lse = look([width] * n)
        w_outs = gather_relative(w_out, "head", n, lambda *w: [o_t])
        ctxs = exchange_relative(ctx, "head", n)

    if not ringed:
        ogs = gather_relative(og_own, "head", n)
    middle, normed_two, normed_near = far_call(
        functools.partial(join_body, n, tile),
        "join",
        [],
        [gain_two],
        [*[(a, per) for a in (*ctxs, x_own)], *w_outs],
        [(shape((shard, dim), F32), per)] + [(shape((shard, dim), BF16), per)] * 2,
        flops=2 * shard * dim * dim,
        after=[og_far, held[3], other[2]] if ringed else ogs[1:],
    )

    if ringed:
        og_far = gate(og_far, [normed_near])
        ogs = [og_own, og_near, og_far, swap(og_far, "head", n, 1)]
    half = n // 2
    groups = []

    def mlp(tokens, lo, weights):
        hiddens = [(shape((half * shard, hidden), BF16), half)] * 3
        made = [(shape((3 * hidden, dim), BF16), 1)] if len(weights) > 1 else []
        out = far_call(
            functools.partial(mlp_body, half, tile),
            "mlp",
            [sources],
            [],
            [*weights, *tokens, *ogs[lo : lo + half]],
            hiddens + [(shape((shard, dim), BF16), 1)] * half + made,
            flops=10 * half * shard * dim * hidden,
            lazy=[len(weights) + j + k for j in range(half - 1) for k in (0, half)],
        )
        groups.append(out)
        return [out[3]]

    if ringed:
        near = swap(gate(normed_near, other[3:]), "head", n, 1)
        pair = swap(normed_two, "head", n, 2)
        pair = gate(pair, mlp([normed_two, near], 0, mlp_columns))
        normed = [normed_two, near, pair, swap(pair, "head", n, 1)]
    else:
        normed = gather_relative(normed_two, "head", n)
        mlp(normed[:half], 0, mlp_columns)
    w_mlp = groups[0][-1] if ringed else mlp_columns[0]
    mlp(normed[half:], half, [w_mlp])
    gn_parts = [p for g in groups for p in g[3 : 3 + half]]
    if n == 4:
        gn_two, *gn_sent = sum_far(*sum_near(gn_parts))
    else:
        gn_two, gn_sent = sum_relative(gn_parts, "head", n)

    orders, grad_outs = None, lambda rows: [(shape((n_dp, rows, lanes), BF16), 3)]
    if ringed:
        bit_orders = [bits[::-1] for bits in column_orders(n_dp)]
        orders = [column_places(n_dp, bits) for bits in bit_orders]
        grad_outs = lambda rows: [(shape((n_dp // 2, rows // 2, lanes), BF16), 1)] * 4
    rest = far_call(
        functools.partial(mlp_rest_body, n, tile, orders),
        "mlp_rest",
        [dp],
        [],
        [(w_mlp, 1, 2 * hidden, 3 * hidden), groups[0][0], groups[1][0], *ogs]
        + [groups[0][1], groups[1][1], *normed, groups[0][2], groups[1][2]],
        [(shape((shard, dim), BF16), 1)] * n + grad_outs(3 * hidden),
        [pltpu.VMEM((hidden, dim), F32)],
        flops=8 * SEQ * dim * hidden,
        lazy=range(3, 7 + 2 * n),
        after=[*gn_sent, gn_two[1]],
    )
    mlp_parts, mlp_grads = rest[:n], rest[n:]
    layer_near = sum_near(mlp_parts) if n == 4 else ([mlp_parts[0]] * 2,) * 2
    if ringed:
        mlp_held = scatter_start(mlp_grads, n_dp, bit_orders)
    else:
        mlp_grads = lax.psum_scatter(mlp_grads[0], "dp", scatter_dimension=0, tiled=False)

    widths = [width, width, 2 * width] if n == 4 else [width] * n
    grad_middle, ga, gain_two_part, *gctx = far_call(
        functools.partial(middle_back_body, n, tile),
        "middle_back",
        [],
        [gain_two],
        [*[(a, per) for a in (middle, og_own, *gn_two)], *w_outs],
        [
            (shape((shard, dim), F32), per),
            (shape((shard, dim), BF16), per),
            (shape((1, dim), F32), 1),
        ]
        + [(shape((w, shard), BF16), per) for w in widths],
        flops=2 * shard * dim * dim,
        after=mlp_parts[:1],
    )
    if n == 4:
        dos = [gctx[0], *exchange_pair(*gctx[1:])]
    else:
        dos = exchange_relative(gctx, "head", n)
    layer_folded = [fold(layer_near[1], layer_near[0][1:])] if n == 4 else []
    out_parts = far_call(
        functools.partial(out_weight_body, n),
        "out_weight",
        [],
        [],
        [*ctxs, ga],
        [(shape((width, dim), BF16), 1)] * n,
        flops=2 * shard * dim * dim,
        after=layer_folded,
    )
    first_sums = []
    if n == 4:
        out_near = sum_near(out_parts, dos[2:3])
        layer_sent = gate(layer_folded[0], dos[2:3])
        layer_terms = [*layer_near[0], swap(layer_sent, "head", n, 2)]
        if ringed:
            out_sent, first_sums = fold_and_scatter(out_near[1], mlp_held, out_near[0][1:])
            out_terms = [*out_near[0], swap(out_sent, "head", n, 2)]
        else:
            out_terms, out_sent = sum_far(*out_near, after=dos[2:3])
        sums_sent = [layer_sent, out_sent, out_terms[1]]
    else:
        layer_terms, _ = sum_relative(mlp_parts, "head", n)
        out_terms, sums_sent = sum_relative(out_parts, "head", n)
    second_sums = []
    if ringed:
        mlp_held = scatter_swap(mlp_held, first_sums, n_dp, bit_orders)
        second_sums = [h[-1] for h in mlp_held]
    gp_t, *dv = far_call(
        functools.partial(attend_back_body, n, min(256, shard)),
        "attend_back",
        [doc_lengths, me],
        [lse, starts, cos, sin],
        [*dos, o_t, q_t, keys, k_t, values],
        [(shape((3 * width, SEQ), BF16), 3)] + [(shape((shard, w), BF16), 1) for w in widths],
        [pltpu.VMEM((width, SEQ), F32)] * 3
        + [pltpu.VMEM((width, SEQ), BF16), pltpu.VMEM((width // HEAD_DIM, SEQ), F32)],
        flops=20 * SEQ * SEQ * width,
        after=[*sums_sent, *first_sums],
    )
    dvs = [dv[0], *exchange_pair(*dv[1:])] if n == 4 else exchange_relative(dv, "head", n)

    mlp_sent, third_sums = [], []
    if ringed:
        mlp_sent = scatter_kernel(mlp_held, [], after=[gp_t])
        mlp_held = scatter_swap(mlp_held, mlp_sent, n_dp, bit_orders)
        third_sums = [h[-1] for h in mlp_held]
    *grads, gains = far_call(
        functools.partial(qkv_weight_body, n, orders),
        "qkv_weight",
        [me, dp],
        [gain_one, gain_two_part],
        [gp_t, w_qkv, *xs, *out_terms],
        grad_outs(4 * width) + [(shape((2 * dim // 128, 128), F32), 1)],
        [pltpu.VMEM((4 * width, dim), F32)],
        after=[*layer_terms[1:], *mlp_sent],
        lazy=[1, *range(3, 2 + n + len(out_terms))],
    )
    if n == 4:
        gains_far = swap(gains, "head", n, 2)
        gains = gains + gains_far
    if ringed:
        held = scatter_start(grads, n_dp, bit_orders)
    gn_parts = far_call(
        functools.partial(unproject_body, n, tile),
        "unproject",
        [me],
        [],
        [w_qkv, gp_t],
        [(shape((shard, dim), BF16), 1)] * n,
        after=[*grads[:1], *third_sums, *dvs[1:3]],
    )
    first_grad = None

    def first_grad_of(after):
        return far_call(
            first_grad_body, "first_grad", [me], [], dvs, [(shape((shard, dim), F32), 1)], after=after
        )[0]

    if n == 4:
        gains = gate(gains, gn_parts[:1])
        gains = gains + swap(gains, "head", n, 1)
    else:
        gains = sum_all(gains, "head", n)
    def layer_out_of(after):
        return far_call(
            functools.partial(layer_out_body, tile),
            "layer_out",
            [],
            [],
            [(a, per) for a in (middle, *layer_terms)],
            [(shape((shard, dim), BF16), per)],
            after=after,
        )[0]

    def input_grad_of():
        return far_call(
            functools.partial(input_back_body, tile),
            "input_back",
            [],
            [gain_one],
            [(a, per) for a in (x_own, grad_middle, *gn_one)],
            [(shape((shard, dim), F32), per)],
        )[0]

    if ringed:
        layer_out = layer_out_of(gn_parts[:1])
        sent = scatter_kernel(held, [])
        gn_near = sum_near(gn_parts, [gains_far, layer_out, *[h[-1] for h in held]])
        gn_one, gn_sent = sum_far(*gn_near, fold_after=sent)
        held = scatter_swap(held, sent, n_dp, bit_orders)
        gains = gate(gains, [gn_sent, gn_one[1]])
        gains = gains + swap(gains, "dp", n_dp, bit_orders[0][0])
        first_grad = first_grad_of([gn_sent])
        mlp_gu, mlp_down = scatter_end(mlp_held, [], 2 * hidden, after=[gn_sent])
        gains = gate(gains, [first_grad, mlp_down])
        gains = gains + swap(gains, "dp", n_dp, bit_orders[0][1])
        input_grad = input_grad_of()
        *sent, gains = scatter_kernel(held, [gains])
        held = scatter_swap(held, sent, n_dp, bit_orders)
    else:
        gn_one, _ = sum_relative(gn_parts, "head", n)
        layer_out, input_grad = layer_out_of([]), input_grad_of()
        gains = sum_all(gains, "dp", n_dp)
        grads = lax.psum_scatter(grads[0], "dp", scatter_dimension=0, tiled=False).astype(F32)
        qkv_grad, out_grad_w = grads[: 3 * width], grads[3 * width :]
        mlp_grads = mlp_grads.astype(F32)
        mlp_gu, mlp_down = mlp_grads[: 2 * hidden], mlp_grads[2 * hidden :]
    if ringed:
        qkv_grad, out_grad_w, gain_one_grad, gain_two_grad = scatter_end(
            held, [gains], 3 * width, after=[input_grad]
        )
        qkv_grad = qkv_grad.transpose(1, 0, 2)
    else:
        qkv_grad = qkv_grad.reshape(3, width, lanes).transpose(2, 0, 1)
        gain_one_grad, gain_two_grad = gains.reshape(2, dim)
    if first_grad is None:
        stacked = jnp.stack(dvs)
        placed = [
            lax.dynamic_index_in_dim(stacked, me[0] ^ i, keepdims=False) for i in range(n)
        ]
        first_grad = jnp.concatenate(placed, axis=1).astype(F32)
    return (
        layer_out[None],
        input_grad[None],
        first_grad[None],
        qkv_grad,
        out_grad_w,
        mlp_gu.reshape(2, hidden, lanes).transpose(2, 0, 1),
        mlp_down,
        gain_one_grad.reshape(dim),
        gain_two_grad.reshape(dim),
    )


def solution(mesh):
    tokens = P("dp", "head", None)
    columns = P("dp", None, "head")
    rows = P("head", "dp")
    return jax.shard_map(
        functools.partial(local, mesh.shape["head"], mesh.shape["dp"]),
        mesh=mesh,
        in_specs=(tokens, tokens, P("dp", None), tokens, columns, rows, columns, rows, P(), P()),
        out_specs=(tokens, tokens, tokens, columns, rows, columns, rows, P(), P()),
        check_vma=False,
    )
```
